32 devices in a mesh: dp: 4 (over x, core), sp: 8 (over z, y).
Axes of the slice: x: 2, y: 2, z: 4, core: 2. Of those that a mesh axis runs over, the one named last changes fastest.
Arguments:
- images: bfloat16 [2, 16, 32, 32, 384], P(None, 'dp', 'sp'), may hold values from -30 to 30
- timesteps: int32 [2, 16], P(None, 'dp'), may hold values from 0 to 3999
- loss_weight: float32 [2, 16], P(None, 'dp'), may hold values from 0.5 to 2
- out_grad: bfloat16 [2, 16, 32, 32, 384], P(None, 'dp', 'sp'), may hold values from -6 to 6
- norm_gains: bfloat16 [3, 384], P(None, ('dp', 'sp')), may hold values from 0.25 to 1.75
- norm_biases: bfloat16 [3, 384], P(None, ('dp', 'sp')), may hold values from -1.5 to 1.5
- conv_biases: bfloat16 [2, 384], P(None, ('dp', 'sp')), may hold values from -1.5 to 1.5
- film_weight: bfloat16 [512, 2, 384], P(('dp', 'sp')), may hold values from -0.5 to 0.5
- film_bias: bfloat16 [2, 384], P(None, ('dp', 'sp')), may hold values from -1.5 to 1.5
- conv1_weight: bfloat16 [3, 3, 384, 384], P(None, None, ('dp', 'sp')), may hold values from -0.109375 to 0.109375
- conv2_weight: bfloat16 [3, 3, 384, 384], P(None, None, ('dp', 'sp')), may hold values from -0.109375 to 0.109375
- qkv_weight: bfloat16 [384, 4, 3, 96], P(('dp', 'sp')), may hold values from -0.4375 to 0.4375
- qv_bias: bfloat16 [2, 384], P(None, ('dp', 'sp')), may hold values from -0.59765625 to 0.59765625
- proj_weight: bfloat16 [4, 96, 384], P(None, None, ('dp', 'sp')), may hold values from -3.5 to 3.5
- proj_bias: bfloat16 [384], P(('dp', 'sp')), may hold values from -3.5 to 3.5
Outputs:
- block_out: bfloat16 [2, 16, 32, 32, 384], P(None, 'dp', 'sp')
- image_grad: bfloat16 [2, 16, 32, 32, 384], P(None, 'dp', 'sp')
- norm_gains_grad: float32 [3, 384], P(None, ('dp', 'sp'))
- norm_biases_grad: float32 [3, 384], P(None, ('dp', 'sp'))
- conv_biases_grad: float32 [2, 384], P(None, ('dp', 'sp'))
- film_weight_grad: float32 [512, 2, 384], P(('dp', 'sp'))
- film_bias_grad: float32 [2, 384], P(None, ('dp', 'sp'))
- conv1_weight_grad: float32 [3, 3, 384, 384], P(None, None, ('dp', 'sp'))
- conv2_weight_grad: float32 [3, 3, 384, 384], P(None, None, ('dp', 'sp'))
- qkv_weight_grad: float32 [384, 4, 3, 96], P(('dp', 'sp'))
- qv_bias_grad: float32 [2, 384], P(None, ('dp', 'sp'))
- proj_weight_grad: float32 [4, 96, 384], P(None, None, ('dp', 'sp'))
- proj_bias_grad: float32 [384], P(('dp', 'sp'))
The draws below stay inside these ranges and needn't reach their ends.
All inputs are finite; a program needn't handle non-finite values.
Results may differ from the reference program's by a relative error of at most 0.03.
Values may be sent and summed in bfloat16 or wider, within the bound.
No kernel may reach another device: no remote copies, remote signals or barrier semaphores. Data moves between devices by JAX's collectives and lax.ppermute only.
A program may use at most 128 MiB of HBM per device.

```python
import math
import jax
import jax.numpy as jnp
from jax import lax

C = 384
E = 512
HEADS = 4
HD = 96
GROUPS = 32
H = 32
W = 32
MB = 2
NB = 16


def draw_images(key, part):
    key = jax.random.fold_in(key, 7)
    keys_list = jax.random.split(key, 3)
    row_ramp = jnp.exp(jnp.log(3.0) * jnp.arange(H, dtype=jnp.float32) / (H - 1)) / 1.7
    row_rough = jnp.exp(jax.random.uniform(keys_list[0], (MB, NB, H, 1, 1), minval=-0.5, maxval=0.5))
    channel_scale = jnp.exp(jax.random.uniform(keys_list[1], (C,), minval=-0.7, maxval=0.7))
    base_values = jnp.clip(jax.random.normal(keys_list[2], (MB, NB, H, W, C)), -5.0, 5.0)
    values = base_values * row_rough * channel_scale * row_ramp[:, None, None]
    return values.astype(jnp.bfloat16)


def with_ends(entries, rng, least, top_value):
    index_at = [jax.random.randint(jax.random.fold_in(rng, axis), (), 0, length) for axis, length in enumerate(entries.shape)]
    longest = entries.shape.index(max(entries.shape))
    next_to = index_at[:longest] + [(index_at[longest] + 1) % entries.shape[longest]] + index_at[longest + 1:]
    return entries.at[tuple(index_at)].set(least).at[tuple(next_to)].set(top_value)


def levels(own_key, extent, pieces, low, high):
    loudness, own = 1.0, jax.random.fold_in(own_key, 6)
    for position, blocks in pieces:
        steps = jnp.exp(jax.random.uniform(jax.random.fold_in(own, position), (blocks,), jnp.float32, low / len(pieces), high / len(pieces)))
        loudness = loudness * jnp.repeat(steps, extent[position] // blocks).reshape([-1 if axis == position else 1 for axis in range(len(extent))])
    return loudness


def bell_draw(rng, shape, scale, reach, cuts=(), kind=jnp.bfloat16):
    result = scale * jax.random.normal(rng, shape, jnp.float32)
    if cuts:
        result = result * levels(rng, shape, cuts, -0.22, 0.18)
    return jnp.clip(result, -reach, reach).astype(kind)


def setup_inputs(seed: int = 0) -> dict:
    streams_of = jax.random.split(jax.random.key(seed), 16)
    return {
        "images": draw_images(jax.random.fold_in(streams_of[15], 71), 0),
        "timesteps": with_ends(jax.random.randint(streams_of[1], (MB, NB), 0, 4000), jax.random.fold_in(streams_of[1], 1), 0, 3999).astype(jnp.int32),
        "loss_weight": jnp.clip(jnp.exp(math.log(2.0) - 1.3862944 * jax.random.uniform(streams_of[2], (MB, NB), jnp.float32) ** levels(streams_of[2], (MB, NB), ((1, 4),), -0.2, 0.2)), 0.5, 2.0),
        "out_grad": bell_draw(streams_of[3], (MB, NB, H, W, C), 1.0, 6.0, ((1, 4), (2, 8))),
        "norm_gains": jnp.clip(1.0 + 0.15 * jax.random.normal(streams_of[4], (3, C), jnp.float32), 0.25, 1.75).astype(jnp.bfloat16),
        "norm_biases": bell_draw(streams_of[5], (3, C), 0.3, 1.5, ((1, 32),)),
        "conv_biases": bell_draw(streams_of[6], (2, C), 0.3, 1.5, ((1, 32),)),
        "film_weight": bell_draw(streams_of[7], (E, 2, C), (E // 4) ** -0.5, 0.5, ((0, 32),)),
        "film_bias": bell_draw(streams_of[8], (2, C), 0.3, 1.5, ((1, 32),)),
        "conv1_weight": bell_draw(streams_of[9], (3, 3, C, C), (9 * C) ** -0.5, 0.109375, ((2, 32),)),
        "conv2_weight": bell_draw(streams_of[10], (3, 3, C, C), (9 * C) ** -0.5, 0.109375, ((2, 32),)),
        "qkv_weight": bell_draw(streams_of[11], (C, HEADS, 3, HD), (C // 2) ** -0.5, 0.4375, ((0, 32),)),
        "qv_bias": bell_draw(streams_of[12], (2, C), 0.1, 0.59765625, ((1, 32),)),
        "proj_weight": bell_draw(streams_of[13], (HEADS, HD, C), (C // 128) ** -0.5, 3.5, ((2, 32),)),
        "proj_bias": bell_draw(streams_of[14], (C,), 0.7, 3.5, ((0, 32),)),
    }


highest = lax.Precision.HIGHEST
norm_eps = 1e-05

@jax.custom_vjp
def low(v):
    return lax.optimization_barrier(v.astype(jnp.bfloat16)).astype(jnp.float32)

@jax.custom_vjp
def low_back(v):
    return v

def low_keep(v):
    return (low(v), None)

def low_pass(kept, grad):
    return (grad,)

def back_keep(v):
    return (v, None)

def back_low(kept, grad):
    return (low(grad),)
low.defvjp(low_keep, low_pass)
low_back.defvjp(back_keep, back_low)

def time_embedding(steps):
    half_width = E // 2
    frequencies = jnp.exp(-math.log(10000.0) * jnp.arange(half_width, dtype=jnp.float32) / half_width)
    angles = steps.astype(jnp.float32)[:, None] * frequencies[None, :]
    return jnp.concatenate([jnp.cos(angles), jnp.sin(angles)], axis=1)

def group_norm(value, gain, shift):
    samples, row_count, col_count, channels = value.shape
    shaped = value.reshape(samples, row_count, col_count, GROUPS, channels // GROUPS)
    group_mean = lax.optimization_barrier(jnp.mean(shaped, axis=(1, 2, 4), keepdims=True))
    spread = lax.optimization_barrier(jnp.mean(jnp.square(shaped - group_mean), axis=(1, 2, 4), keepdims=True))
    normed = ((shaped - group_mean) * lax.rsqrt(spread + norm_eps)).reshape(value.shape)
    return normed * gain + shift

def convolve(value, weight):
    return lax.conv_general_dilated(value, weight, (1, 1), 'SAME', dimension_numbers=('NHWC', 'HWIO', 'NHWC'), precision=highest)

def forward(source, embedding, norm_gains, norm_shift, conv_shift, film_weight, film_shift, conv1_weight, conv2_weight, qkv_weight, qv_shift, proj_weight, proj_shift):
    samples = source.shape[0]
    first_input = low(jax.nn.silu(group_norm(source, norm_gains[0], norm_shift[0])))
    hidden = low_back(convolve(first_input, conv1_weight) + conv_shift[0])
    film_out = jnp.einsum('ne,ekc->nkc', jax.nn.silu(embedding), film_weight, precision=highest) + film_shift
    scaled = group_norm(hidden, norm_gains[1], norm_shift[1]) * (1.0 + film_out[:, 0][:, None, None, :]) + film_out[:, 1][:, None, None, :]
    second_input = low(jax.nn.silu(scaled))
    residual = source + low_back(convolve(second_input, conv2_weight) + conv_shift[1])
    attn_input = low(group_norm(residual, norm_gains[2], norm_shift[2]))
    empty_keys = jnp.zeros((HEADS, HD), dtype=qv_shift.dtype)
    qkv_shift = jnp.stack([qv_shift[0].reshape(HEADS, HD), empty_keys, qv_shift[1].reshape(HEADS, HD)], axis=1)
    projected = jnp.einsum('nhwc,cgkd->nghwkd', attn_input, qkv_weight, precision=highest) + qkv_shift[None, :, None, None]
    projected = low_back(low(projected)).reshape(samples, HEADS, H * W, 3, HD)
    queries = projected[:, :, :, 0, :]
    key_rows = projected[:, :, :, 1, :]
    values = projected[:, :, :, 2, :]
    scores = low_back(jnp.einsum('ngtd,ngud->ngtu', queries, key_rows, precision=highest) / math.sqrt(HD))
    row_max = lax.optimization_barrier(jnp.max(scores, axis=-1, keepdims=True))
    exponent = jnp.exp(scores - row_max)
    soft_weights = low(exponent / lax.optimization_barrier(jnp.sum(exponent, axis=-1, keepdims=True)))
    attended = low_back(low(jnp.einsum('ngtu,ngud->ngtd', soft_weights, values, precision=highest)))
    attended = attended.reshape(samples, HEADS, H, W, HD)
    branch = low_back(jnp.einsum('nghwd,gdc->nhwc', attended, proj_weight, precision=highest) + proj_shift)
    return residual + branch

def reference(images, timesteps, loss_weight, out_grad, norm_gains, norm_biases, conv_biases, film_weight, film_bias, conv1_weight, conv2_weight, qkv_weight, qv_bias, proj_weight, proj_bias):
    params = tuple((weight_arg.astype(jnp.float32) for weight_arg in (norm_gains, norm_biases, conv_biases, film_weight, film_bias, conv1_weight, conv2_weight, qkv_weight, qv_bias, proj_weight, proj_bias)))
    per_step = 4
    step_count = MB * NB // per_step
    image_blocks = images.astype(jnp.float32).reshape(step_count, per_step, H, W, C)
    time_blocks = timesteps.reshape(step_count, per_step)
    weight_blocks = loss_weight.reshape(step_count, per_step)
    grad_blocks = out_grad.astype(jnp.float32).reshape(step_count, per_step, H, W, C)

    def one_step(totals, sample_block):
        image_part, time_part, weight_part, grad_part = sample_block
        embedding = time_embedding(time_part)

        def evaluate(source, *weights):
            return forward(source, embedding, *weights)
        block_out, pullback = jax.vjp(evaluate, image_part, *params)
        gradients = pullback(grad_part * weight_part[:, None, None, None])
        new_totals = tuple((total + extra for total, extra in zip(totals, gradients[1:])))
        return (new_totals, (block_out.astype(jnp.bfloat16), gradients[0].astype(jnp.bfloat16)))
    start = tuple((jnp.zeros_like(weight_arg) for weight_arg in params))
    totals, (outputs, input_grads) = lax.scan(one_step, start, (image_blocks, time_blocks, weight_blocks, grad_blocks))
    return (outputs.reshape(MB, NB, H, W, C), input_grads.reshape(MB, NB, H, W, C), totals[0], totals[1], totals[2], totals[3], totals[4], totals[5], totals[6], totals[7], totals[8], totals[9], totals[10])
```

```python
import math

import jax
import jax.numpy as jnp
from jax import lax
from jax.sharding import PartitionSpec as P

C = 384
E = 512
HEADS = 4
HD = 96
GROUPS = 32
H = 32
W = 32
PIX = H * W

highest = lax.Precision.HIGHEST
norm_eps = 1e-05
both = ("dp", "sp")


def silu_grad(value):
    sigmoid = jax.nn.sigmoid(value)
    return sigmoid * (1.0 + value * (1.0 - sigmoid))


def time_embedding(steps):
    half_width = E // 2
    frequencies = jnp.exp(
        -math.log(10000.0) * jnp.arange(half_width, dtype=jnp.float32) / half_width
    )
    angles = steps.astype(jnp.float32)[:, None] * frequencies[None, :]
    return jnp.concatenate([jnp.cos(angles), jnp.sin(angles)], axis=1)


def group_mean(value):
    sums = jnp.mean(jnp.mean(value, axis=0).reshape(GROUPS, C // GROUPS), axis=1)
    return jnp.repeat(sums, C // GROUPS)[None, :]


def norm_forward(value, gain, shift):
    centred = value - group_mean(value)
    inverse = lax.rsqrt(group_mean(centred * centred) + norm_eps)
    normed = centred * inverse
    return normed, inverse, normed * gain + shift


def norm_backward(grad_out, normed, inverse, gain):
    grad_hat = grad_out * gain
    grad_in = inverse * (
        grad_hat - group_mean(grad_hat) - normed * group_mean(grad_hat * normed)
    )
    return grad_in, jnp.sum(grad_out * normed, axis=0), jnp.sum(grad_out, axis=0)


def patches(value):
    padded = jnp.pad(value.reshape(H, W, C), ((1, 1), (1, 1), (0, 0)))
    return jnp.concatenate(
        [padded[i : i + H, j : j + W].reshape(PIX, C) for i in range(3) for j in range(3)], axis=1
    )


def dot(a, b, ca, cb):
    return lax.dot_general(a, b, (((ca,), (cb,)), ((), ())), preferred_element_type=jnp.float32)


def one_sample(source, step, sample_weight, out_grad, weights):
    gains, shifts, conv_shift, film_w, film_b, w1, w2, wqkv, qv_shift, wproj, proj_shift = weights
    source = source.astype(jnp.float32)
    n1, r1, pre1 = norm_forward(source, gains[0], shifts[0])
    first_cols = patches(jax.nn.silu(pre1).astype(jnp.bfloat16))
    hidden = dot(first_cols, w1.reshape(9 * C, C), 1, 0) + conv_shift[0]
    embedding = jax.nn.silu(time_embedding(step[None]))
    film = jnp.einsum("ne,ekc->nkc", embedding, film_w, precision=highest)[0] + film_b
    n2, r2, norm2 = norm_forward(hidden, gains[1], shifts[1])
    scaled = norm2 * (1.0 + film[0]) + film[1]
    second_cols = patches(jax.nn.silu(scaled).astype(jnp.bfloat16))
    residual = source + dot(second_cols, w2.reshape(9 * C, C), 1, 0) + conv_shift[1]
    n3, r3, norm3 = norm_forward(residual, gains[2], shifts[2])
    attn_in = norm3.astype(jnp.bfloat16)
    qkv_shift = jnp.stack(
        [
            qv_shift[0].reshape(HEADS, HD),
            jnp.zeros((HEADS, HD), jnp.float32),
            qv_shift[1].reshape(HEADS, HD),
        ],
        axis=1,
    )
    projected = (dot(attn_in, wqkv.reshape(C, 3 * C), 1, 0) + qkv_shift.reshape(3 * C)).astype(
        jnp.bfloat16
    )
    packed = projected.reshape(PIX, HEADS, 3, HD).transpose(1, 2, 0, 3)
    factor = 1.0 / math.sqrt(HD)
    cotangent = out_grad.astype(jnp.float32) * sample_weight
    grad_branch = cotangent.astype(jnp.bfloat16)
    grad_attended = dot(grad_branch, wproj, 1, 1).astype(jnp.bfloat16)
    grad_heads = grad_attended.reshape(PIX, HEADS, HD).transpose(1, 0, 2)

    def head(args):
        block, grad_block = args
        q, k, v = block[0], block[1], block[2]
        scores = dot(q, k, 1, 1) * factor
        exponent = jnp.exp(scores - jnp.max(scores, axis=-1, keepdims=True))
        probs = exponent / jnp.sum(exponent, axis=-1, keepdims=True)
        soft = probs.astype(jnp.bfloat16)
        attended = dot(soft, v, 1, 0).astype(jnp.bfloat16)
        grad_probs = dot(grad_block, v, 1, 1)
        grad_v = dot(soft, grad_block, 0, 0)
        inner = jnp.sum(grad_probs * probs, axis=-1, keepdims=True)
        grad_scores = (probs * (grad_probs - inner)).astype(jnp.bfloat16)
        grad_q = dot(grad_scores, k, 1, 0) * factor
        grad_k = dot(grad_scores, q, 0, 0) * factor
        return attended, jnp.stack([grad_q, grad_k, grad_v]).astype(jnp.bfloat16)

    attended, grad_packed = lax.map(head, (packed, grad_heads))
    attended = attended.transpose(1, 0, 2).reshape(PIX, C)
    grad_proj = grad_packed.transpose(2, 0, 1, 3).reshape(PIX, 3 * C)
    block_out = (residual + dot(attended, wproj, 1, 0) + proj_shift).astype(jnp.bfloat16)
    wproj_grad = dot(attended, grad_branch, 0, 0)
    proj_shift_grad = jnp.sum(grad_branch.astype(jnp.float32), axis=0)
    wqkv_grad = dot(attn_in, grad_proj, 0, 0)
    sums = jnp.sum(grad_proj.astype(jnp.float32), axis=0).reshape(HEADS, 3, HD)
    qv_grad = jnp.stack([sums[:, 0].reshape(C), sums[:, 2].reshape(C)])
    grad_attn = dot(grad_proj, wqkv.reshape(C, 3 * C), 1, 1)
    grad3, gain3, shift3 = norm_backward(grad_attn, n3, r3, gains[2])
    grad_residual = cotangent + grad3
    g2 = grad_residual.astype(jnp.bfloat16)
    w2_grad = dot(second_cols, g2, 0, 0)
    conv2_shift_grad = jnp.sum(g2.astype(jnp.float32), axis=0)
    flip = lambda w: w[::-1, ::-1].transpose(0, 1, 3, 2).reshape(9 * C, C)
    grad_second = dot(patches(g2), flip(w2), 1, 0)
    grad_scaled = grad_second * silu_grad(scaled)
    film_grad = jnp.stack([jnp.sum(grad_scaled * norm2, axis=0), jnp.sum(grad_scaled, axis=0)])
    film_w_grad = embedding[0][:, None, None] * film_grad[None]
    grad_hidden, gain2, shift2 = norm_backward(grad_scaled * (1.0 + film[0]), n2, r2, gains[1])
    g1 = grad_hidden.astype(jnp.bfloat16)
    w1_grad = dot(first_cols, g1, 0, 0)
    conv1_shift_grad = jnp.sum(g1.astype(jnp.float32), axis=0)
    grad_first = dot(patches(g1), flip(w1), 1, 0) * silu_grad(pre1)
    grad_source, gain1, shift1 = norm_backward(grad_first, n1, r1, gains[0])
    image_grad = (grad_residual + grad_source).astype(jnp.bfloat16)
    small = jnp.concatenate(
        [
            jnp.stack([gain1, gain2, gain3, shift1, shift2, shift3, conv1_shift_grad, conv2_shift_grad]),
            film_grad,
            qv_grad,
            proj_shift_grad[None],
        ]
    )
    return block_out, image_grad, (w1_grad, w2_grad, wqkv_grad, wproj_grad, film_w_grad, small)


def body(
    images,
    timesteps,
    loss_weight,
    out_grad,
    norm_gains,
    norm_biases,
    conv_biases,
    film_weight,
    film_bias,
    conv1_weight,
    conv2_weight,
    qkv_weight,
    qv_bias,
    proj_weight,
    proj_bias,
):
    row_parts = lax.axis_size("sp")
    devices = lax.axis_size("dp") * row_parts
    samples = images.shape[0] * images.shape[1]
    rows = images.shape[2]
    per = max(1, samples // row_parts)
    copies = max(1, row_parts // samples)
    share = C // devices
    embed_share = E // devices
    place = lax.axis_index("sp")

    def to_samples(value):
        value = value.reshape(samples // per, per * rows * W, C)
        if copies > 1:
            value = jnp.repeat(value, copies, axis=0)
        value = lax.all_to_all(value, "sp", split_axis=0, concat_axis=0, tiled=True)
        value = value.reshape(row_parts, per, rows * W, C).transpose(1, 0, 2, 3)
        return value.reshape(per, PIX, C)

    def to_rows(value):
        value = value.reshape(per, row_parts, rows * W, C).transpose(1, 0, 2, 3)
        value = value.reshape(row_parts, per * rows * W, C)
        value = lax.all_to_all(value, "sp", split_axis=0, concat_axis=0, tiled=True)
        return value[::copies].reshape(images.shape)

    first = (place // copies) * per
    steps = lax.dynamic_slice_in_dim(timesteps.reshape(samples), first, per)
    loss = lax.dynamic_slice_in_dim(loss_weight.reshape(samples), first, per)

    small = jnp.concatenate(
        [norm_gains, norm_biases, conv_biases, film_bias, qv_bias, proj_bias[None]], axis=0
    ).reshape(13 * share)
    small = jnp.pad(small, (0, C - 13 * share))[None]
    pieces = [
        conv1_weight.reshape(9 * share, C),
        conv2_weight.reshape(9 * share, C),
        qkv_weight.reshape(3 * share, C),
        proj_weight.transpose(2, 0, 1).reshape(share, C),
        film_weight.reshape(2 * embed_share, C),
        small,
    ]
    counts = [piece.shape[0] for piece in pieces]
    length = -(-sum(counts) // 16) * 16
    packed = jnp.pad(jnp.concatenate(pieces), ((0, length - sum(counts)), (0, 0)))
    gathered = lax.all_gather(packed, both, axis=0, tiled=False)
    parts = []
    start = 0
    for count in counts:
        parts.append(gathered[:, start : start + count])
        start += count
    w1, w2 = (
        p.reshape(devices, 9, share, C).transpose(1, 0, 2, 3).reshape(3, 3, C, C) for p in parts[:2]
    )
    wqkv = parts[2].reshape(C, 3 * C)
    wproj = parts[3].reshape(C, C).T
    film_w = parts[4].reshape(E, 2, C).astype(jnp.float32)
    small = parts[5][:, 0, : 13 * share].reshape(devices, 13, share).transpose(1, 0, 2)
    small = small.reshape(13, C).astype(jnp.float32)
    weights = (
        small[0:3], small[3:6], small[6:8], film_w, small[8:10], w1, w2, wqkv, small[10:12], wproj, small[12],
    )

    images_in = to_samples(images)
    grads_in = to_samples(out_grad)
    outs, image_grads, totals = [], [], None
    for index in range(per):
        block_out, image_grad, grads = one_sample(
            images_in[index], steps[index], loss[index], grads_in[index], weights
        )
        outs.append(block_out)
        image_grads.append(image_grad)
        totals = grads if totals is None else tuple(a + b for a, b in zip(totals, grads))
    if copies > 1:
        totals = tuple(jnp.where(place % copies == 0, t, 0.0) for t in totals)
    w1_grad, w2_grad, wqkv_grad, wproj_grad, film_w_grad, small_grad = totals
    small_grad = small_grad.reshape(13, devices, share).transpose(1, 0, 2).reshape(devices, 13 * share)
    pieces = [
        w1_grad.reshape(9, devices, share, C).transpose(1, 0, 2, 3).reshape(devices, 9 * share, C),
        w2_grad.reshape(9, devices, share, C).transpose(1, 0, 2, 3).reshape(devices, 9 * share, C),
        wqkv_grad.reshape(devices, 3 * share, C),
        wproj_grad.T.reshape(devices, share, C),
        film_w_grad.reshape(devices, 2 * embed_share, C),
        jnp.pad(small_grad, ((0, 0), (0, C - 13 * share)))[:, None],
    ]
    packed = jnp.concatenate([p.astype(jnp.bfloat16) for p in pieces], axis=1)
    packed = jnp.pad(packed, ((0, 0), (0, length - sum(counts)), (0, 0)))
    reduced = lax.psum_scatter(packed, both, scatter_dimension=0, tiled=True)[0].astype(jnp.float32)
    parts = []
    start = 0
    for count in counts:
        parts.append(reduced[start : start + count])
        start += count
    small = parts[5][0, : 13 * share].reshape(13, share)
    return (
        to_rows(jnp.stack(outs)),
        to_rows(jnp.stack(image_grads)),
        small[0:3],
        small[3:6],
        small[6:8],
        parts[4].reshape(embed_share, 2, C),
        small[8:10],
        parts[0].reshape(3, 3, share, C),
        parts[1].reshape(3, 3, share, C),
        parts[2].reshape(share, HEADS, 3, HD),
        small[10:12],
        parts[3].T.reshape(HEADS, HD, share),
        small[12],
    )


def solution(mesh):
    return jax.shard_map(
        body,
        mesh=mesh,
        in_specs=(
            P(None, "dp", "sp", None, None),
            P(None, "dp"),
            P(None, "dp"),
            P(None, "dp", "sp", None, None),
            P(None, both),
            P(None, both),
            P(None, both),
            P(both, None, None),
            P(None, both),
            P(None, None, both, None),
            P(None, None, both, None),
            P(both, None, None, None),
            P(None, both),
            P(None, None, both),
            P(both),
        ),
        out_specs=(
            P(None, "dp", "sp", None, None),
            P(None, "dp", "sp", None, None),
            P(None, both),
            P(None, both),
            P(None, both),
            P(both, None, None),
            P(None, both),
            P(None, None, both, None),
            P(None, None, both, None),
            P(both, None, None, None),
            P(None, both),
            P(None, None, both),
            P(both),
        ),
        check_vma=False,
    )
```

```python
import functools
import math

import jax
import jax.numpy as jnp
from jax import lax
from jax.experimental import pallas as pl
from jax.experimental.pallas import tpu as pltpu
from jax.sharding import PartitionSpec as P

C = 384
E = 512
HEADS = 4
HD = 96
PAD = 128
GROUPS = 32
H = 32
W = 32
PIX = H * W
TAPS = 3 * C
QKV = HEADS * 3 * PAD
ATT = HEADS * PAD
ROWS = PIX + 2 * W
CHUNK = 128
norm_eps = 1e-05
bf16 = jnp.bfloat16
f32 = jnp.float32


def dot(a, b, ca=1, cb=0):
    return lax.dot_general(a, b, (((ca,), (cb,)), ((), ())), preferred_element_type=f32)


def rows(i, size=CHUNK):
    return pl.ds(pl.multiple_of(i * size, size), size)


def over(body, init, count=PIX // CHUNK, unroll=2):
    return lax.fori_loop(0, count, body, init, unroll=unroll)


def split3(v):
    hi = v.astype(bf16)
    rest = v - hi.astype(f32)
    mid = rest.astype(bf16)
    low = (rest - mid.astype(f32)).astype(bf16)
    return hi, mid, low


def same_group():
    lane = lax.broadcasted_iota(jnp.int32, (C, C), 1).astype(f32)
    sub = lax.broadcasted_iota(jnp.int32, (C, C), 0).astype(f32)
    width = GROUPS / C
    return (jnp.floor((lane + 0.5) * width) == jnp.floor((sub + 0.5) * width)).astype(f32).astype(bf16)


def group_means(vectors, ones):
    parts = [p for v in vectors for p in split3(v)]
    count = len(parts)
    stacked = jnp.concatenate(
        [p.astype(f32) for p in parts] + [jnp.zeros((16 - count, C), f32)], axis=0
    ).astype(bf16)
    sums = dot(stacked, ones)
    scale = 1.0 / (PIX * (C // GROUPS))
    return [
        (sums[3 * i : 3 * i + 1] + sums[3 * i + 1 : 3 * i + 2] + sums[3 * i + 2 : 3 * i + 3]) * scale
        for i in range(len(vectors))
    ]


def total(v):
    return jnp.sum(v, axis=0, keepdims=True)


def norm_stats(load, ones):
    zero = jnp.zeros((1, C), f32)
    (mean,) = group_means([over(lambda i, s: s + total(load(i)), zero)], ones)

    def square(i, s):
        centred = load(i) - mean
        return s + total(centred * centred)

    (variance,) = group_means([over(square, zero)], ones)
    return mean, lax.rsqrt(variance + norm_eps)


def put_shifted(dst, i, value, step):
    size = value.shape[0]
    column = lax.broadcasted_iota(jnp.int32, (size, C), 0) & (W - 1)
    at = pl.ds(pl.multiple_of(W + i * size, W), size)
    back = jnp.where(column == 0, 0.0, pltpu.roll(value, 1, 0))
    ahead = jnp.where(column == W - 1, 0.0, pltpu.roll(value, size - 1, 0))
    order = (back, value, ahead) if step == 1 else (ahead, value, back)
    for k in range(3):
        dst[at, k * C : (k + 1) * C] = order[k].astype(bf16)


def zero_edges(dst):
    dst[0:W, :] = jnp.zeros((W, TAPS), bf16)
    dst[W + PIX : ROWS, :] = jnp.zeros((W, TAPS), bf16)


def lay_weight(dst, src):
    for tap in range(9):
        dst[tap * C : (tap + 1) * C, :] = src[:, tap * C : (tap + 1) * C]


def conv_rows(shifted, weight, i, size):
    acc = None
    for kh in range(3):
        part = dot(
            shifted[pl.ds(pl.multiple_of(i * size + kh * W, W), size), :],
            weight[kh * TAPS : (kh + 1) * TAPS, :],
        )
        acc = part if acc is None else acc + part
    return acc


def conv_back_rows(shifted, weight, i, size):
    acc = None
    for kh in range(3):
        part = dot(
            shifted[pl.ds(pl.multiple_of(i * size + (2 - kh) * W, W), size), :],
            weight[:, kh * TAPS : (kh + 1) * TAPS],
            1,
            1,
        )
        acc = part if acc is None else acc + part
    return acc


def sigmoid(v):
    return 1.0 / (1.0 + jnp.exp(-v))


def silu_grad(v):
    s = sigmoid(v)
    return s * (1.0 + v * (1.0 - s))


def forward_kernel(
    x_ref, w1_ref, w2_ref, wqkv_ref, film1_ref, film2_ref, small_ref, emb_ref,
    first_ref, hidden_ref, second_ref, residual_ref, attn_ref, projected_ref, stats_ref,
    shifted, weight,
):
    ones = same_group()
    zero_edges(shifted)
    par = small_ref[...].astype(f32).T
    row = lambda k: par[k : k + 1, :]
    lay_weight(weight, w1_ref)

    load = lambda i: x_ref[rows(i), :].astype(f32)
    mean0, inv0 = norm_stats(load, ones)

    def start(i, carry):
        pre = (load(i) - mean0) * inv0 * row(0) + row(3)
        act = pre * sigmoid(pre)
        first_ref[rows(i), :] = act.astype(bf16)
        put_shifted(shifted, i, act, 1)
        return carry

    over(start, 0)

    def conv1(i, s):
        value = conv_rows(shifted, weight, i, 256) + row(6)
        hidden_ref[rows(i, 256), :] = value
        return s + total(value)

    sums = lax.fori_loop(0, PIX // 256, conv1, jnp.zeros((1, C), f32))
    (mean1,) = group_means([sums], ones)
    lay_weight(weight, w2_ref)

    def square(i, s):
        centred = hidden_ref[rows(i), :] - mean1
        return s + total(centred * centred)

    (var1,) = group_means([over(square, jnp.zeros((1, C), f32))], ones)
    inv1 = lax.rsqrt(var1 + norm_eps)

    wide = dot(emb_ref[...], film1_ref[...])
    narrow = dot(emb_ref[...], film2_ref[...])
    film = total(wide[0:3]) + jnp.concatenate(
        [total(narrow[3 + 3 * k : 6 + 3 * k]) for k in range(3)], axis=1
    )
    scale = 1.0 + film[:, :C] + row(8)
    shift = film[:, C:] + row(9)

    def middle(i, carry):
        norm = (hidden_ref[rows(i), :] - mean1) * inv1 * row(1) + row(4)
        scaled = norm * scale + shift
        act = scaled * sigmoid(scaled)
        second_ref[rows(i), :] = act.astype(bf16)
        put_shifted(shifted, i, act, 1)
        return carry

    over(middle, 0)

    def conv2(i, s):
        value = (
            conv_rows(shifted, weight, i, 256) + row(7) + x_ref[rows(i, 256), :].astype(f32)
        )
        residual_ref[rows(i, 256), :] = value
        return s + total(value)

    sums = lax.fori_loop(0, PIX // 256, conv2, jnp.zeros((1, C), f32))
    (mean2,) = group_means([sums], ones)

    def square2(i, s):
        centred = residual_ref[rows(i), :] - mean2
        return s + total(centred * centred)

    (var2,) = group_means([over(square2, jnp.zeros((1, C), f32))], ones)
    inv2 = lax.rsqrt(var2 + norm_eps)

    lane = lax.broadcasted_iota(jnp.int32, (8, PAD), 1)
    biases = []
    for g in range(HEADS):
        for k, which in ((0, 10), (1, None), (2, 11)):
            if which is None:
                biases.append(jnp.zeros((1, PAD), f32))
            else:
                turned = jnp.broadcast_to(row(which), (8, C))
                if g:
                    turned = pltpu.roll(turned, C - g * HD, 1)
                biases.append(jnp.where(lane < HD, turned[:, :PAD], 0.0)[0:1])
    bias = jnp.concatenate(biases, axis=1)

    def last(i, carry):
        norm = (residual_ref[rows(i, 256), :] - mean2) * inv2 * row(2) + row(5)
        attn = norm.astype(bf16)
        attn_ref[rows(i, 256), :] = attn
        projected_ref[rows(i, 256), :] = (dot(attn, wqkv_ref[...]) + bias).astype(bf16)
        return carry

    lax.fori_loop(0, PIX // 256, last, 0)
    stats_ref[...] = jnp.concatenate(
        [mean0, inv0, mean1, inv1, mean2, inv2, scale, shift]
        + [par[0:13, :], jnp.zeros((3, C), f32)],
        axis=0,
    )


def attention_kernel(
    loss_ref, grad_ref, wproj_ref, residual_ref, stats_ref, qkv_ref,
    out_ref, gqkv_ref, wproj_grad_ref, sums_ref,
    branch, attended, keys_grad, values_grad,
):
    g = pl.program_id(0)
    factor = 1.0 / math.sqrt(HD)
    size = 256

    @pl.when(g == 0)
    def _():
        def scaled(i, s):
            value = (grad_ref[rows(i), :].astype(f32) * loss_ref[0, 0]).astype(bf16)
            branch[rows(i), :] = value
            return s + total(value.astype(f32))

        sums_ref[...] = jnp.broadcast_to(over(scaled, jnp.zeros((1, C), f32)), (8, C))

    lanes = pl.ds(pl.multiple_of(g * PAD, PAD), PAD)
    keys_grad[...] = jnp.zeros_like(keys_grad)
    values_grad[...] = jnp.zeros_like(values_grad)

    def chunk(i, carry):
        queries = qkv_ref[rows(i, size), 0:PAD]
        keys = qkv_ref[:, PAD : 2 * PAD]
        values = qkv_ref[:, 2 * PAD : 3 * PAD]
        grad = dot(branch[rows(i, size), :], wproj_ref[:, lanes]).astype(bf16)
        scores = dot(queries, keys, 1, 1)
        top = jnp.max(scores, axis=1, keepdims=True)
        power = jnp.exp((scores - top) * factor)
        probs = power * (1.0 / jnp.sum(power, axis=1, keepdims=True))
        soft = probs.astype(bf16)
        attended[rows(i, size), lanes] = dot(soft, values).astype(bf16)
        grad_probs = dot(grad, values, 1, 1)
        inner = jnp.sum(grad_probs * probs, axis=1, keepdims=True)
        grad_scores = (probs * (grad_probs - inner)).astype(bf16)
        gqkv_ref[rows(i, size), 0:PAD] = (dot(grad_scores, keys) * factor).astype(bf16)
        keys_grad[...] += dot(queries, grad_scores, 0, 0)
        values_grad[...] += dot(grad, soft, 0, 0)
        return carry

    lax.fori_loop(0, PIX // size, chunk, 0)
    gqkv_ref[:, PAD : 2 * PAD] = (keys_grad[...].T * factor).astype(bf16)
    gqkv_ref[:, 2 * PAD : 3 * PAD] = values_grad[...].T.astype(bf16)

    @pl.when(g == HEADS - 1)
    def _():
        def project(i, carry):
            value = residual_ref[rows(i, size), :] + dot(attended[rows(i, size), :], wproj_ref[...], 1, 1)
            out_ref[rows(i, size), :] = (value + stats_ref[20:21, :]).astype(bf16)
            return carry

        lax.fori_loop(0, PIX // size, project, 0)
        wproj_grad_ref[...] = dot(branch[...], attended[...], 0, 0).astype(bf16)


def weight_grad(dst, act, shifted):
    turned = act[...].astype(f32).T.astype(bf16)
    for kh in range(3):
        dst[:, kh * TAPS : (kh + 1) * TAPS] = dot(
            turned, shifted[(2 - kh) * W : (2 - kh) * W + PIX, :]
        ).astype(bf16)


def middle_kernel(
    loss_ref, grad_ref, attn_ref, gqkv_ref, wqkv_ref, residual_ref, stats_ref, second_ref,
    wqkv_grad_ref, w2_grad_ref, grad_residual_ref, shifted, sums_ref, work,
):
    ones = same_group()
    zero_edges(shifted)
    size = 256
    mean, inv, gain = stats_ref[4:5, :], stats_ref[5:6, :], stats_ref[10:11, :]
    zero = jnp.zeros((1, C), f32)

    def step(i, carry):
        q_sum, u_sum, p_sum = carry
        packed = gqkv_ref[rows(i, size), :]
        q = dot(packed, wqkv_ref[...], 1, 1)
        work[rows(i, size), :] = q
        u = (residual_ref[rows(i, size), :] - mean) * inv
        return q_sum + total(q), u_sum + total(q * u), p_sum + total(packed.astype(f32))

    q_sum, u_sum, p_sum = lax.fori_loop(0, PIX // size, step, (zero, zero, jnp.zeros((1, QKV), f32)))
    first, second = group_means([q_sum * gain, u_sum * gain], ones)
    turned = attn_ref[...].astype(f32).T.astype(bf16)
    wqkv_grad_ref[...] = dot(turned, gqkv_ref[...]).astype(bf16)

    def apply(i, s):
        u = (residual_ref[rows(i), :] - mean) * inv
        value = grad_ref[rows(i), :].astype(f32) * loss_ref[0, 0] + inv * (
            work[rows(i), :] * gain - first - u * second
        )
        grad_residual_ref[rows(i), :] = value
        rounded = value.astype(bf16).astype(f32)
        put_shifted(shifted, i, rounded, -1)
        return s + total(rounded)

    conv_sum = over(apply, zero)
    weight_grad(w2_grad_ref, second_ref, shifted)

    def heads(k):
        value = jnp.zeros((8, C), f32)
        for g in range(HEADS):
            at = (3 * g + k) * PAD
            block = jnp.concatenate(
                [jnp.broadcast_to(p_sum[:, at : at + PAD], (8, PAD)), jnp.zeros((8, C - PAD), f32)], axis=1
            )
            value = value + (pltpu.roll(block, g * HD, 1) if g else block)
        return value[0:1]

    sums_ref[...] = jnp.concatenate(
        [u_sum, q_sum, conv_sum, heads(0), heads(2), jnp.zeros((3, C), f32)], axis=0
    )


def hidden_kernel(
    shifted, w2_ref, hidden_ref, stats_ref, g1_ref, sums_ref, work
):
    ones = same_group()
    size = 256
    stat = lambda k: stats_ref[k : k + 1, :]
    mean, inv, scale, shift, gain, bias = stat(2), stat(3), stat(6), stat(7), stat(9), stat(12)
    zero = jnp.zeros((1, C), f32)

    def step(i, carry):
        u_sum, s_sum = carry
        u = (hidden_ref[rows(i, size), :] - mean) * inv
        scaled = (u * gain + bias) * scale + shift
        value = conv_back_rows(shifted, w2_ref, i, size) * silu_grad(scaled)
        work[rows(i, size), :] = value
        return u_sum + total(value * u), s_sum + total(value)

    u_sum, s_sum = lax.fori_loop(0, PIX // size, step, (zero, zero))
    film0 = u_sum * gain + s_sum * bias
    u_up, s_up = u_sum * scale, s_sum * scale
    first, second = group_means([s_up * gain, u_up * gain], ones)
    factor = scale * gain

    def apply(i, s):
        u = (hidden_ref[rows(i), :] - mean) * inv
        value = (inv * (work[rows(i), :] * factor - first - u * second)).astype(bf16)
        g1_ref[rows(i), :] = value
        return s + total(value.astype(f32))

    conv_sum = over(apply, zero)
    sums_ref[...] = jnp.concatenate(
        [u_up, s_up, conv_sum, film0, s_sum, jnp.zeros((3, C), f32)], axis=0
    )


def first_weight_kernel(g1_ref, first_ref, w1_grad_ref, shifted):
    zero_edges(shifted)

    def step(i, carry):
        put_shifted(shifted, i, g1_ref[rows(i), :].astype(f32), -1)
        return carry

    over(step, 0)
    weight_grad(w1_grad_ref, first_ref, shifted)


def image_kernel(shifted, w1_ref, x_ref, stats_ref, grad_residual_ref, out_ref, sums_ref, work):
    ones = same_group()
    size = 256
    stat = lambda k: stats_ref[k : k + 1, :]
    mean, inv, gain, bias = stat(0), stat(1), stat(8), stat(11)
    zero = jnp.zeros((1, C), f32)

    def step(i, carry):
        u_sum, s_sum = carry
        u = (x_ref[rows(i, size), :].astype(f32) - mean) * inv
        value = conv_back_rows(shifted, w1_ref, i, size) * silu_grad(u * gain + bias)
        work[rows(i, size), :] = value
        return u_sum + total(value * u), s_sum + total(value)

    u_sum, s_sum = lax.fori_loop(0, PIX // size, step, (zero, zero))
    first, second = group_means([s_sum * gain, u_sum * gain], ones)

    def apply(i, carry):
        u = (x_ref[rows(i), :].astype(f32) - mean) * inv
        value = inv * (work[rows(i), :] * gain - first - u * second)
        out_ref[rows(i), :] = (grad_residual_ref[rows(i), :] + value).astype(bf16)
        return carry

    over(apply, 0)
    sums_ref[...] = jnp.concatenate([u_sum, s_sum, jnp.zeros((6, C), f32)], axis=0)


VMEM = pl.BlockSpec(memory_space=pltpu.VMEM)
SMEM = pl.BlockSpec(memory_space=pltpu.SMEM)


def shape(*dims, dtype=bf16):
    return jax.ShapeDtypeStruct(dims, dtype)


def cost(flops):
    return pl.CostEstimate(flops=int(flops), bytes_accessed=10_000_000, transcendentals=0)


def call(kernel, operands, outs, scratch, flops, name, scalars=0):
    return pl.pallas_call(
        kernel,
        out_shape=outs,
        in_specs=[SMEM] * scalars + [VMEM] * (len(operands) - scalars),
        out_specs=[VMEM] * len(outs),
        scratch_shapes=scratch,
        compiler_params=pltpu.CompilerParams(vmem_limit_bytes=60 * 2**20),
        cost_estimate=cost(flops),
        name=name,
    )(*operands)


def sample_step(x, grad, loss, w1, w2, wqkv, wproj, film1, film2, small, emb):
    field = 2 * PIX * C
    first, hidden, second, residual, attn, projected, stats = call(
        forward_kernel,
        [x, w1, w2, wqkv, film1, film2, small, emb],
        [
            shape(PIX, C), shape(PIX, C, dtype=f32), shape(PIX, C), shape(PIX, C, dtype=f32),
            shape(PIX, C), shape(PIX, QKV), shape(24, C, dtype=f32),
        ],
        [pltpu.VMEM((ROWS, TAPS), bf16), pltpu.VMEM((9 * C, C), bf16)],
        field * (18 * C + QKV), "forward",
    )
    whole = lambda *dims: pl.BlockSpec(dims, lambda g: (0, 0))
    block_out, gqkv, wproj_grad, proj_sums = pl.pallas_call(
        attention_kernel,
        grid=(HEADS,),
        out_shape=[shape(PIX, C), shape(PIX, QKV), shape(C, ATT), shape(8, C, dtype=f32)],
        in_specs=[
            SMEM, whole(PIX, C), whole(C, ATT), whole(PIX, C), whole(24, C),
            pl.BlockSpec((PIX, 3 * PAD), lambda g: (0, g)),
        ],
        out_specs=[whole(PIX, C), pl.BlockSpec((PIX, 3 * PAD), lambda g: (0, g)), whole(C, ATT), whole(8, C)],
        scratch_shapes=[
            pltpu.VMEM((PIX, C), bf16), pltpu.VMEM((PIX, ATT), bf16),
            pltpu.VMEM((PAD, PIX), f32), pltpu.VMEM((PAD, PIX), f32),
        ],
        compiler_params=pltpu.CompilerParams(vmem_limit_bytes=60 * 2**20),
        cost_estimate=cost(field * (6 * HEADS * PIX // 3)),
        name="attention",
    )(loss, grad, wproj, residual, stats, projected)
    wqkv_grad, w2_grad, grad_residual, shifted2, sums2 = call(
        middle_kernel,
        [loss, grad, attn, gqkv, wqkv, residual, stats, second],
        [shape(C, QKV), shape(C, 9 * C), shape(PIX, C, dtype=f32), shape(ROWS, TAPS), shape(8, C, dtype=f32)],
        [pltpu.VMEM((PIX, C), f32)],
        field * (9 * C + 2 * QKV), "middle", 1,
    )
    g1, sums1 = call(
        hidden_kernel,
        [shifted2, w2, hidden, stats],
        [shape(PIX, C), shape(8, C, dtype=f32)],
        [pltpu.VMEM((PIX, C), f32)],
        field * 9 * C, "hidden",
    )
    w1_grad, shifted1 = call(
        first_weight_kernel,
        [g1, first],
        [shape(C, 9 * C), shape(ROWS, TAPS)],
        [],
        field * 9 * C, "first_weight",
    )
    image_grad, sums0 = call(
        image_kernel,
        [shifted1, w1, x, stats, grad_residual],
        [shape(PIX, C), shape(8, C, dtype=f32)],
        [pltpu.VMEM((PIX, C), f32)],
        field * 9 * C, "image",
    )
    small_grad = jnp.concatenate(
        [
            sums0[0:1], sums1[0:1], sums2[0:1], sums0[1:2], sums1[1:2], sums2[1:2],
            sums1[2:3], sums2[2:3], sums1[3:5], sums2[3:5], proj_sums[0:1],
        ]
    )
    return block_out, image_grad, w1_grad, w2_grad, wqkv_grad, wproj_grad, small_grad


both = ("dp", "sp")
WIDTHS = (9 * C, 9 * C, 2 * C, QKV, ATT, 2 * PAD, PAD)


def time_embedding(steps):
    half_width = E // 2
    frequencies = jnp.exp(
        -math.log(10000.0) * jnp.arange(half_width, dtype=jnp.float32) / half_width
    )
    angles = steps.astype(jnp.float32)[:, None] * frequencies[None, :]
    return jnp.concatenate([jnp.cos(angles), jnp.sin(angles)], axis=1)


def padded_heads(value, axis):
    pads = [(0, 0)] * value.ndim
    pads[axis] = (0, PAD - HD)
    return jnp.pad(value, pads)


def embedding_rows(embedding, devices):
    share = C // devices
    by_device = embedding.reshape(devices, E // devices)
    wide = by_device[:, :share].reshape(C)
    narrow = jnp.repeat(by_device[:, share:], 3, axis=1).reshape(C)
    third = jnp.arange(C) % 3
    return jnp.stack([wide] + [jnp.where(third == k, narrow, 0.0) for k in range(3)])


def body(
    images,
    timesteps,
    loss_weight,
    out_grad,
    norm_gains,
    norm_biases,
    conv_biases,
    film_weight,
    film_bias,
    conv1_weight,
    conv2_weight,
    qkv_weight,
    qv_bias,
    proj_weight,
    proj_bias,
):
    row_parts = lax.axis_size("sp")
    devices = lax.axis_size("dp") * row_parts
    samples = images.shape[0] * images.shape[1]
    rows_here = images.shape[2]
    per = max(1, samples // row_parts)
    copies = max(1, row_parts // samples)
    share = C // devices
    embed_share = E // devices
    place = lax.axis_index("sp")

    def to_samples(value):
        value = value.reshape(samples // per, per * rows_here * W, C)
        if copies > 1:
            value = jnp.repeat(value, copies, axis=0)
        value = lax.all_to_all(value, "sp", split_axis=0, concat_axis=0, tiled=True)
        value = value.reshape(row_parts, per, rows_here * W, C).transpose(1, 0, 2, 3)
        return value.reshape(per, PIX, C)

    def to_rows(value):
        value = value.reshape(per, row_parts, rows_here * W, C).transpose(1, 0, 2, 3)
        value = value.reshape(row_parts, per * rows_here * W, C)
        value = lax.all_to_all(value, "sp", split_axis=0, concat_axis=0, tiled=True)
        return value[::copies].reshape(images.shape)

    first = (place // copies) * per
    steps = lax.dynamic_slice_in_dim(timesteps.reshape(samples), first, per)
    loss = lax.dynamic_slice_in_dim(loss_weight.reshape(samples), first, per)

    small = jnp.concatenate(
        [norm_gains, norm_biases, conv_biases, film_bias, qv_bias, proj_bias[None]], axis=0
    )
    by_input = lambda w: w.transpose(2, 0, 1, 3).reshape(share, 9 * C)
    film = film_weight.reshape(embed_share, 2 * C)
    packed = jnp.concatenate(
        [
            by_input(conv1_weight),
            by_input(conv2_weight),
            film[:share],
            padded_heads(qkv_weight, 3).reshape(share, QKV),
            padded_heads(proj_weight.transpose(2, 0, 1), 2).reshape(share, ATT),
            film[share:].reshape(share, 2 * PAD),
            jnp.pad(small.T, ((0, 0), (0, PAD - 13))),
        ],
        axis=1,
    )
    gathered = lax.all_gather(packed, both, axis=0, tiled=True)
    starts = [sum(WIDTHS[:k]) for k in range(len(WIDTHS))]
    weights = [gathered[:, s : s + w] for s, w in zip(starts, WIDTHS)]

    images_in = to_samples(images)
    grads_in = to_samples(out_grad)
    outs, image_grads, totals = [], [], None
    for index in range(per):
        embedding = embedding_rows(
            jax.nn.silu(time_embedding(steps[index][None]))[0], devices
        )
        emb = jnp.pad(jnp.stack(split3(embedding), axis=1).reshape(12, C), ((0, 4), (0, 0)))
        w1, w2, film1, wqkv, wproj, film2, small_w = weights
        block_out, image_grad, *grads, small_grad = sample_step(
            images_in[index], grads_in[index], loss[index].reshape(1, 1), w1, w2, wqkv, wproj,
            film1, film2, small_w, emb,
        )
        film_grad = small_grad[8:10].reshape(2 * C)
        thirds = film_grad.reshape(3, 2 * PAD)
        grads = [g.astype(f32) for g in grads] + [
            embedding[0][:, None] * film_grad[None],
            sum(embedding[k + 1][:, None] * thirds[k][None] for k in range(3)),
            jnp.pad(small_grad.T, ((0, 0), (0, PAD - 13))),
        ]
        outs.append(block_out)
        image_grads.append(image_grad)
        totals = grads if totals is None else [a + b for a, b in zip(totals, grads)]
    if copies > 1:
        totals = [jnp.where(place % copies == 0, t, 0.0) for t in totals]
    w1_grad, w2_grad, wqkv_grad, wproj_grad, film1_grad, film2_grad, small_grad = [
        t.astype(bf16) for t in totals
    ]
    reduce = lambda parts: lax.psum_scatter(
        jnp.concatenate(parts, axis=1).reshape(devices, share, -1), both, scatter_dimension=0
    ).astype(f32)
    early = reduce([w2_grad, wqkv_grad, wproj_grad])
    late = reduce([w1_grad, film1_grad, film2_grad, small_grad])
    conv = lambda g: g.reshape(share, 3, 3, C).transpose(1, 2, 0, 3)
    wqkv_grad = early[:, 9 * C : 9 * C + QKV].reshape(share, HEADS, 3, PAD)[..., :HD]
    wproj_grad = early[:, 9 * C + QKV :].reshape(share, HEADS, PAD)[..., :HD]
    film_grad = jnp.concatenate(
        [late[:, 9 * C : 11 * C], late[:, 11 * C : 11 * C + 2 * PAD].reshape(-1, 2 * C)]
    )
    small = late[:, 11 * C + 2 * PAD : 11 * C + 2 * PAD + 13].T
    return (
        to_rows(jnp.stack(outs)),
        to_rows(jnp.stack(image_grads)),
        small[0:3],
        small[3:6],
        small[6:8],
        film_grad.reshape(embed_share, 2, C),
        small[8:10],
        conv(late[:, : 9 * C]),
        conv(early[:, : 9 * C]),
        wqkv_grad,
        small[10:12],
        wproj_grad.transpose(1, 2, 0),
        small[12],
    )


def solution(mesh):
    return jax.shard_map(
        body,
        mesh=mesh,
        in_specs=(
            P(None, "dp", "sp", None, None),
            P(None, "dp"),
            P(None, "dp"),
            P(None, "dp", "sp", None, None),
            P(None, both),
            P(None, both),
            P(None, both),
            P(both, None, None),
            P(None, both),
            P(None, None, both, None),
            P(None, None, both, None),
            P(both, None, None, None),
            P(None, both),
            P(None, None, both),
            P(both),
        ),
        out_specs=(
            P(None, "dp", "sp", None, None),
            P(None, "dp", "sp", None, None),
            P(None, both),
            P(None, both),
            P(None, both),
            P(both, None, None),
            P(None, both),
            P(None, None, both, None),
            P(None, None, both, None),
            P(both, None, None, None),
            P(None, both),
            P(None, None, both),
            P(both),
        ),
        check_vma=False,
    )
```

```python
import functools
import functools
import math

import jax
import jax.numpy as jnp
from jax import lax
from jax.experimental import pallas as pl
from jax.experimental.pallas import tpu as pltpu
from jax.sharding import PartitionSpec as P

C = 384
E = 512
HEADS = 4
HD = 96
PAD = 128
GROUPS = 32
H = 32
W = 32
PIX = H * W
TAPS = 3 * C
QKV = HEADS * 3 * PAD
ATT = HEADS * PAD
ROWS = PIX + 2 * W
CHUNK = 128
norm_eps = 1e-05
bf16 = jnp.bfloat16
f32 = jnp.float32


def dot(a, b, ca=1, cb=0):
    return lax.dot_general(a, b, (((ca,), (cb,)), ((), ())), preferred_element_type=f32)


def rows(i, size=CHUNK):
    return pl.ds(pl.multiple_of(i * size, size), size)


def over(body, init, count=PIX // CHUNK, unroll=2):
    return lax.fori_loop(0, count, body, init, unroll=unroll)


def split3(v):
    hi = v.astype(bf16)
    rest = v - hi.astype(f32)
    mid = rest.astype(bf16)
    low = (rest - mid.astype(f32)).astype(bf16)
    return hi, mid, low


def same_group():
    lane = lax.broadcasted_iota(jnp.int32, (C, C), 1).astype(f32)
    sub = lax.broadcasted_iota(jnp.int32, (C, C), 0).astype(f32)
    width = GROUPS / C
    return (jnp.floor((lane + 0.5) * width) == jnp.floor((sub + 0.5) * width)).astype(f32).astype(bf16)


def group_means(vectors, ones):
    parts = [p for v in vectors for p in split3(v)]
    count = len(parts)
    stacked = jnp.concatenate(
        [p.astype(f32) for p in parts] + [jnp.zeros((16 - count, C), f32)], axis=0
    ).astype(bf16)
    sums = dot(stacked, ones)
    scale = 1.0 / (PIX * (C // GROUPS))
    return [
        (sums[3 * i : 3 * i + 1] + sums[3 * i + 1 : 3 * i + 2] + sums[3 * i + 2 : 3 * i + 3]) * scale
        for i in range(len(vectors))
    ]


def total(v):
    return jnp.sum(v, axis=0, keepdims=True)


def norm_stats(load, ones):
    zero = jnp.zeros((1, C), f32)
    (mean,) = group_means([over(lambda i, s: s + total(load(i)), zero)], ones)

    def square(i, s):
        centred = load(i) - mean
        return s + total(centred * centred)

    (variance,) = group_means([over(square, zero)], ones)
    return mean, lax.rsqrt(variance + norm_eps)


def put_shifted(dst, i, value, step):
    size = value.shape[0]
    column = lax.broadcasted_iota(jnp.int32, (size, C), 0) & (W - 1)
    at = pl.ds(pl.multiple_of(W + i * size, W), size)
    back = jnp.where(column == 0, 0.0, pltpu.roll(value, 1, 0))
    ahead = jnp.where(column == W - 1, 0.0, pltpu.roll(value, size - 1, 0))
    order = (back, value, ahead) if step == 1 else (ahead, value, back)
    for k in range(3):
        dst[at, k * C : (k + 1) * C] = order[k].astype(bf16)


def zero_edges(dst):
    dst[0:W, :] = jnp.zeros((W, TAPS), bf16)
    dst[W + PIX : ROWS, :] = jnp.zeros((W, TAPS), bf16)


def conv_rows(shifted, weight, i, size):
    acc = None
    for kh in range(3):
        part = dot(
            shifted[pl.ds(pl.multiple_of(i * size + kh * W, W), size), :],
            weight[kh * TAPS : (kh + 1) * TAPS, :],
        )
        acc = part if acc is None else acc + part
    return acc


def conv_back_rows(shifted, weight, i, size):
    acc = None
    for kh in range(3):
        part = dot(
            shifted[pl.ds(pl.multiple_of(i * size + (2 - kh) * W, W), size), :],
            weight[:, kh * TAPS : (kh + 1) * TAPS],
            1,
            1,
        )
        acc = part if acc is None else acc + part
    return acc


def sigmoid(v):
    return 1.0 / (1.0 + jnp.exp(-v))


def silu_grad(v):
    s = sigmoid(v)
    return s * (1.0 + v * (1.0 - s))


def fetch(pieces, places, dst, sems):
    copies = []
    for k, (piece, (row, column)) in enumerate(zip(pieces, places)):
        height, width = piece.shape
        copies.append(
            pltpu.make_async_copy(
                piece, dst.at[pl.ds(row, height), pl.ds(column, width)], sems.at[k]
            )
        )
        copies[-1].start()
    return copies


def settle(copies):
    for copy in copies:
        copy.wait()


def square_sum(ref, mean):
    def square(i, s):
        centred = ref[rows(i), :].astype(f32) - mean
        return s + total(centred * centred)

    return over(square, jnp.zeros((1, C), f32))


def prepare_kernel(conv_ref, gains, biases, conv_b, film_b, qv_b, proj_b, out_ref):
    for tap in range(9):
        out_ref[:, tap * C : (tap + 1) * C] = conv_ref[tap]
    share = out_ref.shape[0]
    stacked = jnp.concatenate(
        [ref[...].astype(f32) for ref in (gains, biases, conv_b, film_b, qv_b, proj_b)]
        + [jnp.zeros((3, share), f32)],
        axis=0,
    ).astype(bf16)
    unit = lax.broadcasted_iota(jnp.int32, (16, PAD), 0) == lax.broadcasted_iota(
        jnp.int32, (16, PAD), 1
    )
    out_ref[:, 9 * C :] = dot(stacked, unit.astype(f32).astype(bf16), 0, 0).astype(bf16)


def first_kernel(places, order_ref, x_ref, *refs):
    count = len(places)
    pieces = refs[:count]
    first_ref, hidden_ref, w1_ref, stats_ref, shifted, weight, raw, sems = refs[count:]
    copies = fetch(pieces, places, raw, sems)
    ones = same_group()
    zero_edges(shifted)
    order = order_ref[...]
    load = lambda i: x_ref[rows(i), :].astype(f32)
    mean0, inv0 = norm_stats(load, ones)
    settle(copies)
    par = dot(raw[:, 9 * C :], order, 0, 1)
    row = lambda k: par[k : k + 1, :]
    for tap in range(9):
        part = dot(order, raw[:, tap * C : (tap + 1) * C]).astype(bf16)
        weight[tap * C : (tap + 1) * C, :] = part
        w1_ref[:, tap * C : (tap + 1) * C] = part

    def start(i, carry):
        pre = (load(i) - mean0) * inv0 * row(0) + row(3)
        act = pre * sigmoid(pre)
        first_ref[rows(i), :] = act.astype(bf16)
        put_shifted(shifted, i, act, 1)
        return carry

    over(start, 0)

    def conv1(i, s):
        value = conv_rows(shifted, weight, i, 256) + row(6)
        hidden_ref[rows(i, 256), :] = value
        return s + total(value)

    sums = lax.fori_loop(0, PIX // 256, conv1, jnp.zeros((1, C), f32))
    (mean1,) = group_means([sums], ones)
    (var1,) = group_means([square_sum(hidden_ref, mean1)], ones)
    inv1 = lax.rsqrt(var1 + norm_eps)
    zero = jnp.zeros((1, C), f32)
    stats_ref[...] = jnp.concatenate(
        [mean0, inv0, mean1, inv1, zero, zero, zero, zero] + [par[0:13, :], jnp.zeros((3, C), f32)],
        axis=0,
    )


def second_kernel(places, order_ref, x_ref, hidden_ref, stats_ref, emb_ref, *refs):
    count = len(places)
    pieces = refs[:count]
    (
        second_ref, residual_ref, attn_ref, projected_ref, w2_ref, wqkv_ref, wproj_ref, norm_ref,
        shifted, weight, raw, sems,
    ) = refs[count:]
    copies = fetch(pieces, places, raw, sems)
    ones = same_group()
    zero_edges(shifted)
    order = order_ref[...]
    row = lambda k: stats_ref[8 + k : 9 + k, :]
    settle(copies)
    for tap in range(9):
        part = dot(order, raw[:, tap * C : (tap + 1) * C]).astype(bf16)
        weight[tap * C : (tap + 1) * C, :] = part
        w2_ref[:, tap * C : (tap + 1) * C] = part
    column = 9 * C
    wqkv_ref[...] = dot(order, raw[:, column : column + QKV]).astype(bf16)
    column += QKV
    wproj_ref[...] = dot(order, raw[:, column : column + ATT]).astype(bf16)
    column += ATT
    emb = dot(emb_ref[...], order).astype(bf16)
    wide = dot(emb, raw[:, column : column + 2 * C])
    column += 2 * C
    narrow = dot(emb, raw[:, column : column + 2 * PAD])
    film = total(wide[0:3]) + jnp.concatenate(
        [total(narrow[3 + 3 * k : 6 + 3 * k]) for k in range(3)], axis=1
    )
    scale = 1.0 + film[:, :C] + row(8)
    shift = film[:, C:] + row(9)
    mean1, inv1 = stats_ref[2:3, :], stats_ref[3:4, :]

    def middle(i, carry):
        norm = (hidden_ref[rows(i), :] - mean1) * inv1 * row(1) + row(4)
        scaled = norm * scale + shift
        act = scaled * sigmoid(scaled)
        second_ref[rows(i), :] = act.astype(bf16)
        put_shifted(shifted, i, act, 1)
        return carry

    over(middle, 0)

    def conv2(i, s):
        value = (
            conv_rows(shifted, weight, i, 256) + row(7) + x_ref[rows(i, 256), :].astype(f32)
        )
        residual_ref[rows(i, 256), :] = value
        return s + total(value)

    sums = lax.fori_loop(0, PIX // 256, conv2, jnp.zeros((1, C), f32))
    (mean2,) = group_means([sums], ones)
    (var2,) = group_means([square_sum(residual_ref, mean2)], ones)
    inv2 = lax.rsqrt(var2 + norm_eps)

    lane = lax.broadcasted_iota(jnp.int32, (8, PAD), 1)
    biases = []
    for g in range(HEADS):
        for which in (10, None, 11):
            if which is None:
                biases.append(jnp.zeros((1, PAD), f32))
            else:
                turned = jnp.broadcast_to(row(which), (8, C))
                if g:
                    turned = pltpu.roll(turned, C - g * HD, 1)
                biases.append(jnp.where(lane < HD, turned[:, :PAD], 0.0)[0:1])
    bias = jnp.concatenate(biases, axis=1)

    def last(i, carry):
        norm = (residual_ref[rows(i, 256), :] - mean2) * inv2 * row(2) + row(5)
        attn = norm.astype(bf16)
        attn_ref[rows(i, 256), :] = attn
        projected_ref[rows(i, 256), :] = (dot(attn, wqkv_ref[...]) + bias).astype(bf16)
        return carry

    lax.fori_loop(0, PIX // 256, last, 0)
    norm_ref[...] = jnp.concatenate([mean2, inv2, scale, shift, jnp.zeros((4, C), f32)], axis=0)


def attention_kernel(
    loss_ref, order_ref, grad_ref, wproj_ref, residual_ref, stats_ref, qkv_ref,
    out_ref, gqkv_ref, wproj_grad_ref, sums_ref,
    branch, attended, keys_grad, values_grad,
):
    g = pl.program_id(0)
    factor = 1.0 / math.sqrt(HD)
    size = 256

    @pl.when(g == 0)
    def _():
        def scaled(i, s):
            value = (grad_ref[rows(i), :].astype(f32) * loss_ref[0, 0]).astype(bf16)
            branch[rows(i), :] = value
            return s + total(value.astype(f32))

        sums_ref[...] = jnp.broadcast_to(over(scaled, jnp.zeros((1, C), f32)), (8, C))

    lanes = pl.ds(pl.multiple_of(g * PAD, PAD), PAD)
    keys_grad[...] = jnp.zeros_like(keys_grad)
    values_grad[...] = jnp.zeros_like(values_grad)

    def chunk(i, carry):
        queries = qkv_ref[rows(i, size), 0:PAD]
        keys = qkv_ref[:, PAD : 2 * PAD]
        values = qkv_ref[:, 2 * PAD : 3 * PAD]
        grad = dot(branch[rows(i, size), :], wproj_ref[:, lanes]).astype(bf16)
        scores = dot(queries, keys, 1, 1)
        top = jnp.max(scores, axis=1, keepdims=True)
        power = jnp.exp((scores - top) * factor)
        probs = power * (1.0 / jnp.sum(power, axis=1, keepdims=True))
        soft = probs.astype(bf16)
        attended[rows(i, size), lanes] = dot(soft, values).astype(bf16)
        grad_probs = dot(grad, values, 1, 1)
        inner = jnp.sum(grad_probs * probs, axis=1, keepdims=True)
        grad_scores = (probs * (grad_probs - inner)).astype(bf16)
        gqkv_ref[rows(i, size), 0:PAD] = (dot(grad_scores, keys) * factor).astype(bf16)
        keys_grad[...] += dot(queries, grad_scores, 0, 0)
        values_grad[...] += dot(grad, soft, 0, 0)
        return carry

    lax.fori_loop(0, PIX // size, chunk, 0)
    gqkv_ref[:, PAD : 2 * PAD] = (keys_grad[...].T * factor).astype(bf16)
    gqkv_ref[:, 2 * PAD : 3 * PAD] = values_grad[...].T.astype(bf16)

    @pl.when(g == HEADS - 1)
    def _():
        def project(i, carry):
            value = residual_ref[rows(i, size), :] + dot(attended[rows(i, size), :], wproj_ref[...], 1, 1)
            out_ref[rows(i, size), :] = (value + stats_ref[20:21, :]).astype(bf16)
            return carry

        lax.fori_loop(0, PIX // size, project, 0)
        turned = dot(order_ref[...], branch[...], 0, 1).astype(bf16)
        wproj_grad_ref[...] = dot(turned, attended[...]).astype(bf16)


def put_halves(own, other, column, value):
    at = slice(column, column + value.shape[1])
    own[:, at] = value[: C // 2].astype(bf16)
    other[:, at] = value[C // 2 :].astype(bf16)


def weight_grad(own, other, order, act, shifted):
    turned = dot(order, act[...], 0, 1).astype(bf16)
    for kh in range(3):
        part = dot(turned, shifted[(2 - kh) * W : (2 - kh) * W + PIX, :])
        put_halves(own, other, kh * TAPS, part)


def middle_kernel(
    loss_ref, order_ref, grad_ref, attn_ref, gqkv_ref, wqkv_ref, residual_ref, stats_ref, norm_ref,
    second_ref, wproj_grad_ref, own_ref, other_ref, grad_residual_ref, shifted, sums_ref, work,
):
    ones = same_group()
    zero_edges(shifted)
    size = 256
    mean, inv, gain = norm_ref[0:1, :], norm_ref[1:2, :], stats_ref[10:11, :]
    order = order_ref[...]
    zero = jnp.zeros((1, C), f32)

    def step(i, carry):
        q_sum, u_sum, p_sum = carry
        packed = gqkv_ref[rows(i, size), :]
        q = dot(packed, wqkv_ref[...], 1, 1)
        work[rows(i, size), :] = q
        u = (residual_ref[rows(i, size), :] - mean) * inv
        return q_sum + total(q), u_sum + total(q * u), p_sum + total(packed.astype(f32))

    q_sum, u_sum, p_sum = lax.fori_loop(0, PIX // size, step, (zero, zero, jnp.zeros((1, QKV), f32)))
    first, second = group_means([q_sum * gain, u_sum * gain], ones)
    turned = dot(order, attn_ref[...], 0, 1).astype(bf16)
    put_halves(own_ref, other_ref, 9 * C, dot(turned, gqkv_ref[...]))
    put_halves(own_ref, other_ref, 9 * C + QKV, wproj_grad_ref[...])

    def apply(i, s):
        u = (residual_ref[rows(i), :] - mean) * inv
        value = grad_ref[rows(i), :].astype(f32) * loss_ref[0, 0] + inv * (
            work[rows(i), :] * gain - first - u * second
        )
        grad_residual_ref[rows(i), :] = value
        rounded = value.astype(bf16).astype(f32)
        put_shifted(shifted, i, rounded, -1)
        return s + total(rounded)

    conv_sum = over(apply, zero)
    weight_grad(own_ref, other_ref, order, second_ref, shifted)

    def heads(k):
        value = jnp.zeros((8, C), f32)
        for g in range(HEADS):
            at = (3 * g + k) * PAD
            block = jnp.concatenate(
                [jnp.broadcast_to(p_sum[:, at : at + PAD], (8, PAD)), jnp.zeros((8, C - PAD), f32)], axis=1
            )
            value = value + (pltpu.roll(block, g * HD, 1) if g else block)
        return value[0:1]

    sums_ref[...] = jnp.concatenate(
        [u_sum, q_sum, conv_sum, heads(0), heads(2), jnp.zeros((3, C), f32)], axis=0
    )


def hidden_kernel(
    order_ref, emb_ref, shifted, w2_ref, hidden_ref, stats_ref, norm_ref,
    g1_ref, sums_ref, own_ref, other_ref, work,
):
    ones = same_group()
    size = 256
    stat = lambda k: stats_ref[k : k + 1, :]
    mean, inv, gain, bias = stat(2), stat(3), stat(9), stat(12)
    scale, shift = norm_ref[2:3, :], norm_ref[3:4, :]
    zero = jnp.zeros((1, C), f32)

    def step(i, carry):
        u_sum, s_sum = carry
        u = (hidden_ref[rows(i, size), :] - mean) * inv
        scaled = (u * gain + bias) * scale + shift
        value = conv_back_rows(shifted, w2_ref, i, size) * silu_grad(scaled)
        work[rows(i, size), :] = value
        return u_sum + total(value * u), s_sum + total(value)

    u_sum, s_sum = lax.fori_loop(0, PIX // size, step, (zero, zero))
    film0 = u_sum * gain + s_sum * bias
    u_up, s_up = u_sum * scale, s_sum * scale
    first, second = group_means([s_up * gain, u_up * gain], ones)
    factor = scale * gain

    def apply(i, s):
        u = (hidden_ref[rows(i), :] - mean) * inv
        value = (inv * (work[rows(i), :] * factor - first - u * second)).astype(bf16)
        g1_ref[rows(i), :] = value
        return s + total(value.astype(f32))

    conv_sum = over(apply, zero)
    sums_ref[...] = jnp.concatenate(
        [u_up, s_up, conv_sum, film0, s_sum, jnp.zeros((3, C), f32)], axis=0
    )
    emb = sum(dot(order_ref[...], part, 0, 1) for part in split3(emb_ref[...]))
    film = jnp.concatenate([film0, s_sum], axis=1)
    put_halves(own_ref, other_ref, 0, emb[:, 0:1] * film)
    narrow = sum(
        emb[:, k + 1 : k + 2] * film[:, k * 2 * PAD : (k + 1) * 2 * PAD] for k in range(3)
    )
    put_halves(own_ref, other_ref, 2 * C, narrow)


def late_kernel(
    order_ref, shifted, first_ref, proj_ref, sums2_ref, sums1_ref, sums0_ref, own_ref, other_ref
):
    order = order_ref[...]
    weight_grad(own_ref, other_ref, order, first_ref, shifted)
    stacked = jnp.concatenate(
        [
            sums0_ref[0:1, :], sums1_ref[0:1, :], sums2_ref[0:1, :],
            sums0_ref[1:2, :], sums1_ref[1:2, :], sums2_ref[1:2, :],
            sums1_ref[2:3, :], sums2_ref[2:3, :], sums1_ref[3:5, :], sums2_ref[3:5, :], proj_ref[0:1, :],
            jnp.zeros((PAD - 13, C), f32),
        ],
        axis=0,
    )
    put_halves(own_ref, other_ref, 9 * C, dot(order, stacked.astype(bf16), 0, 1))


def image_kernel(
    g1_ref, w1_ref, x_ref, stats_ref, grad_residual_ref, out_ref, sums_ref, shifted, work
):
    ones = same_group()
    zero_edges(shifted)

    def shift_rows(i, carry):
        put_shifted(shifted, i, g1_ref[rows(i), :].astype(f32), -1)
        return carry

    over(shift_rows, 0)
    size = 256
    stat = lambda k: stats_ref[k : k + 1, :]
    mean, inv, gain, bias = stat(0), stat(1), stat(8), stat(11)
    zero = jnp.zeros((1, C), f32)

    def step(i, carry):
        u_sum, s_sum = carry
        u = (x_ref[rows(i, size), :].astype(f32) - mean) * inv
        value = conv_back_rows(shifted, w1_ref, i, size) * silu_grad(u * gain + bias)
        work[rows(i, size), :] = value
        return u_sum + total(value * u), s_sum + total(value)

    u_sum, s_sum = lax.fori_loop(0, PIX // size, step, (zero, zero))
    first, second = group_means([s_sum * gain, u_sum * gain], ones)

    def apply(i, carry):
        u = (x_ref[rows(i), :].astype(f32) - mean) * inv
        value = inv * (work[rows(i), :] * gain - first - u * second)
        out_ref[rows(i), :] = (grad_residual_ref[rows(i), :] + value).astype(bf16)
        return carry

    over(apply, 0)
    sums_ref[...] = jnp.concatenate([u_sum, s_sum, jnp.zeros((6, C), f32)], axis=0)


VMEM = pl.BlockSpec(memory_space=pltpu.VMEM)
SMEM = pl.BlockSpec(memory_space=pltpu.SMEM)
ANY = pl.BlockSpec(memory_space=pl.ANY)
FIRST = 9 * C + PAD
SECOND = 9 * C + QKV + ATT + 2 * C + 2 * PAD
EARLY = 9 * C + QKV + ATT
FILM = 2 * C + 2 * PAD
LATE = 9 * C + PAD


def shape(*dims, dtype=bf16):
    return jax.ShapeDtypeStruct(dims, dtype)


def cost(us):
    return pl.CostEstimate(
        flops=int(us * 1_000_000_000), bytes_accessed=int(us * 3_600_000), transcendentals=0
    )


def call(kernel, operands, outs, scratch, us, name, scalars=0, pieces=0):
    whole = len(operands) - scalars - pieces
    return pl.pallas_call(
        kernel,
        out_shape=outs,
        in_specs=[SMEM] * scalars + [VMEM] * whole + [ANY] * pieces,
        out_specs=[VMEM] * len(outs),
        scratch_shapes=scratch,
        compiler_params=pltpu.CompilerParams(vmem_limit_bytes=60 * 2**20),
        cost_estimate=cost(us),
        name=name,
    )(*operands)


def prepare(conv, *small):
    share = conv.shape[2]
    return call(
        prepare_kernel, [conv.reshape(9, share, C), *small], [shape(share, FIRST)], [], 1, "prepare"
    )[0]


def forward_first(places, pieces, order, x):
    count = len(pieces)
    return call(
        functools.partial(first_kernel, places),
        [order, x, *pieces],
        [shape(PIX, C), shape(PIX, C, dtype=f32), shape(C, 9 * C), shape(24, C, dtype=f32)],
        [
            pltpu.VMEM((ROWS, TAPS), bf16), pltpu.VMEM((9 * C, C), bf16), pltpu.VMEM((C, FIRST), bf16),
            pltpu.SemaphoreType.DMA((count,)),
        ],
        13, "forward_first", 0, count,
    )


def forward_second(places, pieces, order, x, hidden, stats, emb):
    count = len(pieces)
    return call(
        functools.partial(second_kernel, places),
        [order, x, hidden, stats, emb, *pieces],
        [
            shape(PIX, C), shape(PIX, C, dtype=f32), shape(PIX, C), shape(PIX, QKV), shape(C, 9 * C),
            shape(C, QKV), shape(C, ATT), shape(8, C, dtype=f32),
        ],
        [
            pltpu.VMEM((ROWS, TAPS), bf16), pltpu.VMEM((9 * C, C), bf16), pltpu.VMEM((C, SECOND), bf16),
            pltpu.SemaphoreType.DMA((count,)),
        ],
        19, "forward_second", 0, count,
    )


def attend(loss, order, grad, wproj, residual, stats, projected):
    whole = lambda *dims: pl.BlockSpec(dims, lambda g: (0, 0))
    head = pl.BlockSpec((PIX, 3 * PAD), lambda g: (0, g))
    return pl.pallas_call(
        attention_kernel,
        grid=(HEADS,),
        out_shape=[shape(PIX, C), shape(PIX, QKV), shape(C, ATT), shape(8, C, dtype=f32)],
        in_specs=[SMEM, whole(C, C), whole(PIX, C), whole(C, ATT), whole(PIX, C), whole(24, C), head],
        out_specs=[whole(PIX, C), head, whole(C, ATT), whole(8, C)],
        scratch_shapes=[
            pltpu.VMEM((PIX, C), bf16), pltpu.VMEM((PIX, ATT), bf16),
            pltpu.VMEM((PAD, PIX), f32), pltpu.VMEM((PAD, PIX), f32),
        ],
        compiler_params=pltpu.CompilerParams(vmem_limit_bytes=60 * 2**20),
        cost_estimate=cost(31),
        name="attention",
    )(loss, order, grad, wproj, residual, stats, projected)


def backward_middle(loss, order, grad, attn, gqkv, wqkv, residual, stats, norm, second, wproj_grad):
    return call(
        middle_kernel,
        [loss, order, grad, attn, gqkv, wqkv, residual, stats, norm, second, wproj_grad],
        [
            shape(C // 2, EARLY), shape(C // 2, EARLY), shape(PIX, C, dtype=f32), shape(ROWS, TAPS),
            shape(8, C, dtype=f32),
        ],
        [pltpu.VMEM((PIX, C), f32)],
        16, "backward_middle", 1,
    )


def backward_hidden(order, emb, shifted, w2, hidden, stats, norm):
    return call(
        hidden_kernel,
        [order, emb, shifted, w2, hidden, stats, norm],
        [shape(PIX, C), shape(8, C, dtype=f32), shape(C // 2, FILM), shape(C // 2, FILM)],
        [pltpu.VMEM((PIX, C), f32)],
        10, "backward_hidden",
    )


def backward_image(g1, w1, x, stats, grad_residual):
    return call(
        image_kernel,
        [g1, w1, x, stats, grad_residual],
        [shape(PIX, C), shape(8, C, dtype=f32), shape(ROWS, TAPS)],
        [pltpu.VMEM((PIX, C), f32)],
        10, "backward_image",
    )


def backward_late(order, shifted, first, proj_sums, sums2, sums1, sums0):
    return call(
        late_kernel,
        [order, shifted, first, proj_sums, sums2, sums1, sums0],
        [shape(C // 2, LATE), shape(C // 2, LATE)],
        [],
        7, "backward_late",
    )


def finish_kernel(own_ref, got_ref, conv_ref, *outs):
    value = own_ref[...].astype(f32) + got_ref[...].astype(f32)
    for tap in range(9):
        conv_ref[tap] = value[:, tap * C : (tap + 1) * C]
    share = value.shape[0]
    small = jnp.concatenate([value[:, 9 * C :], jnp.zeros((PAD - share, PAD), f32)], axis=0).T
    row = 0
    for out in outs:
        out[...] = small[row : row + out.shape[0], :share]
        row += out.shape[0]


def finish(own, got):
    share = own.shape[0]
    return call(
        finish_kernel,
        [own, got],
        [shape(9, share, C, dtype=f32)] + [shape(n, share, dtype=f32) for n in (3, 3, 2, 2, 2, 1)],
        [], 1, "finish",
    )


def halves(width):
    return width * 11 // 16 // PAD * PAD


def corner_kernel(groups, *refs):
    owns, gots = refs[:groups], refs[groups : 2 * groups]
    left_ref, right_ref, *kept = refs[2 * groups :]
    block = kept[0].shape[0]
    cut = left_ref.shape[1]
    column = 0
    for own, got in zip(owns, gots):
        width = own.shape[1]
        for k in range(4):
            at = slice(k * block, (k + 1) * block)
            value = (own[at, :].astype(f32) + got[at, :].astype(f32)).astype(bf16)
            if k < 3:
                kept[k][:, column : column + width] = value
            else:
                split = min(max(cut - column, 0), width)
                if split > 0:
                    left_ref[:, column : column + split] = value[:, :split]
                if split < width:
                    start = column + split - cut
                    right_ref[:, start : start + width - split] = value[:, split:]
        column += width


def reduce_corner(owns, gots):
    block = owns[0].shape[0] // 4
    width = sum(own.shape[1] for own in owns)
    cut = halves(width)
    left, right, *kept = call(
        functools.partial(corner_kernel, len(owns)),
        [*owns, *gots],
        [shape(block, cut), shape(block, width - cut)] + [shape(block, width)] * 3,
        [], 2, "reduce_corner",
    )
    return left, right, kept


def side_kernel(left_ref, right_ref, y_ref, x_ref, to_y, to_x):
    cut = left_ref.shape[1]
    to_y[:, :cut] = (y_ref[:, :cut].astype(f32) + left_ref[...].astype(f32)).astype(bf16)
    to_y[:, cut:] = y_ref[:, cut:]
    to_x[:, :cut] = x_ref[:, :cut]
    to_x[:, cut:] = (x_ref[:, cut:].astype(f32) + right_ref[...].astype(f32)).astype(bf16)


def reduce_side(left, right, kept):
    own, to_y, to_x = kept
    to_y, to_x = call(
        side_kernel, [left, right, to_y, to_x], [shape(*to_y.shape)] * 2, [], 1, "reduce_side"
    )
    return own, to_x, to_y


def plane_kernel(own_ref, x_ref, y_ref, near_own, near_other):
    value = own_ref[...].astype(f32) + x_ref[...].astype(f32) + y_ref[...].astype(f32)
    near = near_own.shape[0]
    near_own[...] = value[:near].astype(bf16)
    near_other[...] = value[near:].astype(bf16)


def reduce_plane(own, got_x, got_y):
    block, width = own.shape
    return call(
        plane_kernel, [own, got_x, got_y], [shape(block // 2, width)] * 2, [], 1, "reduce_plane"
    )


both = ("dp", "sp")


def swap(value, axis, bit):
    count = lax.axis_size(axis)
    return lax.ppermute(value, axis, [(i, i ^ bit) for i in range(count)])


X, Y, CORE, Z_NEAR, Z_FAR = ("dp", 2), ("sp", 1), ("dp", 1), ("sp", 2), ("sp", 4)


def after(value, *others):
    return lax.optimization_barrier((value, *others))[0]


def gather_column(shard):
    block = jnp.concatenate([shard, swap(shard, *Z_FAR)])
    return jnp.concatenate([block, swap(block, *Z_NEAR)])


def gather_plane(block):
    return swap(block, *X), swap(block, *Y)


def gather_corner(from_x, from_y):
    cut = halves(from_x.shape[1])
    return swap(from_y[:, :cut], *X), swap(from_x[:, cut:], *Y)


def gather_rest(block, from_x, from_y, left, right):
    mine = [block, from_y, from_x, left, right]
    return mine + [swap(piece, *CORE) for piece in mine]


def add(a, b):
    return (a.astype(f32) + b.astype(f32)).astype(bf16)


def reduce_near(own, got):
    own = add(own, got)
    far = own.shape[0] // 2
    return own[:far], own[far:]


def piece_places(width):
    cut = halves(width)
    places = [(0, 0), (48, 0), (96, 0), (144, 0), (144, cut)]
    return places + [(row + C // 2, column) for row, column in places]


def row_order(tree):
    row = jnp.arange(C)
    if tree:
        share = C // 32
        k = row // share
        dp = lax.axis_index("dp") ^ (k >> 4) ^ ((k >> 3 & 1) * 2)
        sp = lax.axis_index("sp") ^ (k >> 2 & 1) ^ ((k >> 1 & 1) * 2) ^ ((k & 1) * 4)
        row = (dp * 8 + sp) * share + row % share
    return (jnp.arange(C)[:, None] == row[None, :]).astype(bf16)


def time_embedding(steps):
    half_width = E // 2
    frequencies = jnp.exp(
        -math.log(10000.0) * jnp.arange(half_width, dtype=jnp.float32) / half_width
    )
    angles = steps.astype(jnp.float32)[:, None] * frequencies[None, :]
    return jnp.concatenate([jnp.cos(angles), jnp.sin(angles)], axis=1)


def padded_heads(value, axis):
    pads = [(0, 0)] * value.ndim
    pads[axis] = (0, PAD - HD)
    return jnp.pad(value, pads)


def embedding_rows(embedding, devices):
    share = C // devices
    by_device = embedding.reshape(devices, E // devices)
    wide = by_device[:, :share].reshape(C)
    narrow = jnp.repeat(by_device[:, share:], 3, axis=1).reshape(C)
    third = jnp.arange(C) % 3
    return jnp.stack([wide] + [jnp.where(third == k, narrow, 0.0) for k in range(3)])


def body(
    images,
    timesteps,
    loss_weight,
    out_grad,
    norm_gains,
    norm_biases,
    conv_biases,
    film_weight,
    film_bias,
    conv1_weight,
    conv2_weight,
    qkv_weight,
    qv_bias,
    proj_weight,
    proj_bias,
):
    row_parts = lax.axis_size("sp")
    devices = lax.axis_size("dp") * row_parts
    samples = images.shape[0] * images.shape[1]
    rows_here = images.shape[2]
    per = max(1, samples // row_parts)
    copies = max(1, row_parts // samples)
    share = C // devices
    embed_share = E // devices
    place = lax.axis_index("sp")
    tree = lax.axis_size("dp") == 4 and row_parts == 8

    def to_samples(value):
        value = value.reshape(samples // per, per * rows_here * W, C)
        if copies > 1:
            value = jnp.repeat(value, copies, axis=0)
        value = lax.all_to_all(value, "sp", split_axis=0, concat_axis=0, tiled=True)
        value = value.reshape(row_parts, per, rows_here * W, C).transpose(1, 0, 2, 3)
        return value.reshape(per, PIX, C)

    def to_rows(value):
        value = value.reshape(per, row_parts, rows_here * W, C).transpose(1, 0, 2, 3)
        value = value.reshape(row_parts, per * rows_here * W, C)
        value = lax.all_to_all(value, "sp", split_axis=0, concat_axis=0, tiled=True)
        return value[::copies].reshape(images.shape)

    first = (place // copies) * per
    steps = lax.dynamic_slice_in_dim(timesteps.reshape(samples), first, per)
    loss = lax.dynamic_slice_in_dim(loss_weight.reshape(samples), first, per)

    first_shard = prepare(
        conv1_weight, norm_gains, norm_biases, conv_biases, film_bias, qv_bias, proj_bias[None]
    )
    by_input = lambda w: w.transpose(2, 0, 1, 3).reshape(share, 9 * C)
    film = film_weight.reshape(embed_share, 2 * C)
    second_shard = jnp.concatenate(
        [
            by_input(conv2_weight),
            padded_heads(qkv_weight, 3).reshape(share, QKV),
            padded_heads(proj_weight.transpose(2, 0, 1), 2).reshape(share, ATT),
            film[:share],
            film[share:].reshape(share, 2 * PAD),
        ],
        axis=1,
    )
    order = row_order(tree)
    staged = tree and per == 1
    if tree:
        places = piece_places
        block = gather_column(first_shard)
        from_x, from_y = gather_plane(block)
        second_block = gather_column(after(second_shard, block))
        images_in = to_samples(after(images, from_x, from_y))
        left, right = gather_corner(from_x, from_y)
        first_pieces = gather_rest(block, from_x, from_y, left, right)
        from_x, from_y = gather_plane(after(second_block, left, right))
        if not staged:
            second_pieces = gather_rest(
                second_block, from_x, from_y, *gather_corner(from_x, from_y)
            )
    else:
        places = lambda width: [(0, 0)]
        gather = lambda shard: [lax.all_gather(shard, both, axis=0, tiled=True)]
        first_pieces, second_pieces = gather(first_shard), gather(second_shard)
        images_in = to_samples(images)
    if not staged:
        grads_in = to_samples(out_grad)

    outs, image_grads, totals = [], [], None
    for index in range(per):
        embedding = embedding_rows(
            jax.nn.silu(time_embedding(steps[index][None]))[0], devices
        )
        emb = jnp.pad(jnp.stack(split3(embedding), axis=1).reshape(12, C), ((0, 4), (0, 0)))
        embedding = jnp.pad(embedding, ((0, 4), (0, 0)))
        weight = loss[index].reshape(1, 1)
        x = images_in[index]
        if staged:
            x = after(x, from_x, from_y)
            left, right = gather_corner(from_x, from_y)
        first, hidden, w1, stats = forward_first(places(FIRST), first_pieces, order, x)
        if staged:
            second_pieces = gather_rest(
                second_block, from_x, from_y, after(left, hidden), after(right, hidden)
            )
            grads_in = to_samples(after(out_grad, hidden))
        grad = grads_in[index]
        second, residual, attn, projected, w2, wqkv, wproj, norm = forward_second(
            places(SECOND), second_pieces, order, x, hidden, stats, emb
        )
        block_out, gqkv, wproj_grad, proj_sums = attend(
            weight, order, grad, wproj, residual, stats, projected
        )
        own, other, grad_residual, shifted, sums2 = backward_middle(
            weight, order, grad, attn, gqkv, wqkv, residual, stats, norm, second, wproj_grad
        )
        if staged:
            out_rows = to_rows(block_out[None])
            got = swap(other, *CORE)
            shifted = after(shifted, out_rows)
        g1, sums1, film_own, film_other = backward_hidden(
            order, embedding, shifted, w2, hidden, stats, norm
        )
        if staged:
            film_got = swap(film_other, *CORE)
            left, right, kept = reduce_corner([own, film_own], [after(got, g1), film_got])
            g1 = after(g1, left, right)
            left, right = swap(left, *X), swap(right, *Y)
        image_grad, sums0, shifted = backward_image(g1, w1, x, stats, grad_residual)
        if staged:
            left, right = after(left, image_grad), after(right, image_grad)
            own, to_x, to_y = reduce_side(left, right, kept)
            shifted = after(shifted, to_x, to_y)
            got_x, got_y = swap(to_x, *X), swap(to_y, *Y)
        late_own, late_other = backward_late(
            order, shifted, first, proj_sums, sums2, sums1, sums0
        )
        if staged:
            late_got = swap(late_other, *CORE)
            image_rows = to_rows(after(image_grad, late_other)[None])
        else:
            outs.append(block_out)
            image_grads.append(image_grad)
            grads = [
                jnp.concatenate(
                    [jnp.concatenate([own, film_own], axis=1), jnp.concatenate([other, film_other], axis=1)]
                ),
                jnp.concatenate([late_own, late_other]),
            ]
            grads = [g.astype(f32) for g in grads]
            totals = grads if totals is None else [a + b for a, b in zip(totals, grads)]
    if staged:
        left, right, kept = reduce_corner([late_own], [late_got])
        got_x, got_y = after(got_x, left, right), after(got_y, left, right)
        left, right = swap(left, *X), swap(right, *Y)
        own, other = reduce_plane(own, got_x, got_y)
        got = swap(other, *Z_NEAR)
        late_own, to_x, to_y = reduce_side(left, right, kept)
        got = after(got, to_x, to_y)
        got_x, got_y = swap(to_x, *X), swap(to_y, *Y)
        own, other = reduce_near(own, got)
        early = own.astype(f32) + swap(other, *Z_FAR).astype(f32)
        own, other = reduce_plane(late_own, got_x, got_y)
        own, other = reduce_near(own, swap(other, *Z_NEAR))
        late = own, swap(other, *Z_FAR)
        image_rows = after(image_rows, late[1])
    else:
        image_rows, out_rows = to_rows(jnp.stack(image_grads)), to_rows(jnp.stack(outs))
        if copies > 1:
            totals = [jnp.where(place % copies == 0, t, 0.0) for t in totals]
        if tree:
            totals = [jnp.dot(order, t.astype(bf16), preferred_element_type=f32) for t in totals]
        early, late = (
            lax.psum_scatter(
                t.astype(bf16).reshape(devices, share, -1), both, scatter_dimension=0
            ).astype(f32)
            for t in totals
        )
    if not staged:
        late = (late, jnp.zeros_like(late))
    conv1_grad, gains_grad, biases_grad, conv_b_grad, film_b_grad, qv_grad, proj_b_grad = finish(*late)
    conv2_grad = early[:, : 9 * C].reshape(share, 3, 3, C).transpose(1, 2, 0, 3)
    wqkv_grad = early[:, 9 * C : 9 * C + QKV].reshape(share, HEADS, 3, PAD)[..., :HD]
    wproj_grad = early[:, 9 * C + QKV : EARLY].reshape(share, HEADS, PAD)[..., :HD]
    film_grad = jnp.concatenate(
        [early[:, EARLY : EARLY + 2 * C], early[:, EARLY + 2 * C :].reshape(-1, 2 * C)]
    )
    return (
        out_rows,
        image_rows,
        gains_grad,
        biases_grad,
        conv_b_grad,
        film_grad.reshape(embed_share, 2, C),
        film_b_grad,
        conv1_grad.reshape(3, 3, share, C),
        conv2_grad,
        wqkv_grad,
        qv_grad,
        wproj_grad.transpose(1, 2, 0),
        proj_b_grad[0],
    )


def solution(mesh):
    return jax.shard_map(
        body,
        mesh=mesh,
        in_specs=(
            P(None, "dp", "sp", None, None),
            P(None, "dp"),
            P(None, "dp"),
            P(None, "dp", "sp", None, None),
            P(None, both),
            P(None, both),
            P(None, both),
            P(both, None, None),
            P(None, both),
            P(None, None, both, None),
            P(None, None, both, None),
            P(both, None, None, None),
            P(None, both),
            P(None, None, both),
            P(both),
        ),
        out_specs=(
            P(None, "dp", "sp", None, None),
            P(None, "dp", "sp", None, None),
            P(None, both),
            P(None, both),
            P(None, both),
            P(both, None, None),
            P(None, both),
            P(None, None, both, None),
            P(None, None, both, None),
            P(both, None, None, None),
            P(None, both),
            P(None, None, both),
            P(both),
        ),
        check_vma=False,
    )
```

```python
import functools
import functools
import math

import jax
import jax.numpy as jnp
from jax import lax
from jax.experimental import pallas as pl
from jax.experimental.pallas import tpu as pltpu
from jax.sharding import PartitionSpec as P

C = 384
E = 512
HEADS = 4
HD = 96
PAD = 128
GROUPS = 32
H = 32
W = 32
PIX = H * W
TAPS = 3 * C
QKV = HEADS * 3 * PAD
ATT = HEADS * PAD
ROWS = PIX + 2 * W
CHUNK = 128
SIZE = 512
norm_eps = 1e-05
bf16 = jnp.bfloat16
f32 = jnp.float32


def dot(a, b, ca=1, cb=0):
    return lax.dot_general(a, b, (((ca,), (cb,)), ((), ())), preferred_element_type=f32)


def rows(i, size=CHUNK):
    return pl.ds(pl.multiple_of(i * size, size), size)


def over(body, init, count=PIX // CHUNK, unroll=2):
    return lax.fori_loop(0, count, body, init, unroll=unroll)


def split3(v):
    hi = v.astype(bf16)
    rest = v - hi.astype(f32)
    mid = rest.astype(bf16)
    low = (rest - mid.astype(f32)).astype(bf16)
    return hi, mid, low


def same_group():
    lane = lax.broadcasted_iota(jnp.int32, (C, C), 1).astype(f32)
    sub = lax.broadcasted_iota(jnp.int32, (C, C), 0).astype(f32)
    width = GROUPS / C
    return (jnp.floor((lane + 0.5) * width) == jnp.floor((sub + 0.5) * width)).astype(f32).astype(bf16)


def group_means(vectors, ones):
    parts = [p for v in vectors for p in split3(v)]
    count = len(parts)
    stacked = jnp.concatenate(
        [p.astype(f32) for p in parts] + [jnp.zeros((16 - count, C), f32)], axis=0
    ).astype(bf16)
    sums = dot(stacked, ones)
    scale = 1.0 / (PIX * (C // GROUPS))
    return [
        (sums[3 * i : 3 * i + 1] + sums[3 * i + 1 : 3 * i + 2] + sums[3 * i + 2 : 3 * i + 3]) * scale
        for i in range(len(vectors))
    ]


def total(v):
    return jnp.sum(v, axis=0, keepdims=True)


def norm_stats(load, ones):
    zero = jnp.zeros((1, C), f32)
    (mean,) = group_means([over(lambda i, s: s + total(load(i)), zero)], ones)

    def square(i, s):
        centred = load(i) - mean
        return s + total(centred * centred)

    (variance,) = group_means([over(square, zero)], ones)
    return mean, lax.rsqrt(variance + norm_eps)


def put_shifted(dst, i, value, step):
    size = value.shape[0]
    column = lax.broadcasted_iota(jnp.int32, (size, C), 0) & (W - 1)
    at = pl.ds(pl.multiple_of(W + i * size, W), size)
    back = jnp.where(column == 0, 0.0, pltpu.roll(value, 1, 0))
    ahead = jnp.where(column == W - 1, 0.0, pltpu.roll(value, size - 1, 0))
    order = (back, value, ahead) if step == 1 else (ahead, value, back)
    for k in range(3):
        dst[at, k * C : (k + 1) * C] = order[k].astype(bf16)


def zero_edges(dst):
    dst[0:W, :] = jnp.zeros((W, TAPS), bf16)
    dst[W + PIX : ROWS, :] = jnp.zeros((W, TAPS), bf16)


def lay_shifted(mover, dst, src):
    zero_edges(dst)
    mover.ready(src)

    def step(i, carry):
        put_shifted(dst, i, src[rows(i), :].astype(f32), -1)
        return carry

    over(step, 0)


def conv_rows(shifted, weight, i, size):
    acc = None
    for kh in range(3):
        part = dot(
            shifted[pl.ds(pl.multiple_of(i * size + kh * W, W), size), :],
            weight[kh * TAPS : (kh + 1) * TAPS, :],
        )
        acc = part if acc is None else acc + part
    return acc


def conv_back_rows(shifted, weight, i, size):
    acc = None
    for kh in range(3):
        part = dot(
            shifted[pl.ds(pl.multiple_of(i * size + (2 - kh) * W, W), size), :],
            weight[:, kh * TAPS : (kh + 1) * TAPS],
            1,
            1,
        )
        acc = part if acc is None else acc + part
    return acc


def sigmoid(v):
    return 1.0 / (1.0 + jnp.exp(-v))


def silu_grad(v):
    s = sigmoid(v)
    return s * (1.0 + v * (1.0 - s))


def fetch(pieces, places, dst, sems):
    copies = []
    for k, (piece, (row, column)) in enumerate(zip(pieces, places)):
        height, width = piece.shape
        copies.append(
            pltpu.make_async_copy(
                piece, dst.at[pl.ds(row, height), pl.ds(column, width)], sems.at[k]
            )
        )
        copies[-1].start()
    return copies


def settle(copies):
    for copy in copies:
        copy.wait()


def square_sum(ref, mean):
    def square(i, s):
        centred = ref[rows(i), :].astype(f32) - mean
        return s + total(centred * centred)

    return over(square, jnp.zeros((1, C), f32))


def prepare_kernel(mover, conv_ref, gains, biases, conv_b, film_b, qv_b, proj_b, out_ref):
    mover.ready(conv_ref, gains, biases, conv_b, film_b, qv_b, proj_b)
    for tap in range(9):
        out_ref[:, tap * C : (tap + 1) * C] = conv_ref[tap]
    share = out_ref.shape[0]
    stacked = jnp.concatenate(
        [ref[...].astype(f32) for ref in (gains, biases, conv_b, film_b, qv_b, proj_b)]
        + [jnp.zeros((3, share), f32)],
        axis=0,
    ).astype(bf16)
    unit = lax.broadcasted_iota(jnp.int32, (16, PAD), 0) == lax.broadcasted_iota(
        jnp.int32, (16, PAD), 1
    )
    out_ref[:, 9 * C :] = dot(stacked, unit.astype(f32).astype(bf16), 0, 0).astype(bf16)


def first_kernel(places, mover, *refs):
    pieces, refs = refs[: len(places)], refs[len(places) :]
    (
        x_ref, order_ref, first_ref, hidden_ref, w1_ref, stats_ref, shifted, weight, raw, sems,
    ) = refs
    copies = fetch(pieces, places, raw, sems)
    ones = same_group()
    zero_edges(shifted)
    mover.ready(x_ref, order_ref)
    order = order_ref[...]
    load = lambda i: x_ref[rows(i), :].astype(f32)
    mean0, inv0 = norm_stats(load, ones)
    settle(copies)
    par = dot(raw[:, 9 * C :], order, 0, 1)
    row = lambda k: par[k : k + 1, :]
    for tap in range(9):
        part = dot(order, raw[:, tap * C : (tap + 1) * C]).astype(bf16)
        weight[tap * C : (tap + 1) * C, :] = part
        w1_ref[:, tap * C : (tap + 1) * C] = part
    mover.send(w1_ref)
    gain, bias = inv0 * row(0), row(3) - mean0 * inv0 * row(0)

    def start(i, carry):
        pre = load(i) * gain + bias
        act = pre * sigmoid(pre)
        first_ref[rows(i), :] = act.astype(bf16)
        put_shifted(shifted, i, act, 1)
        return carry

    over(start, 0)
    mover.send(first_ref)

    def conv1(i, s):
        value = conv_rows(shifted, weight, i, SIZE) + row(6)
        hidden_ref[rows(i, SIZE), :] = value
        return s + total(value)

    sums = lax.fori_loop(0, PIX // SIZE, conv1, jnp.zeros((1, C), f32))
    mover.send(hidden_ref)
    (mean1,) = group_means([sums], ones)
    (var1,) = group_means([square_sum(hidden_ref, mean1)], ones)
    inv1 = lax.rsqrt(var1 + norm_eps)
    zero = jnp.zeros((1, C), f32)
    stats_ref[...] = jnp.concatenate(
        [mean0, inv0, mean1, inv1, zero, zero, zero, zero] + [par[0:13, :], jnp.zeros((3, C), f32)],
        axis=0,
    )


def second_kernel(places, mover, *refs):
    pieces, refs = refs[: len(places)], refs[len(places) :]
    (
        order_ref, emb_ref, stats_ref, hidden_ref, x_ref,
        second_ref, residual_ref, attn_ref, projected_ref, w2_ref, wqkv_ref, wproj_ref, norm_ref,
        shifted, weight, raw, sems,
    ) = refs
    copies = fetch(pieces, places, raw, sems)
    ones = same_group()
    zero_edges(shifted)
    mover.ready(order_ref, emb_ref, stats_ref)
    order = order_ref[...]
    row = lambda k: stats_ref[8 + k : 9 + k, :]
    settle(copies)
    for tap in range(9):
        part = dot(order, raw[:, tap * C : (tap + 1) * C]).astype(bf16)
        weight[tap * C : (tap + 1) * C, :] = part
        w2_ref[:, tap * C : (tap + 1) * C] = part
    column = 9 * C
    wqkv_ref[...] = dot(order, raw[:, column : column + QKV]).astype(bf16)
    column += QKV
    wproj_ref[...] = dot(order, raw[:, column : column + ATT]).astype(bf16)
    column += ATT
    mover.send(w2_ref, wqkv_ref, wproj_ref)
    emb = dot(emb_ref[...], order).astype(bf16)
    wide = dot(emb, raw[:, column : column + 2 * C])
    column += 2 * C
    narrow = dot(emb, raw[:, column : column + 2 * PAD])
    film = total(wide[0:3]) + jnp.concatenate(
        [total(narrow[3 + 3 * k : 6 + 3 * k]) for k in range(3)], axis=1
    )
    scale = 1.0 + film[:, :C] + row(8)
    shift = film[:, C:] + row(9)
    mean1, inv1 = stats_ref[2:3, :], stats_ref[3:4, :]
    gain = inv1 * row(1) * scale
    bias = (row(4) - mean1 * inv1 * row(1)) * scale + shift
    mover.ready(hidden_ref, x_ref)

    def middle(i, carry):
        scaled = hidden_ref[rows(i), :] * gain + bias
        act = scaled * sigmoid(scaled)
        second_ref[rows(i), :] = act.astype(bf16)
        put_shifted(shifted, i, act, 1)
        return carry

    over(middle, 0)
    mover.send(second_ref)

    def conv2(i, s):
        value = (
            conv_rows(shifted, weight, i, SIZE) + row(7) + x_ref[rows(i, SIZE), :].astype(f32)
        )
        residual_ref[rows(i, SIZE), :] = value
        return s + total(value)

    sums = lax.fori_loop(0, PIX // SIZE, conv2, jnp.zeros((1, C), f32))
    mover.send(residual_ref)
    (mean2,) = group_means([sums], ones)
    (var2,) = group_means([square_sum(residual_ref, mean2)], ones)
    inv2 = lax.rsqrt(var2 + norm_eps)

    lane = lax.broadcasted_iota(jnp.int32, (8, PAD), 1)
    biases = []
    for g in range(HEADS):
        for which in (10, None, 11):
            if which is None:
                biases.append(jnp.zeros((1, PAD), f32))
            else:
                turned = jnp.broadcast_to(row(which), (8, C))
                if g:
                    turned = pltpu.roll(turned, C - g * HD, 1)
                biases.append(jnp.where(lane < HD, turned[:, :PAD], 0.0)[0:1])
    bias = jnp.concatenate(biases, axis=1)

    gain2, bias2 = inv2 * row(2), row(5) - mean2 * inv2 * row(2)

    def last(i, carry):
        attn = (residual_ref[rows(i, SIZE), :] * gain2 + bias2).astype(bf16)
        attn_ref[rows(i, SIZE), :] = attn
        projected_ref[rows(i, SIZE), :] = (dot(attn, wqkv_ref[...]) + bias).astype(bf16)
        return carry

    lax.fori_loop(0, PIX // SIZE, last, 0)
    norm_ref[...] = jnp.concatenate([mean2, inv2, scale, shift, jnp.zeros((4, C), f32)], axis=0)


def attention_kernel(
    loss_ref, order_any, residual_any, grad_ref, wproj_ref, stats_ref, qkv_ref,
    out_ref, gqkv_ref, wproj_grad_ref, sums_ref,
    branch, attended, keys_grad, values_grad, order_ref, residual_ref, sems,
):
    g = pl.program_id(0)
    factor = 1.0 / math.sqrt(HD)
    size = PIX
    loads = [
        pltpu.make_async_copy(residual_any, residual_ref, sems.at[0]),
        pltpu.make_async_copy(order_any, order_ref, sems.at[1]),
    ]

    @pl.when(g == 0)
    def _():
        for load in loads:
            load.start()

        def scaled(i, s):
            value = (grad_ref[rows(i), :].astype(f32) * loss_ref[0, 0]).astype(bf16)
            branch[rows(i), :] = value
            return s + total(value.astype(f32))

        sums_ref[...] = jnp.broadcast_to(over(scaled, jnp.zeros((1, C), f32)), (8, C))

    lanes = pl.ds(pl.multiple_of(g * PAD, PAD), PAD)
    keys_grad[...] = jnp.zeros_like(keys_grad)
    values_grad[...] = jnp.zeros_like(values_grad)

    def chunk(i, carry):
        queries = qkv_ref[rows(i, size), 0:PAD]
        keys = qkv_ref[:, PAD : 2 * PAD]
        values = qkv_ref[:, 2 * PAD : 3 * PAD]
        grad = dot(branch[rows(i, size), :], wproj_ref[:, lanes]).astype(bf16).astype(f32)
        scores = dot(queries, keys, 1, 1)
        top = jnp.max(scores, axis=1, keepdims=True)
        power = jnp.exp2((scores - top) * (factor * math.log2(math.e)))
        scale = 1.0 / jnp.sum(power, axis=1, keepdims=True)
        soft = power.astype(bf16)
        result = dot(soft, values) * scale
        attended[rows(i, size), lanes] = result.astype(bf16)
        inner = jnp.sum(grad * result, axis=1, keepdims=True) * scale
        grad = (grad * scale).astype(bf16)
        grad_scores = (power * (dot(grad, values, 1, 1) - inner)).astype(bf16)
        gqkv_ref[rows(i, size), 0:PAD] = (dot(grad_scores, keys) * factor).astype(bf16)
        keys_grad[...] += dot(queries, grad_scores, 0, 0)
        values_grad[...] += dot(grad, soft, 0, 0)
        return carry

    lax.fori_loop(0, PIX // size, chunk, 0)
    gqkv_ref[:, PAD : 2 * PAD] = (keys_grad[...].T * factor).astype(bf16)
    gqkv_ref[:, 2 * PAD : 3 * PAD] = values_grad[...].T.astype(bf16)

    @pl.when(g == HEADS - 1)
    def _():
        for load in loads:
            load.wait()

        def project(i, carry):
            value = residual_ref[rows(i, size), :] + dot(attended[rows(i, size), :], wproj_ref[...], 1, 1)
            out_ref[rows(i, size), :] = (value + stats_ref[20:21, :]).astype(bf16)
            return carry

        lax.fori_loop(0, PIX // size, project, 0)
        turned = dot(order_ref[...], branch[...], 0, 1).astype(bf16)
        wproj_grad_ref[...] = dot(turned, attended[...]).astype(bf16)


def put_halves(mover, own, others, column, value):
    at = slice(column, column + value.shape[1])
    block = C // 8
    for k, other in enumerate(others):
        other[:, at] = value[C // 2 + k * block : C // 2 + (k + 1) * block].astype(bf16)
        mover.send_columns(other, column, value.shape[1])
    own[:, at] = value[: C // 2].astype(bf16)
    mover.send_columns(own, column, value.shape[1])


def weight_grad(mover, own, others, order, act, shifted):
    turned = dot(order, act[...], 0, 1).astype(bf16)
    for kh in range(3):
        part = dot(turned, shifted[(2 - kh) * W : (2 - kh) * W + PIX, :])
        put_halves(mover, own, others, kh * TAPS, part)


def middle_kernel(
    mover, loss_ref, gqkv_ref, wqkv_ref, norm_ref, stats_ref, residual_ref, order_ref, attn_ref, grad_ref,
    second_ref, wproj_grad_ref, *refs,
):
    own_ref, *other_refs, grad_residual_ref, g2_ref, sums_ref, shifted, work = refs
    ones = same_group()
    zero_edges(shifted)
    size = SIZE
    mover.ready(gqkv_ref, wqkv_ref, norm_ref, stats_ref, residual_ref)
    mean, inv, gain = norm_ref[0:1, :], norm_ref[1:2, :], stats_ref[10:11, :]
    zero = jnp.zeros((1, C), f32)

    def step(i, carry):
        q_sum, u_sum, p_sum = carry
        packed = gqkv_ref[rows(i, size), :]
        q = dot(packed, wqkv_ref[...], 1, 1)
        work[rows(i, size), :] = q
        u = (residual_ref[rows(i, size), :] - mean) * inv
        return q_sum + total(q), u_sum + total(q * u), p_sum + total(packed.astype(f32))

    q_sum, u_sum, p_sum = lax.fori_loop(0, PIX // size, step, (zero, zero, jnp.zeros((1, QKV), f32)))
    first, second = group_means([q_sum * gain, u_sum * gain], ones)
    mover.ready(order_ref, attn_ref, grad_ref, second_ref, wproj_grad_ref)
    order = order_ref[...]
    turned = dot(order, attn_ref[...], 0, 1).astype(bf16)
    put_halves(mover, own_ref, other_refs, 9 * C, dot(turned, gqkv_ref[...]))
    put_halves(mover, own_ref, other_refs, 9 * C + QKV, wproj_grad_ref[...])

    def apply(i, s):
        u = (residual_ref[rows(i), :] - mean) * inv
        value = grad_ref[rows(i), :].astype(f32) * loss_ref[0, 0] + inv * (
            work[rows(i), :] * gain - first - u * second
        )
        grad_residual_ref[rows(i), :] = value
        rounded = value.astype(bf16)
        g2_ref[rows(i), :] = rounded
        rounded = rounded.astype(f32)
        put_shifted(shifted, i, rounded, -1)
        return s + total(rounded)

    conv_sum = over(apply, zero)
    mover.send(g2_ref, grad_residual_ref)
    weight_grad(mover, own_ref, other_refs, order, second_ref, shifted)

    def heads(k):
        value = jnp.zeros((8, C), f32)
        for g in range(HEADS):
            at = (3 * g + k) * PAD
            block = jnp.concatenate(
                [jnp.broadcast_to(p_sum[:, at : at + PAD], (8, PAD)), jnp.zeros((8, C - PAD), f32)], axis=1
            )
            value = value + (pltpu.roll(block, g * HD, 1) if g else block)
        return value[0:1]

    sums_ref[...] = jnp.concatenate(
        [u_sum, q_sum, conv_sum, heads(0), heads(2), jnp.zeros((3, C), f32)], axis=0
    )


def hidden_kernel(
    mover, g2_ref, w2_ref, hidden_ref, stats_ref, norm_ref, order_ref, emb_ref,
    g1_ref, sums_ref, own_ref, *refs,
):
    *other_refs, shifted, work = refs
    ones = same_group()
    size = SIZE
    lay_shifted(mover, shifted, g2_ref)
    mover.ready(w2_ref, hidden_ref, stats_ref, norm_ref)
    stat = lambda k: stats_ref[k : k + 1, :]
    mean, inv, gain, bias = stat(2), stat(3), stat(9), stat(12)
    scale, shift = norm_ref[2:3, :], norm_ref[3:4, :]
    zero = jnp.zeros((1, C), f32)

    def step(i, carry):
        u_sum, s_sum = carry
        u = (hidden_ref[rows(i, size), :] - mean) * inv
        scaled = (u * gain + bias) * scale + shift
        value = conv_back_rows(shifted, w2_ref, i, size) * silu_grad(scaled)
        work[rows(i, size), :] = value
        return u_sum + total(value * u), s_sum + total(value)

    u_sum, s_sum = lax.fori_loop(0, PIX // size, step, (zero, zero))
    film0 = u_sum * gain + s_sum * bias
    u_up, s_up = u_sum * scale, s_sum * scale
    first, second = group_means([s_up * gain, u_up * gain], ones)
    factor = scale * gain

    def apply(i, s):
        u = (hidden_ref[rows(i), :] - mean) * inv
        value = (inv * (work[rows(i), :] * factor - first - u * second)).astype(bf16)
        g1_ref[rows(i), :] = value
        return s + total(value.astype(f32))

    conv_sum = over(apply, zero)
    mover.send(g1_ref)
    sums_ref[...] = jnp.concatenate(
        [u_up, s_up, conv_sum, film0, s_sum, jnp.zeros((3, C), f32)], axis=0
    )
    mover.ready(order_ref, emb_ref)
    emb = sum(dot(order_ref[...], part, 0, 1) for part in split3(emb_ref[...]))
    film = jnp.concatenate([film0, s_sum], axis=1)
    put_halves(mover, own_ref, other_refs, 0, emb[:, 0:1] * film)
    narrow = sum(
        emb[:, k + 1 : k + 2] * film[:, k * 2 * PAD : (k + 1) * 2 * PAD] for k in range(3)
    )
    put_halves(mover, own_ref, other_refs, 2 * C, narrow)


def late_kernel(
    mover, g1_ref, first_ref, order_ref, proj_ref, sums2_ref, sums1_ref, sums0_ref, own_ref, *refs
):
    *other_refs, shifted = refs
    lay_shifted(mover, shifted, g1_ref)
    mover.ready(first_ref, order_ref, proj_ref, sums2_ref, sums1_ref, sums0_ref)
    order = order_ref[...]
    weight_grad(mover, own_ref, other_refs, order, first_ref, shifted)
    stacked = jnp.concatenate(
        [
            sums0_ref[0:1, :], sums1_ref[0:1, :], sums2_ref[0:1, :],
            sums0_ref[1:2, :], sums1_ref[1:2, :], sums2_ref[1:2, :],
            sums1_ref[2:3, :], sums2_ref[2:3, :], sums1_ref[3:5, :], sums2_ref[3:5, :], proj_ref[0:1, :],
            jnp.zeros((PAD - 13, C), f32),
        ],
        axis=0,
    )
    put_halves(mover, own_ref, other_refs, 9 * C, dot(order, stacked.astype(bf16), 0, 1))


def image_kernel(
    mover, g1_ref, w1_ref, stats_ref, x_ref, grad_residual_ref, out_ref, sums_ref, shifted, work
):
    ones = same_group()
    lay_shifted(mover, shifted, g1_ref)
    size = SIZE
    mover.ready(w1_ref, stats_ref, x_ref)
    stat = lambda k: stats_ref[k : k + 1, :]
    mean, inv, gain, bias = stat(0), stat(1), stat(8), stat(11)
    zero = jnp.zeros((1, C), f32)

    def step(i, carry):
        u_sum, s_sum = carry
        u = (x_ref[rows(i, size), :].astype(f32) - mean) * inv
        value = conv_back_rows(shifted, w1_ref, i, size) * silu_grad(u * gain + bias)
        work[rows(i, size), :] = value
        return u_sum + total(value * u), s_sum + total(value)

    u_sum, s_sum = lax.fori_loop(0, PIX // size, step, (zero, zero))
    first, second = group_means([s_sum * gain, u_sum * gain], ones)
    mover.ready(grad_residual_ref)

    def apply(i, carry):
        u = (x_ref[rows(i), :].astype(f32) - mean) * inv
        value = inv * (work[rows(i), :] * gain - first - u * second)
        out_ref[rows(i), :] = (grad_residual_ref[rows(i), :] + value).astype(bf16)
        return carry

    over(apply, 0)
    sums_ref[...] = jnp.concatenate([u_sum, s_sum, jnp.zeros((6, C), f32)], axis=0)


SMEM = pl.BlockSpec(memory_space=pltpu.SMEM)
ANY = pl.BlockSpec(memory_space=pl.ANY)
VMEM_LIMIT = 60 * 2**20
FIRST = 9 * C + PAD
SECOND = 9 * C + QKV + ATT + 2 * C + 2 * PAD
EARLY = 9 * C + QKV + ATT
FILM = 2 * C + 2 * PAD
LATE = 9 * C + PAD


def shape(*dims, dtype=bf16):
    return jax.ShapeDtypeStruct(dims, dtype)


def quarters(width):
    return [shape(C // 8, width)] * 4


def cost(us):
    return pl.CostEstimate(
        flops=int(us * 1_000_000_000), bytes_accessed=int(us * 3_600_000), transcendentals=0
    )


class Mover:
    def __init__(self, sources, inputs, outputs, targets, in_sems, out_sems):
        self.loads = {}
        for k, (source, buffer) in enumerate(zip(sources, inputs)):
            self.loads[id(buffer)] = pltpu.make_async_copy(source, buffer, in_sems.at[k])
            self.loads[id(buffer)].start()
        self.outputs = list(outputs)
        self.targets = {id(buffer): target for buffer, target in zip(outputs, targets)}
        self.sems = out_sems
        self.sent = []

    def ready(self, *buffers):
        for buffer in buffers:
            self.loads.pop(id(buffer)).wait()

    def store(self, source, target):
        copy = pltpu.make_async_copy(source, target, self.sems.at[len(self.sent)])
        copy.start()
        self.sent.append(copy)

    def send(self, *buffers):
        for buffer in buffers:
            self.outputs = [b for b in self.outputs if b is not buffer]
            self.store(buffer, self.targets[id(buffer)])

    def send_columns(self, buffer, start, width):
        self.outputs = [b for b in self.outputs if b is not buffer]
        at = (slice(None), pl.ds(start, width))
        self.store(buffer.at[at], self.targets[id(buffer)].at[at])

    def close(self):
        for load in self.loads.values():
            load.wait()
        self.send(*self.outputs)
        for copy in self.sent:
            copy.wait()


def call(kernel, operands, outs, scratch, us, name, scalars=0, pieces=0):
    count = len(operands) - scalars - pieces

    def body(*refs):
        fixed, refs = refs[: scalars + pieces], refs[scalars + pieces :]
        sources, refs = refs[:count], refs[count:]
        targets, refs = refs[: len(outs)], refs[len(outs) :]
        inputs, refs = refs[:count], refs[count:]
        outputs, refs = refs[: len(outs)], refs[len(outs) :]
        mover = Mover(sources, inputs, outputs, targets, refs[-2], refs[-1])
        kernel(mover, *fixed, *inputs, *outputs, *refs[:-2])
        mover.close()

    buffers = [pltpu.VMEM(v.shape, v.dtype) for v in [*operands[scalars + pieces :], *outs]]
    return pl.pallas_call(
        body,
        out_shape=outs,
        in_specs=[SMEM] * scalars + [ANY] * (pieces + count),
        out_specs=[ANY] * len(outs),
        scratch_shapes=buffers
        + scratch
        + [pltpu.SemaphoreType.DMA((max(count, 1),)), pltpu.SemaphoreType.DMA((len(outs) + 30,))],
        compiler_params=pltpu.CompilerParams(vmem_limit_bytes=VMEM_LIMIT),
        cost_estimate=cost(us),
        name=name,
    )(*operands)


def prepare(conv, *small):
    share = conv.shape[2]
    return call(
        prepare_kernel, [conv.reshape(9, share, C), *small], [shape(share, FIRST)], [], 1, "prepare"
    )[0]


def weight_scratch(pieces, width):
    return [
        pltpu.VMEM((ROWS, TAPS), bf16), pltpu.VMEM((9 * C, C), bf16), pltpu.VMEM((C, width), bf16),
        pltpu.SemaphoreType.DMA((len(pieces),)),
    ]


def forward_first(places, pieces, order, x):
    return call(
        functools.partial(first_kernel, places),
        [*pieces, x, order],
        [shape(PIX, C), shape(PIX, C, dtype=f32), shape(C, 9 * C), shape(24, C, dtype=f32)],
        weight_scratch(pieces, FIRST), 13, "forward_first", 0, len(pieces),
    )


def forward_second(places, pieces, order, x, hidden, stats, emb):
    return call(
        functools.partial(second_kernel, places),
        [*pieces, order, emb, stats, hidden, x],
        [
            shape(PIX, C), shape(PIX, C, dtype=f32), shape(PIX, C), shape(PIX, QKV), shape(C, 9 * C),
            shape(C, QKV), shape(C, ATT), shape(8, C, dtype=f32),
        ],
        weight_scratch(pieces, SECOND), 10, "forward_second", 0, len(pieces),
    )


def attend(loss, order, grad, wproj, residual, stats, projected):
    whole = lambda *dims: pl.BlockSpec(dims, lambda g: (0, 0))
    head = pl.BlockSpec((PIX, 3 * PAD), lambda g: (0, g))
    return pl.pallas_call(
        attention_kernel,
        grid=(HEADS,),
        out_shape=[shape(PIX, C), shape(PIX, QKV), shape(C, ATT), shape(8, C, dtype=f32)],
        in_specs=[SMEM, ANY, ANY, whole(PIX, C), whole(C, ATT), whole(24, C), head],
        out_specs=[whole(PIX, C), head, whole(C, ATT), whole(8, C)],
        scratch_shapes=[
            pltpu.VMEM((PIX, C), bf16), pltpu.VMEM((PIX, ATT), bf16),
            pltpu.VMEM((PAD, PIX), f32), pltpu.VMEM((PAD, PIX), f32),
            pltpu.VMEM((C, C), bf16), pltpu.VMEM((PIX, C), f32), pltpu.SemaphoreType.DMA((2,)),
        ],
        compiler_params=pltpu.CompilerParams(vmem_limit_bytes=VMEM_LIMIT),
        cost_estimate=cost(31),
        name="attention",
    )(loss, order, residual, grad, wproj, stats, projected)


def backward_middle(loss, order, grad, attn, gqkv, wqkv, residual, stats, norm, second, wproj_grad):
    own, *others, grad_residual, g2, sums = call(
        middle_kernel,
        [loss, gqkv, wqkv, norm, stats, residual, order, attn, grad, second, wproj_grad],
        [
            shape(C // 2, EARLY), *quarters(EARLY), shape(PIX, C, dtype=f32), shape(PIX, C),
            shape(8, C, dtype=f32),
        ],
        [pltpu.VMEM((ROWS, TAPS), bf16), pltpu.VMEM((PIX, C), f32)], 16, "backward_middle", 1,
    )
    return own, others, grad_residual, g2, sums


def backward_hidden(order, emb, g2, w2, hidden, stats, norm):
    g1, sums, own, *others = call(
        hidden_kernel,
        [g2, w2, hidden, stats, norm, order, emb],
        [shape(PIX, C), shape(8, C, dtype=f32), shape(C // 2, FILM), *quarters(FILM)],
        [pltpu.VMEM((ROWS, TAPS), bf16), pltpu.VMEM((PIX, C), f32)], 10, "backward_hidden",
    )
    return g1, sums, own, others


def backward_late(order, g1, first, proj_sums, sums2, sums1, sums0):
    own, *others = call(
        late_kernel,
        [g1, first, order, proj_sums, sums2, sums1, sums0],
        [shape(C // 2, LATE), *quarters(LATE)],
        [pltpu.VMEM((ROWS, TAPS), bf16)], 7, "backward_late",
    )
    return own, others


def backward_image(g1, w1, x, stats, grad_residual):
    return call(
        image_kernel,
        [g1, w1, stats, x, grad_residual],
        [shape(PIX, C), shape(8, C, dtype=f32)],
        [pltpu.VMEM((ROWS, TAPS), bf16), pltpu.VMEM((PIX, C), f32)], 10, "backward_image",
    )


def finish_kernel(mover, *refs):
    parts, (conv_ref, *outs) = refs[:4], refs[4:]
    mover.ready(*parts)
    value = sum(part[...].astype(f32) for part in parts)
    for tap in range(9):
        conv_ref[tap] = value[:, tap * C : (tap + 1) * C]
    share = value.shape[0]
    small = jnp.concatenate([value[:, 9 * C :], jnp.zeros((PAD - share, PAD), f32)], axis=0).T
    row = 0
    for out in outs:
        out[...] = small[row : row + out.shape[0], :share]
        row += out.shape[0]


def finish(parts):
    share = parts[0].shape[0]
    return call(
        finish_kernel,
        parts,
        [shape(9, share, C, dtype=f32)] + [shape(n, share, dtype=f32) for n in (3, 3, 2, 2, 2, 1)],
        [], 1, "finish",
    )


def halves(width):
    return width // 2 // PAD * PAD


def corner_kernel(groups, mover, *refs):
    owns, gots, refs = refs[:groups], refs[groups : 5 * groups], refs[5 * groups :]
    mover.ready(*owns, *gots)
    left_ref, right_ref, *kept = refs
    block = kept[0].shape[0]
    cut = left_ref.shape[1]
    column = 0
    for group, own in enumerate(owns):
        width = own.shape[1]
        for k in range(4):
            got = gots[4 * group + k][...].astype(f32)
            value = (own[k * block : (k + 1) * block, :].astype(f32) + got).astype(bf16)
            if k < 3:
                kept[k][:, column : column + width] = value
            else:
                split = min(max(cut - column, 0), width)
                if split > 0:
                    left_ref[:, column : column + split] = value[:, :split]
                if split < width:
                    start = column + split - cut
                    right_ref[:, start : start + width - split] = value[:, split:]
        column += width


def reduce_corner(owns, gots):
    block = owns[0].shape[0] // 4
    width = sum(own.shape[1] for own in owns)
    cut = halves(width)
    left, right, *kept = call(
        functools.partial(corner_kernel, len(owns)),
        [*owns, *gots],
        [shape(block, cut), shape(block, width - cut)] + [shape(block, width)] * 3,
        [], 2, "reduce_corner",
    )
    return left, right, kept


def side_kernel(mover, left_ref, right_ref, y_ref, x_ref, to_y, to_x):
    mover.ready(left_ref, right_ref, y_ref, x_ref)
    cut = left_ref.shape[1]
    to_y[:, :cut] = (y_ref[:, :cut].astype(f32) + left_ref[...].astype(f32)).astype(bf16)
    to_y[:, cut:] = y_ref[:, cut:]
    to_x[:, :cut] = x_ref[:, :cut]
    to_x[:, cut:] = (x_ref[:, cut:].astype(f32) + right_ref[...].astype(f32)).astype(bf16)


def reduce_side(left, right, kept):
    own, to_y, to_x = kept
    to_y, to_x = call(
        side_kernel, [left, right, to_y, to_x], [shape(*to_y.shape)] * 2, [], 1, "reduce_side"
    )
    return own, to_x, to_y


def column_kernel(mover, *refs):
    outs, parts = refs[-4:], refs[:-4]
    mover.ready(*parts)
    value = sum(part[...].astype(f32) for part in parts)
    share = outs[0].shape[0]
    for k, out in enumerate(outs):
        out[...] = value[k * share : (k + 1) * share].astype(bf16)


def reduce_plane(*parts):
    block, width = parts[0].shape
    return call(column_kernel, parts, [shape(block // 4, width)] * 4, [], 1, "reduce_plane")


def core_kernel(groups, mover, *refs):
    owns, gots = refs[:groups], refs[groups : 5 * groups]
    sides = refs[5 * groups :]
    mover.ready(*owns, *gots)
    block = sides[0].shape[0] // 2
    column = 0
    for group, own in enumerate(owns):
        width = own.shape[1]
        for k in range(4):
            got = gots[4 * group + k][...].astype(f32)
            value = (own[k * block : (k + 1) * block, :].astype(f32) + got).astype(bf16)
            at = slice((k % 2) * block, (k % 2 + 1) * block)
            sides[k // 2][at, column : column + width] = value
        column += width


def reduce_core(owns, gots):
    block = owns[0].shape[0] // 4
    width = sum(own.shape[1] for own in owns)
    return call(
        functools.partial(core_kernel, len(owns)),
        [*owns, *gots], [shape(2 * block, width)] * 2, [], 3, "reduce_core",
    )


def cross_kernel(mover, own_ref, got_ref, *outs):
    mover.ready(own_ref, got_ref)
    block = outs[0].shape[0]
    for k, out in enumerate(outs):
        at = slice(k * block, (k + 1) * block)
        out[...] = (own_ref[at, :].astype(f32) + got_ref[at, :].astype(f32)).astype(bf16)


def reduce_cross(own, got):
    block, width = own.shape
    return call(cross_kernel, [own, got], [shape(block // 2, width)] * 2, [], 2, "reduce_cross")


both = ("dp", "sp")


def swap(value, axis, bit):
    count = lax.axis_size(axis)
    return lax.ppermute(value, axis, [(i, i ^ bit) for i in range(count)])


X, Y, CORE, Z_NEAR, Z_FAR = ("dp", 2), ("sp", 1), ("dp", 1), ("sp", 2), ("sp", 4)
Z_BOTH = ("sp", 6)


def after(value, *others):
    return lax.optimization_barrier((value, *others))[0]


def gather_column(shard):
    block = jnp.concatenate([shard, swap(shard, *Z_FAR)])
    return jnp.concatenate([block, swap(block, *Z_NEAR)])


def gather_plane(block):
    return swap(block, *X), swap(block, *Y)


def gather_corner(from_x, from_y):
    cut = halves(from_x.shape[1])
    return swap(from_y[:, :cut], *X), swap(from_x[:, cut:], *Y)


def gather_rest(block, from_x, from_y, left, right):
    mine = [block, from_y, from_x, left, right]
    return mine + [swap(piece, *CORE) for piece in mine]


def swap_column(shards):
    own, far, near, both_ways = shards
    return [own, swap(far, *Z_FAR), swap(near, *Z_NEAR), swap(both_ways, *Z_BOTH)]


def piece_places(width):
    cut = halves(width)
    places = [(0, 0), (48, 0), (96, 0), (144, 0), (144, cut)]
    return places + [(row + C // 2, column) for row, column in places]


def row_order(tree):
    row = jnp.arange(C)
    if tree:
        share = C // 32
        k = row // share
        dp = lax.axis_index("dp") ^ (k >> 4) ^ ((k >> 3 & 1) * 2)
        sp = lax.axis_index("sp") ^ (k >> 2 & 1) ^ ((k >> 1 & 1) * 2) ^ ((k & 1) * 4)
        row = (dp * 8 + sp) * share + row % share
    return (jnp.arange(C)[:, None] == row[None, :]).astype(bf16)


def time_embedding(steps):
    half_width = E // 2
    frequencies = jnp.exp(
        -math.log(10000.0) * jnp.arange(half_width, dtype=jnp.float32) / half_width
    )
    angles = steps.astype(jnp.float32)[:, None] * frequencies[None, :]
    return jnp.concatenate([jnp.cos(angles), jnp.sin(angles)], axis=1)


def padded_heads(value, axis):
    pads = [(0, 0)] * value.ndim
    pads[axis] = (0, PAD - HD)
    return jnp.pad(value, pads)


def embedding_rows(embedding, devices):
    share = C // devices
    by_device = embedding.reshape(devices, E // devices)
    wide = by_device[:, :share].reshape(C)
    narrow = jnp.repeat(by_device[:, share:], 3, axis=1).reshape(C)
    third = jnp.arange(C) % 3
    return jnp.stack([wide] + [jnp.where(third == k, narrow, 0.0) for k in range(3)])


def body(
    images,
    timesteps,
    loss_weight,
    out_grad,
    norm_gains,
    norm_biases,
    conv_biases,
    film_weight,
    film_bias,
    conv1_weight,
    conv2_weight,
    qkv_weight,
    qv_bias,
    proj_weight,
    proj_bias,
):
    row_parts = lax.axis_size("sp")
    devices = lax.axis_size("dp") * row_parts
    samples = images.shape[0] * images.shape[1]
    rows_here = images.shape[2]
    per = max(1, samples // row_parts)
    copies = max(1, row_parts // samples)
    share = C // devices
    embed_share = E // devices
    place = lax.axis_index("sp")
    tree = lax.axis_size("dp") == 4 and row_parts == 8

    def to_samples(value):
        value = value.reshape(samples // per, per * rows_here * W, C)
        if copies > 1:
            value = jnp.repeat(value, copies, axis=0)
        value = lax.all_to_all(value, "sp", split_axis=0, concat_axis=0, tiled=True)
        value = value.reshape(row_parts, per, rows_here * W, C).transpose(1, 0, 2, 3)
        return value.reshape(per, PIX, C)

    def to_rows(value):
        value = value.reshape(per, row_parts, rows_here * W, C).transpose(1, 0, 2, 3)
        value = value.reshape(row_parts, per * rows_here * W, C)
        value = lax.all_to_all(value, "sp", split_axis=0, concat_axis=0, tiled=True)
        return value[::copies].reshape(images.shape)

    first = (place // copies) * per
    steps = lax.dynamic_slice_in_dim(timesteps.reshape(samples), first, per)
    loss = lax.dynamic_slice_in_dim(loss_weight.reshape(samples), first, per)

    first_shard = prepare(
        conv1_weight, norm_gains, norm_biases, conv_biases, film_bias, qv_bias, proj_bias[None]
    )
    by_input = lambda w: w.transpose(2, 0, 1, 3).reshape(share, 9 * C)
    film = film_weight.reshape(embed_share, 2 * C)
    second_shard = jnp.concatenate(
        [
            by_input(conv2_weight),
            padded_heads(qkv_weight, 3).reshape(share, QKV),
            padded_heads(proj_weight.transpose(2, 0, 1), 2).reshape(share, ATT),
            film[:share],
            film[share:].reshape(share, 2 * PAD),
        ],
        axis=1,
    )
    order = row_order(tree)
    staged = tree and per == 1
    if tree:
        places = piece_places
        block = gather_column(first_shard)
        from_x, from_y = gather_plane(block)
        second_block = gather_column(after(second_shard, block))
        images_in = to_samples(images)
        left, right = gather_corner(from_x, from_y)
        first_pieces = gather_rest(block, from_x, from_y, left, right)
        from_x, from_y = gather_plane(after(second_block, left, right, images_in))
        if not staged:
            second_pieces = gather_rest(
                second_block, from_x, from_y, *gather_corner(from_x, from_y)
            )
    else:
        places = lambda width: [(0, 0)]
        gather = lambda shard: [lax.all_gather(shard, both, axis=0, tiled=True)]
        first_pieces, second_pieces = gather(first_shard), gather(second_shard)
        images_in = to_samples(images)
    if not staged:
        grads_in = to_samples(out_grad)

    outs, image_grads, totals = [], [], None
    for index in range(per):
        embedding = embedding_rows(
            jax.nn.silu(time_embedding(steps[index][None]))[0], devices
        )
        emb = jnp.pad(jnp.stack(split3(embedding), axis=1).reshape(12, C), ((0, 4), (0, 0)))
        embedding = jnp.pad(embedding, ((0, 4), (0, 0)))
        weight = loss[index].reshape(1, 1)
        x = images_in[index]
        if staged:
            x = after(x, second_block)
        first, hidden, w1, stats = forward_first(places(FIRST), first_pieces, order, x)
        if staged:
            from_x, from_y = after(from_x, hidden), after(from_y, hidden)
            left, right = gather_corner(from_x, from_y)
            grads_in = to_samples(after(out_grad, from_x, from_y))
            second_pieces = gather_rest(second_block, from_x, from_y, left, right)
        grad = grads_in[index]
        second, residual, attn, projected, w2, wqkv, wproj, norm = forward_second(
            places(SECOND), second_pieces, order, x, hidden, stats, emb
        )
        block_out, gqkv, wproj_grad, proj_sums = attend(
            weight, order, grad, wproj, residual, stats, projected
        )
        own, others, grad_residual, g2, sums2 = backward_middle(
            weight, order, grad, attn, gqkv, wqkv, residual, stats, norm, second, wproj_grad
        )
        if staged:
            out_rows = to_rows(block_out[None])
            gots = [swap(other, *CORE) for other in others]
        g1, sums1, film_own, film_others = backward_hidden(
            order, embedding, g2, w2, hidden, stats, norm
        )
        if staged:
            gots = [after(got, g1) for got in gots] + [swap(other, *CORE) for other in film_others]
            own, to_x = reduce_core([own, film_own], gots)
            g1 = after(g1, to_x, out_rows)
            got_x = swap(to_x, *X)
        image_grad, sums0 = backward_image(g1, w1, x, stats, grad_residual)
        if staged:
            image_rows = to_rows(image_grad[None])
            g1 = after(g1, image_grad)
        late_own, late_others = backward_late(order, g1, first, proj_sums, sums2, sums1, sums0)
        if staged:
            late_gots = [swap(other, *CORE) for other in late_others]
        else:
            outs.append(block_out)
            image_grads.append(image_grad)
            grads = [
                jnp.concatenate(
                    [jnp.concatenate([own, *others]), jnp.concatenate([film_own, *film_others])], axis=1
                ),
                jnp.concatenate([late_own, *late_others]),
            ]
            grads = [g.astype(f32) for g in grads]
            totals = grads if totals is None else [a + b for a, b in zip(totals, grads)]
    if staged:
        own, to_y = reduce_cross(own, after(got_x, late_own))
        got_y = swap(to_y, *Y)
        left, right, kept = reduce_corner([late_own], [after(got, to_y) for got in late_gots])
        left, right = swap(left, *X), swap(right, *Y)
        early = reduce_plane(own, got_y)
        left, right, image_rows, *_ = lax.optimization_barrier((left, right, image_rows, *early))
        early = swap_column(early)
        late_own, to_x, to_y = reduce_side(left, right, kept)
        late_x, late_y = swap(to_x, *X), swap(to_y, *Y)
        late = reduce_plane(late_own, late_x, late_y)
        early[1:] = [after(part, *late) for part in early[1:]]
        late = swap_column(late)
        early = sum(part.astype(f32) for part in early)
    else:
        image_rows, out_rows = to_rows(jnp.stack(image_grads)), to_rows(jnp.stack(outs))
        if copies > 1:
            totals = [jnp.where(place % copies == 0, t, 0.0) for t in totals]
        if tree:
            totals = [jnp.dot(order, t.astype(bf16), preferred_element_type=f32) for t in totals]
        early, late = (
            lax.psum_scatter(
                t.astype(bf16).reshape(devices, share, -1), both, scatter_dimension=0
            ).astype(f32)
            for t in totals
        )
    if not staged:
        late = [late] + [jnp.zeros_like(late)] * 3
    conv1_grad, gains_grad, biases_grad, conv_b_grad, film_b_grad, qv_grad, proj_b_grad = finish(late)
    conv2_grad = early[:, : 9 * C].reshape(share, 3, 3, C).transpose(1, 2, 0, 3)
    wqkv_grad = early[:, 9 * C : 9 * C + QKV].reshape(share, HEADS, 3, PAD)[..., :HD]
    wproj_grad = early[:, 9 * C + QKV : EARLY].reshape(share, HEADS, PAD)[..., :HD]
    film_grad = jnp.concatenate(
        [early[:, EARLY : EARLY + 2 * C], early[:, EARLY + 2 * C :].reshape(-1, 2 * C)]
    )
    return (
        out_rows,
        image_rows,
        gains_grad,
        biases_grad,
        conv_b_grad,
        film_grad.reshape(embed_share, 2, C),
        film_b_grad,
        conv1_grad.reshape(3, 3, share, C),
        conv2_grad,
        wqkv_grad,
        qv_grad,
        wproj_grad.transpose(1, 2, 0),
        proj_b_grad[0],
    )


def solution(mesh):
    return jax.shard_map(
        body,
        mesh=mesh,
        in_specs=(
            P(None, "dp", "sp", None, None),
            P(None, "dp"),
            P(None, "dp"),
            P(None, "dp", "sp", None, None),
            P(None, both),
            P(None, both),
            P(None, both),
            P(both, None, None),
            P(None, both),
            P(None, None, both, None),
            P(None, None, both, None),
            P(both, None, None, None),
            P(None, both),
            P(None, None, both),
            P(both),
        ),
        out_specs=(
            P(None, "dp", "sp", None, None),
            P(None, "dp", "sp", None, None),
            P(None, both),
            P(None, both),
            P(None, both),
            P(both, None, None),
            P(None, both),
            P(None, None, both, None),
            P(None, None, both, None),
            P(both, None, None, None),
            P(None, both),
            P(None, None, both),
            P(both),
        ),
        check_vma=False,
    )
```

```python
import functools
import functools
import math

import jax
import jax.numpy as jnp
from jax import lax
from jax.experimental import pallas as pl
from jax.experimental.pallas import tpu as pltpu
from jax.sharding import PartitionSpec as P

C = 384
E = 512
HEADS = 4
HD = 96
PAD = 128
GROUPS = 32
H = 32
W = 32
PIX = H * W
TAPS = 3 * C
QKV = HEADS * 3 * PAD
ATT = HEADS * PAD
ROWS = PIX + 2 * W
CHUNK = 128
SIZE = 512
norm_eps = 1e-05
X, Y, CORE, Z_NEAR, Z_FAR = ("dp", 2), ("sp", 1), ("dp", 1), ("sp", 2), ("sp", 4)
Z_BOTH = ("sp", 6)
bf16 = jnp.bfloat16
f32 = jnp.float32


def dot(a, b, ca=1, cb=0):
    return lax.dot_general(a, b, (((ca,), (cb,)), ((), ())), preferred_element_type=f32)


def rows(i, size=CHUNK):
    return pl.ds(pl.multiple_of(i * size, size), size)


def over(body, init, count=PIX // CHUNK, unroll=2):
    return lax.fori_loop(0, count, body, init, unroll=unroll)


def split3(v):
    hi = v.astype(bf16)
    rest = v - hi.astype(f32)
    mid = rest.astype(bf16)
    low = (rest - mid.astype(f32)).astype(bf16)
    return hi, mid, low


def same_group():
    lane = lax.broadcasted_iota(jnp.int32, (C, C), 1).astype(f32)
    sub = lax.broadcasted_iota(jnp.int32, (C, C), 0).astype(f32)
    width = GROUPS / C
    return (jnp.floor((lane + 0.5) * width) == jnp.floor((sub + 0.5) * width)).astype(f32).astype(bf16)


def group_means(vectors, ones):
    parts = [p for v in vectors for p in split3(v)]
    count = len(parts)
    stacked = jnp.concatenate(
        [p.astype(f32) for p in parts] + [jnp.zeros((16 - count, C), f32)], axis=0
    ).astype(bf16)
    sums = dot(stacked, ones)
    scale = 1.0 / (PIX * (C // GROUPS))
    return [
        (sums[3 * i : 3 * i + 1] + sums[3 * i + 1 : 3 * i + 2] + sums[3 * i + 2 : 3 * i + 3]) * scale
        for i in range(len(vectors))
    ]


def total(v):
    return jnp.sum(v, axis=0, keepdims=True)


def norm_stats(load, ones):
    zero = jnp.zeros((1, C), f32)
    (mean,) = group_means([over(lambda i, s: s + total(load(i)), zero)], ones)

    def square(i, s):
        centred = load(i) - mean
        return s + total(centred * centred)

    (variance,) = group_means([over(square, zero)], ones)
    return mean, lax.rsqrt(variance + norm_eps)


def put_shifted(dst, i, value, step):
    size = value.shape[0]
    column = lax.broadcasted_iota(jnp.int32, (size, C), 0) & (W - 1)
    at = pl.ds(pl.multiple_of(W + i * size, W), size)
    back = jnp.where(column == 0, 0.0, pltpu.roll(value, 1, 0))
    ahead = jnp.where(column == W - 1, 0.0, pltpu.roll(value, size - 1, 0))
    order = (back, value, ahead) if step == 1 else (ahead, value, back)
    for k in range(3):
        dst[at, k * C : (k + 1) * C] = order[k].astype(bf16)


def zero_edges(dst):
    dst[0:W, :] = jnp.zeros((W, TAPS), bf16)
    dst[W + PIX : ROWS, :] = jnp.zeros((W, TAPS), bf16)


def lay_shifted(mover, dst, src):
    zero_edges(dst)
    mover.ready(src)

    def step(i, carry):
        put_shifted(dst, i, src[rows(i), :].astype(f32), -1)
        return carry

    over(step, 0)


def conv_rows(shifted, weight, i, size):
    acc = None
    for kh in range(3):
        part = dot(
            shifted[pl.ds(pl.multiple_of(i * size + kh * W, W), size), :],
            weight[kh * TAPS : (kh + 1) * TAPS, :],
        )
        acc = part if acc is None else acc + part
    return acc


def conv_back_rows(shifted, weight, i, size):
    acc = None
    for kh in range(3):
        part = dot(
            shifted[pl.ds(pl.multiple_of(i * size + (2 - kh) * W, W), size), :],
            weight[:, kh * TAPS : (kh + 1) * TAPS],
            1,
            1,
        )
        acc = part if acc is None else acc + part
    return acc


def sigmoid(v):
    return 1.0 / (1.0 + jnp.exp(-v))


def silu_grad(v):
    s = sigmoid(v)
    return s * (1.0 + v * (1.0 - s))


def fetch(pieces, places, dst, sems):
    copies = []
    for k, (piece, (row, column)) in enumerate(zip(pieces, places)):
        height, width = piece.shape
        copies.append(
            pltpu.make_async_copy(
                piece, dst.at[pl.ds(row, height), pl.ds(column, width)], sems.at[k]
            )
        )
        copies[-1].start()
    return copies


def settle(copies):
    for copy in copies:
        copy.wait()


def square_sum(ref, mean):
    def square(i, s):
        centred = ref[rows(i), :].astype(f32) - mean
        return s + total(centred * centred)

    return over(square, jnp.zeros((1, C), f32))


def prepare_kernel(mover, conv_ref, gains, biases, conv_b, film_b, qv_b, proj_b, out_ref):
    mover.ready(conv_ref, gains, biases, conv_b, film_b, qv_b, proj_b)
    for tap in range(9):
        out_ref[:, tap * C : (tap + 1) * C] = conv_ref[tap]
    share = out_ref.shape[0]
    stacked = jnp.concatenate(
        [ref[...].astype(f32) for ref in (gains, biases, conv_b, film_b, qv_b, proj_b)]
        + [jnp.zeros((3, share), f32)],
        axis=0,
    ).astype(bf16)
    unit = lax.broadcasted_iota(jnp.int32, (16, PAD), 0) == lax.broadcasted_iota(
        jnp.int32, (16, PAD), 1
    )
    out_ref[:, 9 * C :] = dot(stacked, unit.astype(f32).astype(bf16), 0, 0).astype(bf16)


def first_kernel(places, mover, *refs):
    pieces, refs = refs[: len(places)], refs[len(places) :]
    (
        x_ref, order_ref, first_ref, hidden_ref, w1_ref, stats_ref, shifted, weight, raw, sems,
    ) = refs
    copies = fetch(pieces, places, raw, sems)
    ones = same_group()
    zero_edges(shifted)
    mover.ready(x_ref, order_ref)
    order = order_ref[...]
    load = lambda i: x_ref[rows(i), :].astype(f32)
    mean0, inv0 = norm_stats(load, ones)
    settle(copies)
    par = dot(raw[:, 9 * C :], order, 0, 1)
    row = lambda k: par[k : k + 1, :]
    for tap in range(9):
        part = dot(order, raw[:, tap * C : (tap + 1) * C]).astype(bf16)
        weight[tap * C : (tap + 1) * C, :] = part
        w1_ref[:, tap * C : (tap + 1) * C] = part
    mover.send(w1_ref)
    gain, bias = inv0 * row(0), row(3) - mean0 * inv0 * row(0)

    def start(i, carry):
        pre = load(i) * gain + bias
        act = pre * sigmoid(pre)
        first_ref[rows(i), :] = act.astype(bf16)
        put_shifted(shifted, i, act, 1)
        return carry

    over(start, 0)
    mover.send(first_ref)

    def conv1(i, s):
        value = conv_rows(shifted, weight, i, SIZE) + row(6)
        hidden_ref[rows(i, SIZE), :] = value
        return s + total(value)

    sums = lax.fori_loop(0, PIX // SIZE, conv1, jnp.zeros((1, C), f32))
    mover.send(hidden_ref)
    (mean1,) = group_means([sums], ones)
    (var1,) = group_means([square_sum(hidden_ref, mean1)], ones)
    inv1 = lax.rsqrt(var1 + norm_eps)
    zero = jnp.zeros((1, C), f32)
    stats_ref[...] = jnp.concatenate(
        [mean0, inv0, mean1, inv1, zero, zero, zero, zero] + [par[0:13, :], jnp.zeros((3, C), f32)],
        axis=0,
    )


def second_kernel(places, mover, *refs):
    pieces, refs = refs[: len(places)], refs[len(places) :]
    (
        order_ref, emb_ref, stats_ref, hidden_ref, x_ref,
        second_ref, residual_ref, attn_ref, projected_ref, w2_ref, wqkv_ref, wproj_ref, norm_ref,
        shifted, weight, raw, sems,
    ) = refs
    copies = fetch(pieces, places, raw, sems)
    ones = same_group()
    zero_edges(shifted)
    mover.ready(order_ref, emb_ref, stats_ref)
    order = order_ref[...]
    row = lambda k: stats_ref[8 + k : 9 + k, :]
    settle(copies)
    for tap in range(9):
        part = dot(order, raw[:, tap * C : (tap + 1) * C]).astype(bf16)
        weight[tap * C : (tap + 1) * C, :] = part
        w2_ref[:, tap * C : (tap + 1) * C] = part
    column = 9 * C
    wqkv_ref[...] = dot(order, raw[:, column : column + QKV]).astype(bf16)
    column += QKV
    wproj_ref[...] = dot(order, raw[:, column : column + ATT]).astype(bf16)
    column += ATT
    mover.send(w2_ref, wqkv_ref, wproj_ref)
    emb = dot(emb_ref[...], order).astype(bf16)
    wide = dot(emb, raw[:, column : column + 2 * C])
    column += 2 * C
    narrow = dot(emb, raw[:, column : column + 2 * PAD])
    film = total(wide[0:3]) + jnp.concatenate(
        [total(narrow[3 + 3 * k : 6 + 3 * k]) for k in range(3)], axis=1
    )
    scale = 1.0 + film[:, :C] + row(8)
    shift = film[:, C:] + row(9)
    mean1, inv1 = stats_ref[2:3, :], stats_ref[3:4, :]
    gain = inv1 * row(1) * scale
    bias = (row(4) - mean1 * inv1 * row(1)) * scale + shift
    mover.ready(hidden_ref, x_ref)

    def middle(i, carry):
        scaled = hidden_ref[rows(i), :] * gain + bias
        act = scaled * sigmoid(scaled)
        second_ref[rows(i), :] = act.astype(bf16)
        put_shifted(shifted, i, act, 1)
        return carry

    over(middle, 0)
    mover.send(second_ref)

    def conv2(i, s):
        value = (
            conv_rows(shifted, weight, i, SIZE) + row(7) + x_ref[rows(i, SIZE), :].astype(f32)
        )
        residual_ref[rows(i, SIZE), :] = value
        return s + total(value)

    sums = lax.fori_loop(0, PIX // SIZE, conv2, jnp.zeros((1, C), f32))
    mover.send(residual_ref)
    (mean2,) = group_means([sums], ones)
    (var2,) = group_means([square_sum(residual_ref, mean2)], ones)
    inv2 = lax.rsqrt(var2 + norm_eps)

    lane = lax.broadcasted_iota(jnp.int32, (8, PAD), 1)
    biases = []
    for g in range(HEADS):
        for which in (10, None, 11):
            if which is None:
                biases.append(jnp.zeros((1, PAD), f32))
            else:
                turned = jnp.broadcast_to(row(which), (8, C))
                if g:
                    turned = pltpu.roll(turned, C - g * HD, 1)
                biases.append(jnp.where(lane < HD, turned[:, :PAD], 0.0)[0:1])
    bias = jnp.concatenate(biases, axis=1)

    gain2, bias2 = inv2 * row(2), row(5) - mean2 * inv2 * row(2)

    def last(i, carry):
        attn = (residual_ref[rows(i, SIZE), :] * gain2 + bias2).astype(bf16)
        attn_ref[rows(i, SIZE), :] = attn
        projected_ref[rows(i, SIZE), :] = (dot(attn, wqkv_ref[...]) + bias).astype(bf16)
        return carry

    lax.fori_loop(0, PIX // SIZE, last, 0)
    norm_ref[...] = jnp.concatenate([mean2, inv2, scale, shift, jnp.zeros((4, C), f32)], axis=0)


def attention_kernel(
    loss_ref, order_any, residual_any, grad_ref, wproj_ref, stats_ref, qkv_ref,
    out_ref, gqkv_ref, wproj_grad_ref, sums_ref,
    branch, attended, keys_grad, values_grad, order_ref, residual_ref, sems,
):
    g = pl.program_id(0)
    factor = 1.0 / math.sqrt(HD)
    size = PIX
    loads = [
        pltpu.make_async_copy(residual_any, residual_ref, sems.at[0]),
        pltpu.make_async_copy(order_any, order_ref, sems.at[1]),
    ]

    @pl.when(g == 0)
    def _():
        for load in loads:
            load.start()

        def scaled(i, s):
            value = (grad_ref[rows(i), :].astype(f32) * loss_ref[0, 0]).astype(bf16)
            branch[rows(i), :] = value
            return s + total(value.astype(f32))

        sums_ref[...] = jnp.broadcast_to(over(scaled, jnp.zeros((1, C), f32)), (8, C))

    lanes = pl.ds(pl.multiple_of(g * PAD, PAD), PAD)
    keys_grad[...] = jnp.zeros_like(keys_grad)
    values_grad[...] = jnp.zeros_like(values_grad)

    def chunk(i, carry):
        queries = qkv_ref[rows(i, size), 0:PAD]
        keys = qkv_ref[:, PAD : 2 * PAD]
        values = qkv_ref[:, 2 * PAD : 3 * PAD]
        grad = dot(branch[rows(i, size), :], wproj_ref[:, lanes]).astype(bf16).astype(f32)
        scores = dot(queries, keys, 1, 1)
        top = jnp.max(scores, axis=1, keepdims=True)
        power = jnp.exp2((scores - top) * (factor * math.log2(math.e)))
        scale = 1.0 / jnp.sum(power, axis=1, keepdims=True)
        soft = power.astype(bf16)
        result = dot(soft, values) * scale
        attended[rows(i, size), lanes] = result.astype(bf16)
        inner = jnp.sum(grad * result, axis=1, keepdims=True) * scale
        grad = (grad * scale).astype(bf16)
        grad_scores = (power * (dot(grad, values, 1, 1) - inner)).astype(bf16)
        gqkv_ref[rows(i, size), 0:PAD] = (dot(grad_scores, keys) * factor).astype(bf16)
        keys_grad[...] += dot(queries, grad_scores, 0, 0)
        values_grad[...] += dot(grad, soft, 0, 0)
        return carry

    lax.fori_loop(0, PIX // size, chunk, 0)
    gqkv_ref[:, PAD : 2 * PAD] = (keys_grad[...].T * factor).astype(bf16)
    gqkv_ref[:, 2 * PAD : 3 * PAD] = values_grad[...].T.astype(bf16)

    @pl.when(g == HEADS - 1)
    def _():
        for load in loads:
            load.wait()

        def project(i, carry):
            value = residual_ref[rows(i, size), :] + dot(attended[rows(i, size), :], wproj_ref[...], 1, 1)
            out_ref[rows(i, size), :] = (value + stats_ref[20:21, :]).astype(bf16)
            return carry

        lax.fori_loop(0, PIX // size, project, 0)
        turned = dot(order_ref[...], branch[...], 0, 1).astype(bf16)
        wproj_grad_ref[...] = dot(turned, attended[...]).astype(bf16)


def put_halves(mover, own, others, column, value):
    at = slice(column, column + value.shape[1])
    block = C // 8
    for k, other in enumerate(others):
        other[:, at] = value[C // 2 + k * block : C // 2 + (k + 1) * block].astype(bf16)
        mover.send_columns(other, column, value.shape[1])
    own[:, at] = value[: C // 2].astype(bf16)
    mover.send_columns(own, column, value.shape[1])


def weight_grad(mover, own, others, order, act, shifted):
    turned = dot(order, act[...], 0, 1).astype(bf16)
    for kh in range(3):
        part = dot(turned, shifted[(2 - kh) * W : (2 - kh) * W + PIX, :])
        put_halves(mover, own, others, kh * TAPS, part)


def middle_kernel(
    mover, loss_ref, gqkv_ref, wqkv_ref, norm_ref, stats_ref, residual_ref, order_ref, attn_ref, grad_ref,
    second_ref, wproj_grad_ref, *refs,
):
    own_ref, *other_refs, grad_residual_ref, g2_ref, sums_ref, shifted, work = refs
    ones = same_group()
    zero_edges(shifted)
    size = SIZE
    mover.ready(gqkv_ref, wqkv_ref, norm_ref, stats_ref, residual_ref)
    mean, inv, gain = norm_ref[0:1, :], norm_ref[1:2, :], stats_ref[10:11, :]
    zero = jnp.zeros((1, C), f32)

    def step(i, carry):
        q_sum, u_sum, p_sum = carry
        packed = gqkv_ref[rows(i, size), :]
        q = dot(packed, wqkv_ref[...], 1, 1)
        work[rows(i, size), :] = q
        u = (residual_ref[rows(i, size), :] - mean) * inv
        return q_sum + total(q), u_sum + total(q * u), p_sum + total(packed.astype(f32))

    q_sum, u_sum, p_sum = lax.fori_loop(0, PIX // size, step, (zero, zero, jnp.zeros((1, QKV), f32)))
    first, second = group_means([q_sum * gain, u_sum * gain], ones)
    mover.ready(order_ref, attn_ref, grad_ref, second_ref, wproj_grad_ref)
    order = order_ref[...]
    turned = dot(order, attn_ref[...], 0, 1).astype(bf16)
    put_halves(mover, own_ref, other_refs, 9 * C, dot(turned, gqkv_ref[...]))
    put_halves(mover, own_ref, other_refs, 9 * C + QKV, wproj_grad_ref[...])

    def apply(i, s):
        u = (residual_ref[rows(i), :] - mean) * inv
        value = grad_ref[rows(i), :].astype(f32) * loss_ref[0, 0] + inv * (
            work[rows(i), :] * gain - first - u * second
        )
        grad_residual_ref[rows(i), :] = value
        rounded = value.astype(bf16)
        g2_ref[rows(i), :] = rounded
        rounded = rounded.astype(f32)
        put_shifted(shifted, i, rounded, -1)
        return s + total(rounded)

    conv_sum = over(apply, zero)
    mover.send(g2_ref, grad_residual_ref)
    weight_grad(mover, own_ref, other_refs, order, second_ref, shifted)

    def heads(k):
        value = jnp.zeros((8, C), f32)
        for g in range(HEADS):
            at = (3 * g + k) * PAD
            block = jnp.concatenate(
                [jnp.broadcast_to(p_sum[:, at : at + PAD], (8, PAD)), jnp.zeros((8, C - PAD), f32)], axis=1
            )
            value = value + (pltpu.roll(block, g * HD, 1) if g else block)
        return value[0:1]

    sums_ref[...] = jnp.concatenate(
        [u_sum, q_sum, conv_sum, heads(0), heads(2), jnp.zeros((3, C), f32)], axis=0
    )


def hidden_kernel(
    mover, g2_ref, w2_ref, hidden_ref, stats_ref, norm_ref, order_ref, emb_ref,
    g1_ref, sums_ref, own_ref, *refs,
):
    *other_refs, shifted, work = refs
    ones = same_group()
    size = SIZE
    lay_shifted(mover, shifted, g2_ref)
    mover.ready(w2_ref, hidden_ref, stats_ref, norm_ref)
    stat = lambda k: stats_ref[k : k + 1, :]
    mean, inv, gain, bias = stat(2), stat(3), stat(9), stat(12)
    scale, shift = norm_ref[2:3, :], norm_ref[3:4, :]
    zero = jnp.zeros((1, C), f32)

    def step(i, carry):
        u_sum, s_sum = carry
        u = (hidden_ref[rows(i, size), :] - mean) * inv
        scaled = (u * gain + bias) * scale + shift
        value = conv_back_rows(shifted, w2_ref, i, size) * silu_grad(scaled)
        work[rows(i, size), :] = value
        return u_sum + total(value * u), s_sum + total(value)

    u_sum, s_sum = lax.fori_loop(0, PIX // size, step, (zero, zero))
    film0 = u_sum * gain + s_sum * bias
    u_up, s_up = u_sum * scale, s_sum * scale
    first, second = group_means([s_up * gain, u_up * gain], ones)
    factor = scale * gain

    def apply(i, s):
        u = (hidden_ref[rows(i), :] - mean) * inv
        value = (inv * (work[rows(i), :] * factor - first - u * second)).astype(bf16)
        g1_ref[rows(i), :] = value
        return s + total(value.astype(f32))

    conv_sum = over(apply, zero)
    mover.send(g1_ref)
    sums_ref[...] = jnp.concatenate(
        [u_up, s_up, conv_sum, film0, s_sum, jnp.zeros((3, C), f32)], axis=0
    )
    mover.ready(order_ref, emb_ref)
    emb = sum(dot(order_ref[...], part, 0, 1) for part in split3(emb_ref[...]))
    film = jnp.concatenate([film0, s_sum], axis=1)
    put_halves(mover, own_ref, other_refs, 0, emb[:, 0:1] * film)
    narrow = sum(
        emb[:, k + 1 : k + 2] * film[:, k * 2 * PAD : (k + 1) * 2 * PAD] for k in range(3)
    )
    put_halves(mover, own_ref, other_refs, 2 * C, narrow)


def late_kernel(
    mover, g1_ref, first_ref, order_ref, proj_ref, sums2_ref, sums1_ref, sums0_ref, own_ref, *refs
):
    *other_refs, shifted = refs
    lay_shifted(mover, shifted, g1_ref)
    mover.ready(first_ref, order_ref, proj_ref, sums2_ref, sums1_ref, sums0_ref)
    order = order_ref[...]
    weight_grad(mover, own_ref, other_refs, order, first_ref, shifted)
    stacked = jnp.concatenate(
        [
            sums0_ref[0:1, :], sums1_ref[0:1, :], sums2_ref[0:1, :],
            sums0_ref[1:2, :], sums1_ref[1:2, :], sums2_ref[1:2, :],
            sums1_ref[2:3, :], sums2_ref[2:3, :], sums1_ref[3:5, :], sums2_ref[3:5, :], proj_ref[0:1, :],
            jnp.zeros((PAD - 13, C), f32),
        ],
        axis=0,
    )
    put_halves(mover, own_ref, other_refs, 9 * C, dot(order, stacked.astype(bf16), 0, 1))


def image_kernel(
    mover, g1_ref, w1_ref, stats_ref, x_ref, grad_residual_ref, out_ref, sums_ref, shifted, work
):
    ones = same_group()
    lay_shifted(mover, shifted, g1_ref)
    size = SIZE
    mover.ready(w1_ref, stats_ref, x_ref)
    stat = lambda k: stats_ref[k : k + 1, :]
    mean, inv, gain, bias = stat(0), stat(1), stat(8), stat(11)
    zero = jnp.zeros((1, C), f32)

    def step(i, carry):
        u_sum, s_sum = carry
        u = (x_ref[rows(i, size), :].astype(f32) - mean) * inv
        value = conv_back_rows(shifted, w1_ref, i, size) * silu_grad(u * gain + bias)
        work[rows(i, size), :] = value
        return u_sum + total(value * u), s_sum + total(value)

    u_sum, s_sum = lax.fori_loop(0, PIX // size, step, (zero, zero))
    first, second = group_means([s_sum * gain, u_sum * gain], ones)
    mover.ready(grad_residual_ref)

    def apply(i, carry):
        u = (x_ref[rows(i), :].astype(f32) - mean) * inv
        value = inv * (work[rows(i), :] * gain - first - u * second)
        out_ref[rows(i), :] = (grad_residual_ref[rows(i), :] + value).astype(bf16)
        return carry

    over(apply, 0)
    sums_ref[...] = jnp.concatenate([u_sum, s_sum, jnp.zeros((6, C), f32)], axis=0)


SMEM = pl.BlockSpec(memory_space=pltpu.SMEM)
ANY = pl.BlockSpec(memory_space=pl.ANY)
VMEM_LIMIT = 60 * 2**20
FIRST = 9 * C + PAD
SECOND = 9 * C + QKV + ATT + 2 * C + 2 * PAD
EARLY = 9 * C + QKV + ATT
FILM = 2 * C + 2 * PAD
LATE = 9 * C + PAD


def shape(*dims, dtype=bf16):
    return jax.ShapeDtypeStruct(dims, dtype)


def quarters(width):
    return [shape(C // 8, width)] * 4


def cost(us):
    return pl.CostEstimate(
        flops=int(us * 1_000_000_000), bytes_accessed=int(us * 3_600_000), transcendentals=0
    )


class Mover:
    def __init__(self, sources, inputs, outputs, targets, in_sems, out_sems):
        self.loads = {}
        for k, (source, buffer) in enumerate(zip(sources, inputs)):
            self.loads[id(buffer)] = pltpu.make_async_copy(source, buffer, in_sems.at[k])
            self.loads[id(buffer)].start()
        self.outputs = list(outputs)
        self.targets = {id(buffer): target for buffer, target in zip(outputs, targets)}
        self.sems = out_sems
        self.sent = []

    def ready(self, *buffers):
        for buffer in buffers:
            self.loads.pop(id(buffer)).wait()

    def store(self, source, target):
        copy = pltpu.make_async_copy(source, target, self.sems.at[len(self.sent)])
        copy.start()
        self.sent.append(copy)

    def send(self, *buffers):
        for buffer in buffers:
            self.outputs = [b for b in self.outputs if b is not buffer]
            self.store(buffer, self.targets[id(buffer)])

    def send_columns(self, buffer, start, width):
        self.outputs = [b for b in self.outputs if b is not buffer]
        at = (slice(None), pl.ds(start, width))
        self.store(buffer.at[at], self.targets[id(buffer)].at[at])

    def close(self):
        for load in self.loads.values():
            load.wait()
        self.send(*self.outputs)
        for copy in self.sent:
            copy.wait()


def call(kernel, operands, outs, scratch, us, name, scalars=0, pieces=0):
    count = len(operands) - scalars - pieces

    def body(*refs):
        fixed, refs = refs[: scalars + pieces], refs[scalars + pieces :]
        sources, refs = refs[:count], refs[count:]
        targets, refs = refs[: len(outs)], refs[len(outs) :]
        inputs, refs = refs[:count], refs[count:]
        outputs, refs = refs[: len(outs)], refs[len(outs) :]
        mover = Mover(sources, inputs, outputs, targets, refs[-2], refs[-1])
        kernel(mover, *fixed, *inputs, *outputs, *refs[:-2])
        mover.close()

    buffers = [pltpu.VMEM(v.shape, v.dtype) for v in [*operands[scalars + pieces :], *outs]]
    return pl.pallas_call(
        body,
        out_shape=outs,
        in_specs=[SMEM] * scalars + [ANY] * (pieces + count),
        out_specs=[ANY] * len(outs),
        scratch_shapes=buffers
        + scratch
        + [pltpu.SemaphoreType.DMA((max(count, 1),)), pltpu.SemaphoreType.DMA((len(outs) + 30,))],
        compiler_params=pltpu.CompilerParams(vmem_limit_bytes=VMEM_LIMIT),
        cost_estimate=cost(us),
        name=name,
    )(*operands)


def prepare(conv, *small):
    share = conv.shape[2]
    return call(
        prepare_kernel, [conv.reshape(9, share, C), *small], [shape(share, FIRST)], [], 1, "prepare"
    )[0]


def weight_scratch(pieces, width):
    return [
        pltpu.VMEM((ROWS, TAPS), bf16), pltpu.VMEM((9 * C, C), bf16), pltpu.VMEM((C, width), bf16),
        pltpu.SemaphoreType.DMA((len(pieces),)),
    ]


def forward_first(places, pieces, order, x):
    return call(
        functools.partial(first_kernel, places),
        [*pieces, x, order],
        [shape(PIX, C), shape(PIX, C, dtype=f32), shape(C, 9 * C), shape(24, C, dtype=f32)],
        weight_scratch(pieces, FIRST), 13, "forward_first", 0, len(pieces),
    )


def forward_second(places, pieces, order, x, hidden, stats, emb):
    return call(
        functools.partial(second_kernel, places),
        [*pieces, order, emb, stats, hidden, x],
        [
            shape(PIX, C), shape(PIX, C, dtype=f32), shape(PIX, C), shape(PIX, QKV), shape(C, 9 * C),
            shape(C, QKV), shape(C, ATT), shape(8, C, dtype=f32),
        ],
        weight_scratch(pieces, SECOND), 10, "forward_second", 0, len(pieces),
    )


def attend(loss, order, grad, wproj, residual, stats, projected):
    whole = lambda *dims: pl.BlockSpec(dims, lambda g: (0, 0))
    head = pl.BlockSpec((PIX, 3 * PAD), lambda g: (0, g))
    return pl.pallas_call(
        attention_kernel,
        grid=(HEADS,),
        out_shape=[shape(PIX, C), shape(PIX, QKV), shape(C, ATT), shape(8, C, dtype=f32)],
        in_specs=[SMEM, ANY, ANY, whole(PIX, C), whole(C, ATT), whole(24, C), head],
        out_specs=[whole(PIX, C), head, whole(C, ATT), whole(8, C)],
        scratch_shapes=[
            pltpu.VMEM((PIX, C), bf16), pltpu.VMEM((PIX, ATT), bf16),
            pltpu.VMEM((PAD, PIX), f32), pltpu.VMEM((PAD, PIX), f32),
            pltpu.VMEM((C, C), bf16), pltpu.VMEM((PIX, C), f32), pltpu.SemaphoreType.DMA((2,)),
        ],
        compiler_params=pltpu.CompilerParams(vmem_limit_bytes=VMEM_LIMIT),
        cost_estimate=cost(31),
        name="attention",
    )(loss, order, residual, grad, wproj, stats, projected)


def backward_middle(loss, order, grad, attn, gqkv, wqkv, residual, stats, norm, second, wproj_grad):
    own, *others, grad_residual, g2, sums = call(
        middle_kernel,
        [loss, gqkv, wqkv, norm, stats, residual, order, attn, grad, second, wproj_grad],
        [
            shape(C // 2, EARLY), *quarters(EARLY), shape(PIX, C, dtype=f32), shape(PIX, C),
            shape(8, C, dtype=f32),
        ],
        [pltpu.VMEM((ROWS, TAPS), bf16), pltpu.VMEM((PIX, C), f32)], 16, "backward_middle", 1,
    )
    return own, others, grad_residual, g2, sums


def backward_hidden(order, emb, g2, w2, hidden, stats, norm):
    g1, sums, own, *others = call(
        hidden_kernel,
        [g2, w2, hidden, stats, norm, order, emb],
        [shape(PIX, C), shape(8, C, dtype=f32), shape(C // 2, FILM), *quarters(FILM)],
        [pltpu.VMEM((ROWS, TAPS), bf16), pltpu.VMEM((PIX, C), f32)], 10, "backward_hidden",
    )
    return g1, sums, own, others


def backward_late(order, g1, first, proj_sums, sums2, sums1, sums0):
    own, *others = call(
        late_kernel,
        [g1, first, order, proj_sums, sums2, sums1, sums0],
        [shape(C // 2, LATE), *quarters(LATE)],
        [pltpu.VMEM((ROWS, TAPS), bf16)], 7, "backward_late",
    )
    return own, others


def backward_image(g1, w1, x, stats, grad_residual):
    return call(
        image_kernel,
        [g1, w1, stats, x, grad_residual],
        [shape(PIX, C), shape(8, C, dtype=f32)],
        [pltpu.VMEM((ROWS, TAPS), bf16), pltpu.VMEM((PIX, C), f32)], 10, "backward_image",
    )


def finish_kernel(mover, *refs):
    parts, (conv_ref, *outs) = refs[:4], refs[4:]
    mover.ready(*parts)
    value = sum(part[...].astype(f32) for part in parts)
    for tap in range(9):
        conv_ref[tap] = value[:, tap * C : (tap + 1) * C]
    share = value.shape[0]
    small = jnp.concatenate([value[:, 9 * C :], jnp.zeros((PAD - share, PAD), f32)], axis=0).T
    row = 0
    for out in outs:
        out[...] = small[row : row + out.shape[0], :share]
        row += out.shape[0]


def finish(parts):
    share = parts[0].shape[0]
    return call(
        finish_kernel,
        parts,
        [shape(9, share, C, dtype=f32)] + [shape(n, share, dtype=f32) for n in (3, 3, 2, 2, 2, 1)],
        [], 1, "finish",
    )


def halves(width):
    return width // 2 // PAD * PAD


def core_kernel(groups, mover, *refs):
    owns, gots = refs[:groups], refs[groups:-4]
    stays, goes = refs[-4:-2], refs[-2:]
    mover.ready(*owns, *gots)
    block, cut = stays[0].shape[0] // 2, stays[0].shape[1]
    column = 0
    for group, own in enumerate(owns):
        width = own.shape[1]
        split = min(max(cut - column, 0), width)
        for k in range(4):
            got = gots[4 * group + k][...].astype(f32)
            value = (own[k * block : (k + 1) * block, :].astype(f32) + got).astype(bf16)
            x, y = k // 2, k % 2
            if split > 0:
                at = slice(y * block, (y + 1) * block)
                (goes if x else stays)[0][at, column : column + split] = value[:, :split]
            if split < width:
                at = slice(x * block, (x + 1) * block)
                start = column + split - cut
                (goes if y else stays)[1][at, start : start + width - split] = value[:, split:]
        column += width


def reduce_core(owns, gots):
    block = owns[0].shape[0] // 4
    width = sum(own.shape[1] for own in owns)
    cut = halves(width)
    parts = [shape(2 * block, cut), shape(2 * block, width - cut)]
    outs = call(
        functools.partial(core_kernel, len(owns)),
        [*owns, *gots], parts * 2, [], 3, "reduce_core",
    )
    return outs[:2], outs[2:]


def cross_kernel(mover, *refs):
    stays, gots, own_ref, goes = refs[:2], refs[2:4], refs[4], refs[5:]
    mover.ready(*stays, *gots)
    block, cut = goes[0].shape
    for k, columns in enumerate((slice(0, cut), slice(cut, own_ref.shape[1]))):
        value = (stays[k][...].astype(f32) + gots[k][...].astype(f32)).astype(bf16)
        own_ref[:, columns] = value[:block]
        goes[k][...] = value[block:]


def reduce_cross(stays, gots):
    block = stays[0].shape[0] // 2
    left, right = (stay.shape[1] for stay in stays)
    own, *goes = call(
        cross_kernel,
        [*stays, *gots],
        [shape(block, left + right), shape(block, left), shape(block, right)],
        [], 2, "reduce_cross",
    )
    return own, goes


def column_kernel(mover, own_ref, left_ref, right_ref, *outs):
    mover.ready(own_ref, left_ref, right_ref)
    got = jnp.concatenate([left_ref[...].astype(f32), right_ref[...].astype(f32)], axis=1)
    value = own_ref[...].astype(f32) + got
    share = outs[0].shape[0]
    for k, out in enumerate(outs):
        out[...] = value[k * share : (k + 1) * share].astype(bf16)


def reduce_plane(own, gots):
    block, width = own.shape
    return call(
        column_kernel, [own, *gots], [shape(block // 4, width)] * 4, [], 1, "reduce_plane"
    )


both = ("dp", "sp")


def swap(value, axis, bit):
    count = lax.axis_size(axis)
    return lax.ppermute(value, axis, [(i, i ^ bit) for i in range(count)])


def after(value, *others):
    return lax.optimization_barrier((value, *others))[0]


def gather_column(shard):
    block = jnp.concatenate([shard, swap(shard, *Z_FAR)])
    return jnp.concatenate([block, swap(block, *Z_NEAR)])


def gather_plane(block):
    return swap(block, *X), swap(block, *Y)


def gather_corner(from_x, from_y):
    cut = halves(from_x.shape[1])
    return swap(from_y[:, :cut], *X), swap(from_x[:, cut:], *Y)


def gather_rest(block, from_x, from_y, left, right):
    mine = [block, from_y, from_x, left, right]
    return mine + [swap(piece, *CORE) for piece in mine]


def swap_plane(goes, first, second):
    return [swap(goes[0], *first), swap(goes[1], *second)]


def swap_column(shards):
    own, far, near, both_ways = shards
    return [own, swap(far, *Z_FAR), swap(near, *Z_NEAR), swap(both_ways, *Z_BOTH)]


def piece_places(width):
    cut = halves(width)
    places = [(0, 0), (48, 0), (96, 0), (144, 0), (144, cut)]
    return places + [(row + C // 2, column) for row, column in places]


def row_order(tree):
    row = jnp.arange(C)
    if tree:
        share = C // 32
        k = row // share
        dp = lax.axis_index("dp") ^ (k >> 4) ^ ((k >> 3 & 1) * 2)
        sp = lax.axis_index("sp") ^ (k >> 2 & 1) ^ ((k >> 1 & 1) * 2) ^ ((k & 1) * 4)
        row = (dp * 8 + sp) * share + row % share
    return (jnp.arange(C)[:, None] == row[None, :]).astype(bf16)


def time_embedding(steps):
    half_width = E // 2
    frequencies = jnp.exp(
        -math.log(10000.0) * jnp.arange(half_width, dtype=jnp.float32) / half_width
    )
    angles = steps.astype(jnp.float32)[:, None] * frequencies[None, :]
    return jnp.concatenate([jnp.cos(angles), jnp.sin(angles)], axis=1)


def padded_heads(value, axis):
    pads = [(0, 0)] * value.ndim
    pads[axis] = (0, PAD - HD)
    return jnp.pad(value, pads)


def embedding_rows(embedding, devices):
    share = C // devices
    by_device = embedding.reshape(devices, E // devices)
    wide = by_device[:, :share].reshape(C)
    narrow = jnp.repeat(by_device[:, share:], 3, axis=1).reshape(C)
    third = jnp.arange(C) % 3
    return jnp.stack([wide] + [jnp.where(third == k, narrow, 0.0) for k in range(3)])


def body(
    images,
    timesteps,
    loss_weight,
    out_grad,
    norm_gains,
    norm_biases,
    conv_biases,
    film_weight,
    film_bias,
    conv1_weight,
    conv2_weight,
    qkv_weight,
    qv_bias,
    proj_weight,
    proj_bias,
):
    row_parts = lax.axis_size("sp")
    devices = lax.axis_size("dp") * row_parts
    samples = images.shape[0] * images.shape[1]
    rows_here = images.shape[2]
    per = max(1, samples // row_parts)
    copies = max(1, row_parts // samples)
    share = C // devices
    embed_share = E // devices
    place = lax.axis_index("sp")
    tree = lax.axis_size("dp") == 4 and row_parts == 8

    def to_samples(value):
        value = value.reshape(samples // per, per * rows_here * W, C)
        if copies > 1:
            value = jnp.repeat(value, copies, axis=0)
        value = lax.all_to_all(value, "sp", split_axis=0, concat_axis=0, tiled=True)
        value = value.reshape(row_parts, per, rows_here * W, C).transpose(1, 0, 2, 3)
        return value.reshape(per, PIX, C)

    def to_rows(value):
        value = value.reshape(per, row_parts, rows_here * W, C).transpose(1, 0, 2, 3)
        value = value.reshape(row_parts, per * rows_here * W, C)
        value = lax.all_to_all(value, "sp", split_axis=0, concat_axis=0, tiled=True)
        return value[::copies].reshape(images.shape)

    first = (place // copies) * per
    steps = lax.dynamic_slice_in_dim(timesteps.reshape(samples), first, per)
    loss = lax.dynamic_slice_in_dim(loss_weight.reshape(samples), first, per)

    first_shard = prepare(
        conv1_weight, norm_gains, norm_biases, conv_biases, film_bias, qv_bias, proj_bias[None]
    )
    by_input = lambda w: w.transpose(2, 0, 1, 3).reshape(share, 9 * C)
    film = film_weight.reshape(embed_share, 2 * C)
    second_shard = jnp.concatenate(
        [
            by_input(conv2_weight),
            padded_heads(qkv_weight, 3).reshape(share, QKV),
            padded_heads(proj_weight.transpose(2, 0, 1), 2).reshape(share, ATT),
            film[:share],
            film[share:].reshape(share, 2 * PAD),
        ],
        axis=1,
    )
    order = row_order(tree)
    staged = tree and per == 1
    if tree:
        places = piece_places
        block = gather_column(first_shard)
        from_x, from_y = gather_plane(block)
        second_block = gather_column(after(second_shard, block))
        images_in = to_samples(images)
        left, right = gather_corner(from_x, from_y)
        first_pieces = gather_rest(block, from_x, from_y, left, right)
        from_x, from_y = gather_plane(after(second_block, left, right, images_in))
        if not staged:
            second_pieces = gather_rest(
                second_block, from_x, from_y, *gather_corner(from_x, from_y)
            )
    else:
        places = lambda width: [(0, 0)]
        gather = lambda shard: [lax.all_gather(shard, both, axis=0, tiled=True)]
        first_pieces, second_pieces = gather(first_shard), gather(second_shard)
        images_in = to_samples(images)
    if not staged:
        grads_in = to_samples(out_grad)

    outs, image_grads, totals = [], [], None
    for index in range(per):
        embedding = embedding_rows(
            jax.nn.silu(time_embedding(steps[index][None]))[0], devices
        )
        emb = jnp.pad(jnp.stack(split3(embedding), axis=1).reshape(12, C), ((0, 4), (0, 0)))
        embedding = jnp.pad(embedding, ((0, 4), (0, 0)))
        weight = loss[index].reshape(1, 1)
        x = images_in[index]
        if staged:
            x = after(x, second_block)
        first, hidden, w1, stats = forward_first(places(FIRST), first_pieces, order, x)
        if staged:
            from_x, from_y = after(from_x, hidden), after(from_y, hidden)
            left, right = gather_corner(from_x, from_y)
            grads_in = to_samples(after(out_grad, from_x, from_y))
            second_pieces = gather_rest(second_block, from_x, from_y, left, right)
        grad = grads_in[index]
        second, residual, attn, projected, w2, wqkv, wproj, norm = forward_second(
            places(SECOND), second_pieces, order, x, hidden, stats, emb
        )
        block_out, gqkv, wproj_grad, proj_sums = attend(
            weight, order, grad, wproj, residual, stats, projected
        )
        own, others, grad_residual, g2, sums2 = backward_middle(
            weight, order, grad, attn, gqkv, wqkv, residual, stats, norm, second, wproj_grad
        )
        if staged:
            out_rows = to_rows(block_out[None])
            gots = [swap(other, *CORE) for other in others]
        g1, sums1, film_own, film_others = backward_hidden(
            order, embedding, g2, w2, hidden, stats, norm
        )
        if staged:
            gots = [after(got, g1) for got in gots] + [swap(other, *CORE) for other in film_others]
            stays, goes = reduce_core([own, film_own], gots)
            g1 = after(g1, *goes, out_rows)
            gots = swap_plane(goes, X, Y)
        image_grad, sums0 = backward_image(g1, w1, x, stats, grad_residual)
        if staged:
            g1 = after(g1, image_grad)
        late_own, late_others = backward_late(order, g1, first, proj_sums, sums2, sums1, sums0)
        if staged:
            late_gots = [swap(other, *CORE) for other in late_others]
            image_rows = to_rows(image_grad[None])
        else:
            outs.append(block_out)
            image_grads.append(image_grad)
            grads = [
                jnp.concatenate(
                    [jnp.concatenate([own, *others]), jnp.concatenate([film_own, *film_others])], axis=1
                ),
                jnp.concatenate([late_own, *late_others]),
            ]
            grads = [g.astype(f32) for g in grads]
            totals = grads if totals is None else [a + b for a, b in zip(totals, grads)]
    if staged:
        own, goes = reduce_cross(stays, [after(got, late_own) for got in gots])
        gots = swap_plane(goes, Y, X)
        late_gots = [after(got, *goes) for got in late_gots]
        stays, goes = reduce_core([late_own], late_gots)
        late_gots = swap_plane(goes, X, Y)
        early = reduce_plane(own, [after(got, *goes) for got in gots])
        *late_gots, image_rows = lax.optimization_barrier((*late_gots, image_rows))
        late_own, goes = reduce_cross(stays, [after(got, *early) for got in late_gots])
        early = swap_column(early)
        late_gots = swap_plane(goes, Y, X)
        late = list(reduce_plane(late_own, late_gots))
        early[1:] = [after(part, *late) for part in early[1:]]
        late = swap_column(late)
        early = sum(part.astype(f32) for part in early)
        late[1:] = [after(part, early) for part in late[1:]]
    else:
        image_rows, out_rows = to_rows(jnp.stack(image_grads)), to_rows(jnp.stack(outs))
        if copies > 1:
            totals = [jnp.where(place % copies == 0, t, 0.0) for t in totals]
        if tree:
            totals = [jnp.dot(order, t.astype(bf16), preferred_element_type=f32) for t in totals]
        early, late = (
            lax.psum_scatter(
                t.astype(bf16).reshape(devices, share, -1), both, scatter_dimension=0
            ).astype(f32)
            for t in totals
        )
    if not staged:
        late = [late] + [jnp.zeros_like(late)] * 3
    conv1_grad, gains_grad, biases_grad, conv_b_grad, film_b_grad, qv_grad, proj_b_grad = finish(late)
    conv2_grad = early[:, : 9 * C].reshape(share, 3, 3, C).transpose(1, 2, 0, 3)
    wqkv_grad = early[:, 9 * C : 9 * C + QKV].reshape(share, HEADS, 3, PAD)[..., :HD]
    wproj_grad = early[:, 9 * C + QKV : EARLY].reshape(share, HEADS, PAD)[..., :HD]
    film_grad = jnp.concatenate(
        [early[:, EARLY : EARLY + 2 * C], early[:, EARLY + 2 * C :].reshape(-1, 2 * C)]
    )
    return (
        out_rows,
        image_rows,
        gains_grad,
        biases_grad,
        conv_b_grad,
        film_grad.reshape(embed_share, 2, C),
        film_b_grad,
        conv1_grad.reshape(3, 3, share, C),
        conv2_grad,
        wqkv_grad,
        qv_grad,
        wproj_grad.transpose(1, 2, 0),
        proj_b_grad[0],
    )


def solution(mesh):
    return jax.shard_map(
        body,
        mesh=mesh,
        in_specs=(
            P(None, "dp", "sp", None, None),
            P(None, "dp"),
            P(None, "dp"),
            P(None, "dp", "sp", None, None),
            P(None, both),
            P(None, both),
            P(None, both),
            P(both, None, None),
            P(None, both),
            P(None, None, both, None),
            P(None, None, both, None),
            P(both, None, None, None),
            P(None, both),
            P(None, None, both),
            P(both),
        ),
        out_specs=(
            P(None, "dp", "sp", None, None),
            P(None, "dp", "sp", None, None),
            P(None, both),
            P(None, both),
            P(None, both),
            P(both, None, None),
            P(None, both),
            P(None, None, both, None),
            P(None, None, both, None),
            P(both, None, None, None),
            P(None, both),
            P(None, None, both),
            P(both),
        ),
        check_vma=False,
    )
```

```python
import functools
import functools
import math

import jax
import jax.numpy as jnp
from jax import lax
from jax.experimental import pallas as pl
from jax.experimental.pallas import tpu as pltpu
from jax.sharding import PartitionSpec as P

C = 384
E = 512
HEADS = 4
HD = 96
PAD = 128
GROUPS = 32
H = 32
W = 32
PIX = H * W
TAPS = 3 * C
QKV = HEADS * 3 * PAD
ATT = HEADS * PAD
ROWS = PIX + 2 * W
CHUNK = 128
SIZE = 512
norm_eps = 1e-05
X, Y, CORE, Z_NEAR, Z_FAR = ("dp", 2), ("sp", 1), ("dp", 1), ("sp", 2), ("sp", 4)
Z_BOTH = ("sp", 6)
bf16 = jnp.bfloat16
f32 = jnp.float32


def dot(a, b, ca=1, cb=0):
    return lax.dot_general(a, b, (((ca,), (cb,)), ((), ())), preferred_element_type=f32)


def rows(i, size=CHUNK):
    return pl.ds(pl.multiple_of(i * size, size), size)


def over(body, init, count=PIX // CHUNK, unroll=2):
    return lax.fori_loop(0, count, body, init, unroll=unroll)


def split3(v):
    hi = v.astype(bf16)
    rest = v - hi.astype(f32)
    mid = rest.astype(bf16)
    low = (rest - mid.astype(f32)).astype(bf16)
    return hi, mid, low


def same_group():
    lane = lax.broadcasted_iota(jnp.int32, (C, C), 1).astype(f32)
    sub = lax.broadcasted_iota(jnp.int32, (C, C), 0).astype(f32)
    width = GROUPS / C
    return (jnp.floor((lane + 0.5) * width) == jnp.floor((sub + 0.5) * width)).astype(f32).astype(bf16)


def group_means(vectors, ones):
    parts = [p for v in vectors for p in split3(v)]
    count = len(parts)
    stacked = jnp.concatenate(
        [p.astype(f32) for p in parts] + [jnp.zeros((16 - count, C), f32)], axis=0
    ).astype(bf16)
    sums = dot(stacked, ones)
    scale = 1.0 / (PIX * (C // GROUPS))
    return [
        (sums[3 * i : 3 * i + 1] + sums[3 * i + 1 : 3 * i + 2] + sums[3 * i + 2 : 3 * i + 3]) * scale
        for i in range(len(vectors))
    ]


def total(v):
    return jnp.sum(v, axis=0, keepdims=True)


def norm_stats(load, ones):
    zero = jnp.zeros((1, C), f32)
    (mean,) = group_means([over(lambda i, s: s + total(load(i)), zero)], ones)

    def square(i, s):
        centred = load(i) - mean
        return s + total(centred * centred)

    (variance,) = group_means([over(square, zero)], ones)
    return mean, lax.rsqrt(variance + norm_eps)


def put_shifted(dst, i, value, step):
    size = value.shape[0]
    column = lax.broadcasted_iota(jnp.int32, (size, C), 0) & (W - 1)
    at = pl.ds(pl.multiple_of(W + i * size, W), size)
    back = jnp.where(column == 0, 0.0, pltpu.roll(value, 1, 0))
    ahead = jnp.where(column == W - 1, 0.0, pltpu.roll(value, size - 1, 0))
    order = (back, value, ahead) if step == 1 else (ahead, value, back)
    for k in range(3):
        dst[at, k * C : (k + 1) * C] = order[k].astype(bf16)


def zero_edges(dst):
    dst[0:W, :] = jnp.zeros((W, TAPS), bf16)
    dst[W + PIX : ROWS, :] = jnp.zeros((W, TAPS), bf16)


def lay_shifted(mover, dst, src):
    zero_edges(dst)
    mover.ready(src)

    def step(i, carry):
        put_shifted(dst, i, src[rows(i), :].astype(f32), -1)
        return carry

    over(step, 0)


def conv_rows(shifted, weight, i, size):
    acc = None
    for kh in range(3):
        part = dot(
            shifted[pl.ds(pl.multiple_of(i * size + kh * W, W), size), :],
            weight[kh * TAPS : (kh + 1) * TAPS, :],
        )
        acc = part if acc is None else acc + part
    return acc


def conv_back_rows(shifted, weight, i, size):
    acc = None
    for kh in range(3):
        part = dot(
            shifted[pl.ds(pl.multiple_of(i * size + (2 - kh) * W, W), size), :],
            weight[:, kh * TAPS : (kh + 1) * TAPS],
            1,
            1,
        )
        acc = part if acc is None else acc + part
    return acc


def sigmoid(v):
    return 1.0 / (1.0 + jnp.exp(-v))


def silu_grad(v):
    s = sigmoid(v)
    return s * (1.0 + v * (1.0 - s))


def fetch(pieces, places, dst, sems):
    copies = []
    for k, (piece, (row, column)) in enumerate(zip(pieces, places)):
        height, width = piece.shape
        copies.append(
            pltpu.make_async_copy(
                piece, dst.at[pl.ds(row, height), pl.ds(column, width)], sems.at[k]
            )
        )
        copies[-1].start()
    return copies


def settle(copies):
    for copy in copies:
        copy.wait()


def square_sum(ref, mean):
    def square(i, s):
        centred = ref[rows(i), :].astype(f32) - mean
        return s + total(centred * centred)

    return over(square, jnp.zeros((1, C), f32))


def prepare_kernel(mover, conv_ref, gains, biases, conv_b, film_b, qv_b, proj_b, out_ref):
    mover.ready(conv_ref, gains, biases, conv_b, film_b, qv_b, proj_b)
    for tap in range(9):
        out_ref[:, tap * C : (tap + 1) * C] = conv_ref[tap]
    share = out_ref.shape[0]
    stacked = jnp.concatenate(
        [ref[...].astype(f32) for ref in (gains, biases, conv_b, film_b, qv_b, proj_b)]
        + [jnp.zeros((3, share), f32)],
        axis=0,
    ).astype(bf16)
    unit = lax.broadcasted_iota(jnp.int32, (16, PAD), 0) == lax.broadcasted_iota(
        jnp.int32, (16, PAD), 1
    )
    out_ref[:, 9 * C :] = dot(stacked, unit.astype(f32).astype(bf16), 0, 0).astype(bf16)


def first_kernel(places, mover, *refs):
    pieces, refs = refs[: len(places)], refs[len(places) :]
    (
        x_ref, order_ref, first_ref, hidden_ref, w1_ref, stats_ref, shifted, weight, raw, sems,
    ) = refs
    copies = fetch(pieces, places, raw, sems)
    ones = same_group()
    zero_edges(shifted)
    mover.ready(x_ref, order_ref)
    order = order_ref[...]
    load = lambda i: x_ref[rows(i), :].astype(f32)
    mean0, inv0 = norm_stats(load, ones)
    settle(copies)
    par = dot(raw[:, 9 * C :], order, 0, 1)
    row = lambda k: par[k : k + 1, :]
    for tap in range(9):
        part = dot(order, raw[:, tap * C : (tap + 1) * C]).astype(bf16)
        weight[tap * C : (tap + 1) * C, :] = part
        w1_ref[:, tap * C : (tap + 1) * C] = part
    mover.send(w1_ref)
    gain, bias = inv0 * row(0), row(3) - mean0 * inv0 * row(0)

    def start(i, carry):
        pre = load(i) * gain + bias
        act = pre * sigmoid(pre)
        first_ref[rows(i), :] = act.astype(bf16)
        put_shifted(shifted, i, act, 1)
        return carry

    over(start, 0)
    mover.send(first_ref)

    def conv1(i, s):
        value = conv_rows(shifted, weight, i, SIZE) + row(6)
        hidden_ref[rows(i, SIZE), :] = value
        return s + total(value)

    sums = lax.fori_loop(0, PIX // SIZE, conv1, jnp.zeros((1, C), f32))
    mover.send(hidden_ref)
    (mean1,) = group_means([sums], ones)
    (var1,) = group_means([square_sum(hidden_ref, mean1)], ones)
    inv1 = lax.rsqrt(var1 + norm_eps)
    zero = jnp.zeros((1, C), f32)
    stats_ref[...] = jnp.concatenate(
        [mean0, inv0, mean1, inv1, zero, zero, zero, zero] + [par[0:13, :], jnp.zeros((3, C), f32)],
        axis=0,
    )


def second_kernel(places, mover, *refs):
    pieces, refs = refs[: len(places)], refs[len(places) :]
    (
        order_ref, emb_ref, stats_ref, hidden_ref, x_ref,
        second_ref, residual_ref, attn_ref, projected_ref, w2_ref, wqkv_ref, wproj_ref, norm_ref,
        shifted, weight, raw, sems,
    ) = refs
    copies = fetch(pieces, places, raw, sems)
    ones = same_group()
    zero_edges(shifted)
    mover.ready(order_ref, emb_ref, stats_ref)
    order = order_ref[...]
    row = lambda k: stats_ref[8 + k : 9 + k, :]
    settle(copies)
    for tap in range(9):
        part = dot(order, raw[:, tap * C : (tap + 1) * C]).astype(bf16)
        weight[tap * C : (tap + 1) * C, :] = part
        w2_ref[:, tap * C : (tap + 1) * C] = part
    column = 9 * C
    wqkv_ref[...] = dot(order, raw[:, column : column + QKV]).astype(bf16)
    column += QKV
    wproj_ref[...] = dot(order, raw[:, column : column + ATT]).astype(bf16)
    column += ATT
    mover.send(w2_ref, wqkv_ref, wproj_ref)
    emb = dot(emb_ref[...], order).astype(bf16)
    wide = dot(emb, raw[:, column : column + 2 * C])
    column += 2 * C
    narrow = dot(emb, raw[:, column : column + 2 * PAD])
    film = total(wide[0:3]) + jnp.concatenate(
        [total(narrow[3 + 3 * k : 6 + 3 * k]) for k in range(3)], axis=1
    )
    scale = 1.0 + film[:, :C] + row(8)
    shift = film[:, C:] + row(9)
    mean1, inv1 = stats_ref[2:3, :], stats_ref[3:4, :]
    gain = inv1 * row(1) * scale
    bias = (row(4) - mean1 * inv1 * row(1)) * scale + shift
    mover.ready(hidden_ref, x_ref)

    def middle(i, carry):
        scaled = hidden_ref[rows(i), :] * gain + bias
        act = scaled * sigmoid(scaled)
        second_ref[rows(i), :] = act.astype(bf16)
        put_shifted(shifted, i, act, 1)
        return carry

    over(middle, 0)
    mover.send(second_ref)

    def conv2(i, s):
        value = (
            conv_rows(shifted, weight, i, SIZE) + row(7) + x_ref[rows(i, SIZE), :].astype(f32)
        )
        residual_ref[rows(i, SIZE), :] = value
        return s + total(value)

    sums = lax.fori_loop(0, PIX // SIZE, conv2, jnp.zeros((1, C), f32))
    mover.send(residual_ref)
    (mean2,) = group_means([sums], ones)
    (var2,) = group_means([square_sum(residual_ref, mean2)], ones)
    inv2 = lax.rsqrt(var2 + norm_eps)

    lane = lax.broadcasted_iota(jnp.int32, (8, PAD), 1)
    biases = []
    for g in range(HEADS):
        for which in (10, None, 11):
            if which is None:
                biases.append(jnp.zeros((1, PAD), f32))
            else:
                turned = jnp.broadcast_to(row(which), (8, C))
                if g:
                    turned = pltpu.roll(turned, C - g * HD, 1)
                biases.append(jnp.where(lane < HD, turned[:, :PAD], 0.0)[0:1])
    bias = jnp.concatenate(biases, axis=1)

    gain2, bias2 = inv2 * row(2), row(5) - mean2 * inv2 * row(2)

    def last(i, carry):
        attn = (residual_ref[rows(i, SIZE), :] * gain2 + bias2).astype(bf16)
        attn_ref[rows(i, SIZE), :] = attn
        projected_ref[rows(i, SIZE), :] = (dot(attn, wqkv_ref[...]) + bias).astype(bf16)
        return carry

    lax.fori_loop(0, PIX // SIZE, last, 0)
    norm_ref[...] = jnp.concatenate([mean2, inv2, scale, shift, jnp.zeros((4, C), f32)], axis=0)


def attention_kernel(
    loss_ref, order_any, residual_any, grad_ref, wproj_ref, stats_ref, qkv_ref,
    out_ref, gqkv_ref, wproj_grad_ref, sums_ref,
    branch, attended, keys_grad, values_grad, order_ref, residual_ref, sems,
):
    g = pl.program_id(0)
    factor = 1.0 / math.sqrt(HD)
    size = PIX
    loads = [
        pltpu.make_async_copy(residual_any, residual_ref, sems.at[0]),
        pltpu.make_async_copy(order_any, order_ref, sems.at[1]),
    ]

    @pl.when(g == 0)
    def _():
        for load in loads:
            load.start()

        def scaled(i, s):
            value = (grad_ref[rows(i), :].astype(f32) * loss_ref[0, 0]).astype(bf16)
            branch[rows(i), :] = value
            return s + total(value.astype(f32))

        sums_ref[...] = jnp.broadcast_to(over(scaled, jnp.zeros((1, C), f32)), (8, C))

    lanes = pl.ds(pl.multiple_of(g * PAD, PAD), PAD)
    keys_grad[...] = jnp.zeros_like(keys_grad)
    values_grad[...] = jnp.zeros_like(values_grad)

    def chunk(i, carry):
        queries = qkv_ref[rows(i, size), 0:PAD]
        keys = qkv_ref[:, PAD : 2 * PAD]
        values = qkv_ref[:, 2 * PAD : 3 * PAD]
        grad = dot(branch[rows(i, size), :], wproj_ref[:, lanes]).astype(bf16).astype(f32)
        scores = dot(queries, keys, 1, 1)
        top = jnp.max(scores, axis=1, keepdims=True)
        power = jnp.exp2((scores - top) * (factor * math.log2(math.e)))
        scale = 1.0 / jnp.sum(power, axis=1, keepdims=True)
        soft = power.astype(bf16)
        result = dot(soft, values) * scale
        attended[rows(i, size), lanes] = result.astype(bf16)
        inner = jnp.sum(grad * result, axis=1, keepdims=True) * scale
        grad = (grad * scale).astype(bf16)
        grad_scores = (power * (dot(grad, values, 1, 1) - inner)).astype(bf16)
        gqkv_ref[rows(i, size), 0:PAD] = (dot(grad_scores, keys) * factor).astype(bf16)
        keys_grad[...] += dot(queries, grad_scores, 0, 0)
        values_grad[...] += dot(grad, soft, 0, 0)
        return carry

    lax.fori_loop(0, PIX // size, chunk, 0)
    gqkv_ref[:, PAD : 2 * PAD] = (keys_grad[...].T * factor).astype(bf16)
    gqkv_ref[:, 2 * PAD : 3 * PAD] = values_grad[...].T.astype(bf16)

    @pl.when(g == HEADS - 1)
    def _():
        for load in loads:
            load.wait()

        def project(i, carry):
            value = residual_ref[rows(i, size), :] + dot(attended[rows(i, size), :], wproj_ref[...], 1, 1)
            out_ref[rows(i, size), :] = (value + stats_ref[20:21, :]).astype(bf16)
            return carry

        lax.fori_loop(0, PIX // size, project, 0)
        turned = dot(order_ref[...], branch[...], 0, 1).astype(bf16)
        wproj_grad_ref[...] = dot(turned, attended[...]).astype(bf16)


def put_halves(mover, own, others, column, value):
    at = slice(column, column + value.shape[1])
    block = C // 8
    for k, other in enumerate(others):
        other[:, at] = value[C // 2 + k * block : C // 2 + (k + 1) * block].astype(bf16)
        mover.send_columns(other, column, value.shape[1])
    own[:, at] = value[: C // 2].astype(bf16)
    mover.send_columns(own, column, value.shape[1])


def weight_grad(mover, own, others, order, act, shifted):
    turned = dot(order, act[...], 0, 1).astype(bf16)
    for kh in range(3):
        part = dot(turned, shifted[(2 - kh) * W : (2 - kh) * W + PIX, :])
        put_halves(mover, own, others, kh * TAPS, part)


def middle_kernel(
    mover, loss_ref, gqkv_ref, wqkv_ref, norm_ref, stats_ref, residual_ref, order_ref, attn_ref, grad_ref,
    second_ref, wproj_grad_ref, *refs,
):
    own_ref, *other_refs, grad_residual_ref, g2_ref, sums_ref, shifted, work = refs
    ones = same_group()
    zero_edges(shifted)
    size = SIZE
    mover.ready(gqkv_ref, wqkv_ref, norm_ref, stats_ref, residual_ref)
    mean, inv, gain = norm_ref[0:1, :], norm_ref[1:2, :], stats_ref[10:11, :]
    zero = jnp.zeros((1, C), f32)

    def step(i, carry):
        q_sum, u_sum, p_sum = carry
        packed = gqkv_ref[rows(i, size), :]
        q = dot(packed, wqkv_ref[...], 1, 1)
        work[rows(i, size), :] = q
        u = (residual_ref[rows(i, size), :] - mean) * inv
        return q_sum + total(q), u_sum + total(q * u), p_sum + total(packed.astype(f32))

    q_sum, u_sum, p_sum = lax.fori_loop(0, PIX // size, step, (zero, zero, jnp.zeros((1, QKV), f32)))
    first, second = group_means([q_sum * gain, u_sum * gain], ones)
    mover.ready(order_ref, attn_ref, grad_ref, second_ref, wproj_grad_ref)
    order = order_ref[...]
    turned = dot(order, attn_ref[...], 0, 1).astype(bf16)
    put_halves(mover, own_ref, other_refs, 9 * C, dot(turned, gqkv_ref[...]))
    put_halves(mover, own_ref, other_refs, 9 * C + QKV, wproj_grad_ref[...])

    def apply(i, s):
        u = (residual_ref[rows(i), :] - mean) * inv
        value = grad_ref[rows(i), :].astype(f32) * loss_ref[0, 0] + inv * (
            work[rows(i), :] * gain - first - u * second
        )
        grad_residual_ref[rows(i), :] = value
        rounded = value.astype(bf16)
        g2_ref[rows(i), :] = rounded
        rounded = rounded.astype(f32)
        put_shifted(shifted, i, rounded, -1)
        return s + total(rounded)

    conv_sum = over(apply, zero)
    mover.send(g2_ref, grad_residual_ref)
    weight_grad(mover, own_ref, other_refs, order, second_ref, shifted)

    def heads(k):
        value = jnp.zeros((8, C), f32)
        for g in range(HEADS):
            at = (3 * g + k) * PAD
            block = jnp.concatenate(
                [jnp.broadcast_to(p_sum[:, at : at + PAD], (8, PAD)), jnp.zeros((8, C - PAD), f32)], axis=1
            )
            value = value + (pltpu.roll(block, g * HD, 1) if g else block)
        return value[0:1]

    sums_ref[...] = jnp.concatenate(
        [u_sum, q_sum, conv_sum, heads(0), heads(2), jnp.zeros((3, C), f32)], axis=0
    )


def hidden_kernel(
    mover, g2_ref, w2_ref, hidden_ref, stats_ref, norm_ref, order_ref, emb_ref,
    g1_ref, sums_ref, own_ref, *refs,
):
    *other_refs, shifted, work = refs
    ones = same_group()
    size = SIZE
    lay_shifted(mover, shifted, g2_ref)
    mover.ready(w2_ref, hidden_ref, stats_ref, norm_ref)
    stat = lambda k: stats_ref[k : k + 1, :]
    mean, inv, gain, bias = stat(2), stat(3), stat(9), stat(12)
    scale, shift = norm_ref[2:3, :], norm_ref[3:4, :]
    zero = jnp.zeros((1, C), f32)

    def step(i, carry):
        u_sum, s_sum = carry
        u = (hidden_ref[rows(i, size), :] - mean) * inv
        scaled = (u * gain + bias) * scale + shift
        value = conv_back_rows(shifted, w2_ref, i, size) * silu_grad(scaled)
        work[rows(i, size), :] = value
        return u_sum + total(value * u), s_sum + total(value)

    u_sum, s_sum = lax.fori_loop(0, PIX // size, step, (zero, zero))
    film0 = u_sum * gain + s_sum * bias
    u_up, s_up = u_sum * scale, s_sum * scale
    first, second = group_means([s_up * gain, u_up * gain], ones)
    factor = scale * gain

    def apply(i, s):
        u = (hidden_ref[rows(i), :] - mean) * inv
        value = (inv * (work[rows(i), :] * factor - first - u * second)).astype(bf16)
        g1_ref[rows(i), :] = value
        return s + total(value.astype(f32))

    conv_sum = over(apply, zero)
    mover.send(g1_ref)
    sums_ref[...] = jnp.concatenate(
        [u_up, s_up, conv_sum, film0, s_sum, jnp.zeros((3, C), f32)], axis=0
    )
    mover.ready(order_ref, emb_ref)
    emb = sum(dot(order_ref[...], part, 0, 1) for part in split3(emb_ref[...]))
    film = jnp.concatenate([film0, s_sum], axis=1)
    put_halves(mover, own_ref, other_refs, 0, emb[:, 0:1] * film)
    narrow = sum(
        emb[:, k + 1 : k + 2] * film[:, k * 2 * PAD : (k + 1) * 2 * PAD] for k in range(3)
    )
    put_halves(mover, own_ref, other_refs, 2 * C, narrow)


def late_kernel(
    mover, g1_ref, first_ref, order_ref, proj_ref, sums2_ref, sums1_ref, sums0_ref, own_ref, *refs
):
    *other_refs, shifted = refs
    lay_shifted(mover, shifted, g1_ref)
    mover.ready(first_ref, order_ref, proj_ref, sums2_ref, sums1_ref, sums0_ref)
    order = order_ref[...]
    weight_grad(mover, own_ref, other_refs, order, first_ref, shifted)
    stacked = jnp.concatenate(
        [
            sums0_ref[0:1, :], sums1_ref[0:1, :], sums2_ref[0:1, :],
            sums0_ref[1:2, :], sums1_ref[1:2, :], sums2_ref[1:2, :],
            sums1_ref[2:3, :], sums2_ref[2:3, :], sums1_ref[3:5, :], sums2_ref[3:5, :], proj_ref[0:1, :],
            jnp.zeros((PAD - 13, C), f32),
        ],
        axis=0,
    )
    put_halves(mover, own_ref, other_refs, 9 * C, dot(order, stacked.astype(bf16), 0, 1))


def image_kernel(
    mover, g1_ref, w1_ref, stats_ref, x_ref, grad_residual_ref, out_ref, sums_ref, shifted, work
):
    ones = same_group()
    lay_shifted(mover, shifted, g1_ref)
    size = SIZE
    mover.ready(w1_ref, stats_ref, x_ref)
    stat = lambda k: stats_ref[k : k + 1, :]
    mean, inv, gain, bias = stat(0), stat(1), stat(8), stat(11)
    zero = jnp.zeros((1, C), f32)

    def step(i, carry):
        u_sum, s_sum = carry
        u = (x_ref[rows(i, size), :].astype(f32) - mean) * inv
        value = conv_back_rows(shifted, w1_ref, i, size) * silu_grad(u * gain + bias)
        work[rows(i, size), :] = value
        return u_sum + total(value * u), s_sum + total(value)

    u_sum, s_sum = lax.fori_loop(0, PIX // size, step, (zero, zero))
    first, second = group_means([s_sum * gain, u_sum * gain], ones)
    mover.ready(grad_residual_ref)

    def apply(i, carry):
        u = (x_ref[rows(i), :].astype(f32) - mean) * inv
        value = inv * (work[rows(i), :] * gain - first - u * second)
        out_ref[rows(i), :] = (grad_residual_ref[rows(i), :] + value).astype(bf16)
        return carry

    over(apply, 0)
    sums_ref[...] = jnp.concatenate([u_sum, s_sum, jnp.zeros((6, C), f32)], axis=0)


SMEM = pl.BlockSpec(memory_space=pltpu.SMEM)
ANY = pl.BlockSpec(memory_space=pl.ANY)
VMEM_LIMIT = 60 * 2**20
FIRST = 9 * C + PAD
SECOND = 9 * C + QKV + ATT + 2 * C + 2 * PAD
EARLY = 9 * C + QKV + ATT
FILM = 2 * C + 2 * PAD
LATE = 9 * C + PAD


def shape(*dims, dtype=bf16):
    return jax.ShapeDtypeStruct(dims, dtype)


def quarters(width):
    return [shape(C // 8, width)] * 4


def cost(us):
    return pl.CostEstimate(
        flops=int(us * 1_000_000_000), bytes_accessed=int(us * 3_600_000), transcendentals=0
    )


class Mover:
    def __init__(self, sources, inputs, outputs, targets, in_sems, out_sems):
        self.loads = {}
        for k, (source, buffer) in enumerate(zip(sources, inputs)):
            self.loads[id(buffer)] = pltpu.make_async_copy(source, buffer, in_sems.at[k])
            self.loads[id(buffer)].start()
        self.outputs = list(outputs)
        self.targets = {id(buffer): target for buffer, target in zip(outputs, targets)}
        self.sems = out_sems
        self.sent = []

    def ready(self, *buffers):
        for buffer in buffers:
            self.loads.pop(id(buffer)).wait()

    def store(self, source, target):
        copy = pltpu.make_async_copy(source, target, self.sems.at[len(self.sent)])
        copy.start()
        self.sent.append(copy)

    def send(self, *buffers):
        for buffer in buffers:
            self.outputs = [b for b in self.outputs if b is not buffer]
            self.store(buffer, self.targets[id(buffer)])

    def send_columns(self, buffer, start, width):
        self.outputs = [b for b in self.outputs if b is not buffer]
        at = (slice(None), pl.ds(start, width))
        self.store(buffer.at[at], self.targets[id(buffer)].at[at])

    def close(self):
        for load in self.loads.values():
            load.wait()
        self.send(*self.outputs)
        for copy in self.sent:
            copy.wait()


def call(kernel, operands, outs, scratch, us, name, scalars=0, pieces=0):
    count = len(operands) - scalars - pieces

    def body(*refs):
        fixed, refs = refs[: scalars + pieces], refs[scalars + pieces :]
        sources, refs = refs[:count], refs[count:]
        targets, refs = refs[: len(outs)], refs[len(outs) :]
        inputs, refs = refs[:count], refs[count:]
        outputs, refs = refs[: len(outs)], refs[len(outs) :]
        mover = Mover(sources, inputs, outputs, targets, refs[-2], refs[-1])
        kernel(mover, *fixed, *inputs, *outputs, *refs[:-2])
        mover.close()

    buffers = [pltpu.VMEM(v.shape, v.dtype) for v in [*operands[scalars + pieces :], *outs]]
    return pl.pallas_call(
        body,
        out_shape=outs,
        in_specs=[SMEM] * scalars + [ANY] * (pieces + count),
        out_specs=[ANY] * len(outs),
        scratch_shapes=buffers
        + scratch
        + [pltpu.SemaphoreType.DMA((max(count, 1),)), pltpu.SemaphoreType.DMA((len(outs) + 30,))],
        compiler_params=pltpu.CompilerParams(vmem_limit_bytes=VMEM_LIMIT),
        cost_estimate=cost(us),
        name=name,
    )(*operands)


class Still:
    def ready(self, *buffers):
        pass


def call_small(kernel, operands, outs, us, name):
    vmem = pl.BlockSpec(memory_space=pltpu.VMEM)
    return pl.pallas_call(
        lambda *refs: kernel(Still(), *refs),
        out_shape=outs,
        in_specs=[vmem] * len(operands),
        out_specs=[vmem] * len(outs),
        compiler_params=pltpu.CompilerParams(vmem_limit_bytes=16 * 2**20),
        cost_estimate=cost(us),
        name=name,
    )(*operands)


def prepare(conv, *small):
    share = conv.shape[2]
    return call(
        prepare_kernel, [conv.reshape(9, share, C), *small], [shape(share, FIRST)], [], 1, "prepare"
    )[0]


def weight_scratch(pieces, width):
    return [
        pltpu.VMEM((ROWS, TAPS), bf16), pltpu.VMEM((9 * C, C), bf16), pltpu.VMEM((C, width), bf16),
        pltpu.SemaphoreType.DMA((len(pieces),)),
    ]


def forward_first(places, pieces, order, x):
    return call(
        functools.partial(first_kernel, places),
        [*pieces, x, order],
        [shape(PIX, C), shape(PIX, C, dtype=f32), shape(C, 9 * C), shape(24, C, dtype=f32)],
        weight_scratch(pieces, FIRST), 13, "forward_first", 0, len(pieces),
    )


def forward_second(places, pieces, order, x, hidden, stats, emb):
    return call(
        functools.partial(second_kernel, places),
        [*pieces, order, emb, stats, hidden, x],
        [
            shape(PIX, C), shape(PIX, C, dtype=f32), shape(PIX, C), shape(PIX, QKV), shape(C, 9 * C),
            shape(C, QKV), shape(C, ATT), shape(8, C, dtype=f32),
        ],
        weight_scratch(pieces, SECOND), 10, "forward_second", 0, len(pieces),
    )


def attend(loss, order, grad, wproj, residual, stats, projected):
    whole = lambda *dims: pl.BlockSpec(dims, lambda g: (0, 0))
    head = pl.BlockSpec((PIX, 3 * PAD), lambda g: (0, g))
    return pl.pallas_call(
        attention_kernel,
        grid=(HEADS,),
        out_shape=[shape(PIX, C), shape(PIX, QKV), shape(C, ATT), shape(8, C, dtype=f32)],
        in_specs=[SMEM, ANY, ANY, whole(PIX, C), whole(C, ATT), whole(24, C), head],
        out_specs=[whole(PIX, C), head, whole(C, ATT), whole(8, C)],
        scratch_shapes=[
            pltpu.VMEM((PIX, C), bf16), pltpu.VMEM((PIX, ATT), bf16),
            pltpu.VMEM((PAD, PIX), f32), pltpu.VMEM((PAD, PIX), f32),
            pltpu.VMEM((C, C), bf16), pltpu.VMEM((PIX, C), f32), pltpu.SemaphoreType.DMA((2,)),
        ],
        compiler_params=pltpu.CompilerParams(vmem_limit_bytes=VMEM_LIMIT),
        cost_estimate=cost(31),
        name="attention",
    )(loss, order, residual, grad, wproj, stats, projected)


def backward_middle(loss, order, grad, attn, gqkv, wqkv, residual, stats, norm, second, wproj_grad):
    own, *others, grad_residual, g2, sums = call(
        middle_kernel,
        [loss, gqkv, wqkv, norm, stats, residual, order, attn, grad, second, wproj_grad],
        [
            shape(C // 2, EARLY), *quarters(EARLY), shape(PIX, C, dtype=f32), shape(PIX, C),
            shape(8, C, dtype=f32),
        ],
        [pltpu.VMEM((ROWS, TAPS), bf16), pltpu.VMEM((PIX, C), f32)], 16, "backward_middle", 1,
    )
    return own, others, grad_residual, g2, sums


def backward_hidden(order, emb, g2, w2, hidden, stats, norm):
    g1, sums, own, *others = call(
        hidden_kernel,
        [g2, w2, hidden, stats, norm, order, emb],
        [shape(PIX, C), shape(8, C, dtype=f32), shape(C // 2, FILM), *quarters(FILM)],
        [pltpu.VMEM((ROWS, TAPS), bf16), pltpu.VMEM((PIX, C), f32)], 10, "backward_hidden",
    )
    return g1, sums, own, others


def backward_late(order, g1, first, proj_sums, sums2, sums1, sums0):
    own, *others = call(
        late_kernel,
        [g1, first, order, proj_sums, sums2, sums1, sums0],
        [shape(C // 2, LATE), *quarters(LATE)],
        [pltpu.VMEM((ROWS, TAPS), bf16)], 7, "backward_late",
    )
    return own, others


def backward_image(g1, w1, x, stats, grad_residual):
    return call(
        image_kernel,
        [g1, w1, stats, x, grad_residual],
        [shape(PIX, C), shape(8, C, dtype=f32)],
        [pltpu.VMEM((ROWS, TAPS), bf16), pltpu.VMEM((PIX, C), f32)], 10, "backward_image",
    )


def store_kernel(*refs):
    count = len(refs) // 2
    copies = [
        pltpu.make_async_copy(refs[k], refs[count + k], refs[-1].at[k]) for k in range(count)
    ]
    for copy in copies:
        copy.start()
    settle(copies)


def store(*arrays):
    return pl.pallas_call(
        store_kernel,
        out_shape=[shape(*a.shape, dtype=a.dtype) for a in arrays],
        in_specs=[pl.BlockSpec(memory_space=pltpu.VMEM)] * len(arrays),
        out_specs=[ANY] * len(arrays),
        scratch_shapes=[pltpu.SemaphoreType.DMA((len(arrays),))],
        compiler_params=pltpu.CompilerParams(vmem_limit_bytes=16 * 2**20),
        cost_estimate=cost(2),
        name="store",
    )(*arrays)


def finish_kernel(mover, *refs):
    parts, (conv_ref, *outs) = refs[:4], refs[4:]
    mover.ready(*parts)
    value = sum(part[...].astype(f32) for part in parts)
    for tap in range(9):
        conv_ref[tap] = value[:, tap * C : (tap + 1) * C]
    share = value.shape[0]
    small = jnp.concatenate([value[:, 9 * C :], jnp.zeros((PAD - share, PAD), f32)], axis=0).T
    row = 0
    for out in outs:
        out[...] = small[row : row + out.shape[0], :share]
        row += out.shape[0]


def finish(parts):
    share = parts[0].shape[0]
    return call_small(
        finish_kernel,
        parts,
        [shape(9, share, C, dtype=f32)] + [shape(n, share, dtype=f32) for n in (3, 3, 2, 2, 2, 1)],
        1,
        "finish",
    )


def halves(width):
    return width // 2 // PAD * PAD


def core_kernel(groups, mover, *refs):
    owns, gots = refs[:groups], refs[groups:-4]
    stays, goes = refs[-4:-2], refs[-2:]
    mover.ready(*owns, *gots)
    block, cut = stays[0].shape[0] // 2, stays[0].shape[1]
    column = 0
    for group, own in enumerate(owns):
        width = own.shape[1]
        split = min(max(cut - column, 0), width)
        for k in range(4):
            got = gots[4 * group + k][...].astype(f32)
            value = (own[k * block : (k + 1) * block, :].astype(f32) + got).astype(bf16)
            x, y = k // 2, k % 2
            if split > 0:
                at = slice(y * block, (y + 1) * block)
                (goes if x else stays)[0][at, column : column + split] = value[:, :split]
            if split < width:
                at = slice(x * block, (x + 1) * block)
                start = column + split - cut
                (goes if y else stays)[1][at, start : start + width - split] = value[:, split:]
        column += width


def reduce_core(owns, gots):
    block = owns[0].shape[0] // 4
    width = sum(own.shape[1] for own in owns)
    cut = halves(width)
    parts = [shape(2 * block, cut), shape(2 * block, width - cut)]
    outs = call_small(
        functools.partial(core_kernel, len(owns)), [*owns, *gots], parts * 2, 3, "reduce_core"
    )
    return outs[:2], outs[2:]


def cross_kernel(mover, *refs):
    stays, gots, own_ref, goes = refs[:2], refs[2:4], refs[4], refs[5:]
    mover.ready(*stays, *gots)
    block, cut = goes[0].shape
    for k, columns in enumerate((slice(0, cut), slice(cut, own_ref.shape[1]))):
        value = (stays[k][...].astype(f32) + gots[k][...].astype(f32)).astype(bf16)
        own_ref[:, columns] = value[:block]
        goes[k][...] = value[block:]


def reduce_cross(stays, gots):
    block = stays[0].shape[0] // 2
    left, right = (stay.shape[1] for stay in stays)
    own, *goes = call_small(
        cross_kernel,
        [*stays, *gots],
        [shape(block, left + right), shape(block, left), shape(block, right)],
        2,
        "reduce_cross",
    )
    return own, goes


def column_kernel(mover, own_ref, left_ref, right_ref, *outs):
    mover.ready(own_ref, left_ref, right_ref)
    got = jnp.concatenate([left_ref[...].astype(f32), right_ref[...].astype(f32)], axis=1)
    value = own_ref[...].astype(f32) + got
    share = outs[0].shape[0]
    for k, out in enumerate(outs):
        out[...] = value[k * share : (k + 1) * share].astype(bf16)


def reduce_plane(own, gots):
    block, width = own.shape
    return call_small(
        column_kernel, [own, *gots], [shape(block // 4, width)] * 4, 1, "reduce_plane"
    )


both = ("dp", "sp")


def swap(value, axis, bit):
    count = lax.axis_size(axis)
    return lax.ppermute(value, axis, [(i, i ^ bit) for i in range(count)])


def after(value, *others):
    return lax.optimization_barrier((value, *others))[0]


def gather_pair(shard):
    return jnp.concatenate([shard, swap(shard, *Z_FAR)])


def gather_column(pair):
    return jnp.concatenate([pair, swap(pair, *Z_NEAR)])


def gather_plane(block):
    return swap(block, *X), swap(block, *Y)


def gather_corner(from_x, from_y):
    cut = halves(from_x.shape[1])
    return swap(from_y[:, :cut], *X), swap(from_x[:, cut:], *Y)


def gather_rest(block, from_x, from_y, left, right):
    mine = [block, from_y, from_x, left, right]
    return mine + [swap(piece, *CORE) for piece in mine]


def swap_plane(goes, first, second):
    return [swap(goes[0], *first), swap(goes[1], *second)]


def swap_column(shards):
    own, far, near, both_ways = shards
    return [own, swap(far, *Z_FAR), swap(near, *Z_NEAR), swap(both_ways, *Z_BOTH)]


def piece_places(width):
    cut = halves(width)
    places = [(0, 0), (48, 0), (96, 0), (144, 0), (144, cut)]
    return places + [(row + C // 2, column) for row, column in places]


def row_order(tree):
    row = jnp.arange(C)
    if tree:
        share = C // 32
        k = row // share
        dp = lax.axis_index("dp") ^ (k >> 4) ^ ((k >> 3 & 1) * 2)
        sp = lax.axis_index("sp") ^ (k >> 2 & 1) ^ ((k >> 1 & 1) * 2) ^ ((k & 1) * 4)
        row = (dp * 8 + sp) * share + row % share
    return (jnp.arange(C)[:, None] == row[None, :]).astype(bf16)


def time_embedding(steps):
    half_width = E // 2
    frequencies = jnp.exp(
        -math.log(10000.0) * jnp.arange(half_width, dtype=jnp.float32) / half_width
    )
    angles = steps.astype(jnp.float32)[:, None] * frequencies[None, :]
    return jnp.concatenate([jnp.cos(angles), jnp.sin(angles)], axis=1)


def padded_heads(value, axis):
    pads = [(0, 0)] * value.ndim
    pads[axis] = (0, PAD - HD)
    return jnp.pad(value, pads)


def embedding_rows(embedding, devices):
    share = C // devices
    by_device = embedding.reshape(devices, E // devices)
    wide = by_device[:, :share].reshape(C)
    narrow = jnp.repeat(by_device[:, share:], 3, axis=1).reshape(C)
    third = jnp.arange(C) % 3
    return jnp.stack([wide] + [jnp.where(third == k, narrow, 0.0) for k in range(3)])


def body(
    images,
    timesteps,
    loss_weight,
    out_grad,
    norm_gains,
    norm_biases,
    conv_biases,
    film_weight,
    film_bias,
    conv1_weight,
    conv2_weight,
    qkv_weight,
    qv_bias,
    proj_weight,
    proj_bias,
):
    row_parts = lax.axis_size("sp")
    devices = lax.axis_size("dp") * row_parts
    samples = images.shape[0] * images.shape[1]
    rows_here = images.shape[2]
    per = max(1, samples // row_parts)
    copies = max(1, row_parts // samples)
    share = C // devices
    embed_share = E // devices
    place = lax.axis_index("sp")
    tree = lax.axis_size("dp") == 4 and row_parts == 8

    def to_samples(value):
        value = value.reshape(samples // per, per * rows_here * W, C)
        if copies > 1:
            value = jnp.repeat(value, copies, axis=0)
        value = lax.all_to_all(value, "sp", split_axis=0, concat_axis=0, tiled=True)
        value = value.reshape(row_parts, per, rows_here * W, C).transpose(1, 0, 2, 3)
        return value.reshape(per, PIX, C)

    def to_rows(value):
        value = value.reshape(per, row_parts, rows_here * W, C).transpose(1, 0, 2, 3)
        value = value.reshape(row_parts, per * rows_here * W, C)
        value = lax.all_to_all(value, "sp", split_axis=0, concat_axis=0, tiled=True)
        return value[::copies].reshape(images.shape)

    first = (place // copies) * per
    steps = lax.dynamic_slice_in_dim(timesteps.reshape(samples), first, per)
    loss = lax.dynamic_slice_in_dim(loss_weight.reshape(samples), first, per)

    first_shard = prepare(
        conv1_weight, norm_gains, norm_biases, conv_biases, film_bias, qv_bias, proj_bias[None]
    )
    by_input = lambda w: w.transpose(2, 0, 1, 3).reshape(share, 9 * C)
    film = film_weight.reshape(embed_share, 2 * C)
    second_shard = jnp.concatenate(
        [
            by_input(conv2_weight),
            padded_heads(qkv_weight, 3).reshape(share, QKV),
            padded_heads(proj_weight.transpose(2, 0, 1), 2).reshape(share, ATT),
            film[:share],
            film[share:].reshape(share, 2 * PAD),
        ],
        axis=1,
    )
    order = row_order(tree)
    staged = tree and per == 1
    if tree:
        places = piece_places
        pair = gather_pair(first_shard)
        block = gather_column(pair)
        from_x, from_y = gather_plane(block)
        second_block = gather_column(gather_pair(after(second_shard, block)))
        images_in = to_samples(after(images, first_shard))
        left, right = gather_corner(from_x, from_y)
        first_pieces = gather_rest(block, from_x, from_y, left, right)
        from_x, from_y = gather_plane(after(second_block, left, right, images_in))
        if not staged:
            second_pieces = gather_rest(
                second_block, from_x, from_y, *gather_corner(from_x, from_y)
            )
    else:
        places = lambda width: [(0, 0)]
        gather = lambda shard: [lax.all_gather(shard, both, axis=0, tiled=True)]
        first_pieces, second_pieces = gather(first_shard), gather(second_shard)
        images_in = to_samples(images)
    if not staged:
        grads_in = to_samples(out_grad)

    outs, image_grads, totals = [], [], None
    for index in range(per):
        embedding = embedding_rows(
            jax.nn.silu(time_embedding(steps[index][None]))[0], devices
        )
        emb = jnp.pad(jnp.stack(split3(embedding), axis=1).reshape(12, C), ((0, 4), (0, 0)))
        embedding = jnp.pad(embedding, ((0, 4), (0, 0)))
        weight = loss[index].reshape(1, 1)
        x = images_in[index]
        if staged:
            x = after(x, second_block)
        first, hidden, w1, stats = forward_first(places(FIRST), first_pieces, order, x)
        if staged:
            from_x, from_y = after(from_x, hidden), after(from_y, hidden)
            left, right = gather_corner(from_x, from_y)
            grads_in = to_samples(after(out_grad, from_x, from_y))
            second_pieces = gather_rest(second_block, from_x, from_y, left, right)
        grad = grads_in[index]
        second, residual, attn, projected, w2, wqkv, wproj, norm = forward_second(
            places(SECOND), second_pieces, order, x, hidden, stats, emb
        )
        block_out, gqkv, wproj_grad, proj_sums = attend(
            weight, order, grad, wproj, residual, stats, projected
        )
        own, others, grad_residual, g2, sums2 = backward_middle(
            weight, order, grad, attn, gqkv, wqkv, residual, stats, norm, second, wproj_grad
        )
        if staged:
            out_rows = to_rows(block_out[None])
            gots = [swap(other, *CORE) for other in others]
        g1, sums1, film_own, film_others = backward_hidden(
            order, embedding, g2, w2, hidden, stats, norm
        )
        if staged:
            gots = [after(got, g1) for got in gots] + [swap(other, *CORE) for other in film_others]
            stays, goes = reduce_core([own, film_own], gots)
            g1 = after(g1, *goes, out_rows)
            gots = swap_plane(goes, X, Y)
        image_grad, sums0 = backward_image(g1, w1, x, stats, grad_residual)
        if staged:
            g1 = after(g1, image_grad)
        late_own, late_others = backward_late(order, g1, first, proj_sums, sums2, sums1, sums0)
        if staged:
            late_gots = [swap(other, *CORE) for other in late_others]
            image_rows = to_rows(image_grad[None])
        else:
            outs.append(block_out)
            image_grads.append(image_grad)
            grads = [
                jnp.concatenate(
                    [jnp.concatenate([own, *others]), jnp.concatenate([film_own, *film_others])], axis=1
                ),
                jnp.concatenate([late_own, *late_others]),
            ]
            grads = [g.astype(f32) for g in grads]
            totals = grads if totals is None else [a + b for a, b in zip(totals, grads)]
    if staged:
        own, goes = reduce_cross(stays, [after(got, late_own) for got in gots])
        gots = swap_plane(goes, Y, X)
        late_gots = [after(got, *goes) for got in late_gots]
        stays, goes = reduce_core([late_own], late_gots)
        late_gots = swap_plane(goes, X, Y)
        early = reduce_plane(own, [after(got, *goes) for got in gots])
        early = swap_column(early)
        late_gots[0], early[1] = lax.optimization_barrier((late_gots[0], early[1]))
        *late_gots, image_rows = lax.optimization_barrier((*late_gots, image_rows))
        late_own, goes = reduce_cross(stays, late_gots)
        late_gots = swap_plane(goes, Y, X)
        late = list(reduce_plane(late_own, late_gots))
        late = swap_column(late)
        early[1:] = [after(part, late[1]) for part in early[1:]]
        early = sum(part.astype(f32) for part in early)
        out_rows, image_rows = store(out_rows, image_rows)
        late[2:] = [after(part, early, out_rows) for part in late[2:]]
    else:
        image_rows, out_rows = to_rows(jnp.stack(image_grads)), to_rows(jnp.stack(outs))
        if copies > 1:
            totals = [jnp.where(place % copies == 0, t, 0.0) for t in totals]
        if tree:
            totals = [jnp.dot(order, t.astype(bf16), preferred_element_type=f32) for t in totals]
        early, late = (
            lax.psum_scatter(
                t.astype(bf16).reshape(devices, share, -1), both, scatter_dimension=0
            ).astype(f32)
            for t in totals
        )
    if not staged:
        late = [late] + [jnp.zeros_like(late)] * 3
    conv1_grad, gains_grad, biases_grad, conv_b_grad, film_b_grad, qv_grad, proj_b_grad = finish(late)
    conv2_grad = early[:, : 9 * C].reshape(share, 3, 3, C).transpose(1, 2, 0, 3)
    wqkv_grad = early[:, 9 * C : 9 * C + QKV].reshape(share, HEADS, 3, PAD)[..., :HD]
    wproj_grad = early[:, 9 * C + QKV : EARLY].reshape(share, HEADS, PAD)[..., :HD]
    film_grad = jnp.concatenate(
        [early[:, EARLY : EARLY + 2 * C], early[:, EARLY + 2 * C :].reshape(-1, 2 * C)]
    )
    return (
        out_rows,
        image_rows,
        gains_grad,
        biases_grad,
        conv_b_grad,
        film_grad.reshape(embed_share, 2, C),
        film_b_grad,
        conv1_grad.reshape(3, 3, share, C),
        conv2_grad,
        wqkv_grad,
        qv_grad,
        wproj_grad.transpose(1, 2, 0),
        proj_b_grad[0],
    )


def solution(mesh):
    return jax.shard_map(
        body,
        mesh=mesh,
        in_specs=(
            P(None, "dp", "sp", None, None),
            P(None, "dp"),
            P(None, "dp"),
            P(None, "dp", "sp", None, None),
            P(None, both),
            P(None, both),
            P(None, both),
            P(both, None, None),
            P(None, both),
            P(None, None, both, None),
            P(None, None, both, None),
            P(both, None, None, None),
            P(None, both),
            P(None, None, both),
            P(both),
        ),
        out_specs=(
            P(None, "dp", "sp", None, None),
            P(None, "dp", "sp", None, None),
            P(None, both),
            P(None, both),
            P(None, both),
            P(both, None, None),
            P(None, both),
            P(None, None, both, None),
            P(None, None, both, None),
            P(both, None, None, None),
            P(None, both),
            P(None, None, both),
            P(both),
        ),
        check_vma=False,
    )
```

```python
import functools
import functools
import math

import jax
import jax.numpy as jnp
from jax import lax
from jax.experimental import pallas as pl
from jax.experimental.pallas import tpu as pltpu
from jax.sharding import PartitionSpec as P

C = 384
E = 512
HEADS = 4
HD = 96
PAD = 128
GROUPS = 32
H = 32
W = 32
PIX = H * W
TAPS = 3 * C
QKV = HEADS * 3 * PAD
ATT = HEADS * PAD
ROWS = PIX + 2 * W
CHUNK = 128
SIZE = 512
norm_eps = 1e-05
X, Y, CORE, Z_NEAR, Z_FAR = ("dp", 2), ("sp", 1), ("dp", 1), ("sp", 2), ("sp", 4)
Z_BOTH = ("sp", 6)
bf16 = jnp.bfloat16
f32 = jnp.float32


def dot(a, b, ca=1, cb=0):
    return lax.dot_general(a, b, (((ca,), (cb,)), ((), ())), preferred_element_type=f32)


def rows(i, size=CHUNK):
    return pl.ds(pl.multiple_of(i * size, size), size)


def over(body, init, count=PIX // CHUNK, unroll=2):
    return lax.fori_loop(0, count, body, init, unroll=unroll)


def split3(v):
    hi = v.astype(bf16)
    rest = v - hi.astype(f32)
    mid = rest.astype(bf16)
    low = (rest - mid.astype(f32)).astype(bf16)
    return hi, mid, low


def same_group():
    lane = lax.broadcasted_iota(jnp.int32, (C, C), 1).astype(f32)
    sub = lax.broadcasted_iota(jnp.int32, (C, C), 0).astype(f32)
    width = GROUPS / C
    return (jnp.floor((lane + 0.5) * width) == jnp.floor((sub + 0.5) * width)).astype(f32).astype(bf16)


def group_means(vectors, ones):
    parts = [p for v in vectors for p in split3(v)]
    count = len(parts)
    stacked = jnp.concatenate(
        [p.astype(f32) for p in parts] + [jnp.zeros((16 - count, C), f32)], axis=0
    ).astype(bf16)
    sums = dot(stacked, ones)
    scale = 1.0 / (PIX * (C // GROUPS))
    return [
        (sums[3 * i : 3 * i + 1] + sums[3 * i + 1 : 3 * i + 2] + sums[3 * i + 2 : 3 * i + 3]) * scale
        for i in range(len(vectors))
    ]


def total(v):
    return jnp.sum(v, axis=0, keepdims=True)


def norm_stats(load, ones):
    zero = jnp.zeros((1, C), f32)
    (mean,) = group_means([over(lambda i, s: s + total(load(i)), zero)], ones)

    def square(i, s):
        centred = load(i) - mean
        return s + total(centred * centred)

    (variance,) = group_means([over(square, zero)], ones)
    return mean, lax.rsqrt(variance + norm_eps)


def put_shifted(dst, i, value, step):
    size = value.shape[0]
    column = lax.broadcasted_iota(jnp.int32, (size, C), 0) & (W - 1)
    at = pl.ds(pl.multiple_of(W + i * size, W), size)
    back = jnp.where(column == 0, 0.0, pltpu.roll(value, 1, 0))
    ahead = jnp.where(column == W - 1, 0.0, pltpu.roll(value, size - 1, 0))
    order = (back, value, ahead) if step == 1 else (ahead, value, back)
    for k in range(3):
        dst[at, k * C : (k + 1) * C] = order[k].astype(bf16)


def zero_edges(dst):
    dst[0:W, :] = jnp.zeros((W, TAPS), bf16)
    dst[W + PIX : ROWS, :] = jnp.zeros((W, TAPS), bf16)


def lay_shifted(mover, dst, src):
    zero_edges(dst)
    mover.ready(src)

    def step(i, carry):
        put_shifted(dst, i, src[rows(i), :].astype(f32), -1)
        return carry

    over(step, 0)


def conv_rows(shifted, weight, i, size):
    acc = None
    for kh in range(3):
        part = dot(
            shifted[pl.ds(pl.multiple_of(i * size + kh * W, W), size), :],
            weight[kh * TAPS : (kh + 1) * TAPS, :],
        )
        acc = part if acc is None else acc + part
    return acc


def conv_back_rows(shifted, weight, i, size):
    acc = None
    for kh in range(3):
        part = dot(
            shifted[pl.ds(pl.multiple_of(i * size + (2 - kh) * W, W), size), :],
            weight[:, kh * TAPS : (kh + 1) * TAPS],
            1,
            1,
        )
        acc = part if acc is None else acc + part
    return acc


def sigmoid(v):
    return 1.0 / (1.0 + jnp.exp(-v))


def silu_grad(v):
    s = sigmoid(v)
    return s * (1.0 + v * (1.0 - s))


def fetch(pieces, places, dst, sems):
    copies = []
    for k, (piece, (row, column)) in enumerate(zip(pieces, places)):
        height, width = piece.shape
        copies.append(
            pltpu.make_async_copy(
                piece, dst.at[pl.ds(row, height), pl.ds(column, width)], sems.at[k]
            )
        )
        copies[-1].start()
    return copies


def settle(copies):
    for copy in copies:
        copy.wait()


def square_sum(ref, mean):
    def square(i, s):
        centred = ref[rows(i), :].astype(f32) - mean
        return s + total(centred * centred)

    return over(square, jnp.zeros((1, C), f32))


def prepare_kernel(mover, conv_ref, gains, biases, conv_b, film_b, qv_b, proj_b, out_ref):
    mover.ready(conv_ref, gains, biases, conv_b, film_b, qv_b, proj_b)
    for tap in range(9):
        out_ref[:, tap * C : (tap + 1) * C] = conv_ref[tap]
    share = out_ref.shape[0]
    stacked = jnp.concatenate(
        [ref[...].astype(f32) for ref in (gains, biases, conv_b, film_b, qv_b, proj_b)]
        + [jnp.zeros((3, share), f32)],
        axis=0,
    ).astype(bf16)
    unit = lax.broadcasted_iota(jnp.int32, (16, PAD), 0) == lax.broadcasted_iota(
        jnp.int32, (16, PAD), 1
    )
    out_ref[:, 9 * C :] = dot(stacked, unit.astype(f32).astype(bf16), 0, 0).astype(bf16)


def first_kernel(places, mover, *refs):
    pieces, refs = refs[: len(places)], refs[len(places) :]
    (
        x_ref, order_ref, first_ref, hidden_ref, w1_ref, stats_ref, shifted, weight, raw, sems,
    ) = refs
    copies = fetch(pieces, places, raw, sems)
    ones = same_group()
    zero_edges(shifted)
    mover.ready(x_ref, order_ref)
    order = order_ref[...]
    load = lambda i: x_ref[rows(i), :].astype(f32)
    mean0, inv0 = norm_stats(load, ones)
    settle(copies)
    par = dot(raw[:, 9 * C :], order, 0, 1)
    row = lambda k: par[k : k + 1, :]
    for tap in range(9):
        part = dot(order, raw[:, tap * C : (tap + 1) * C]).astype(bf16)
        weight[tap * C : (tap + 1) * C, :] = part
        w1_ref[:, tap * C : (tap + 1) * C] = part
    mover.send(w1_ref)
    gain, bias = inv0 * row(0), row(3) - mean0 * inv0 * row(0)

    def start(i, carry):
        pre = load(i) * gain + bias
        act = pre * sigmoid(pre)
        first_ref[rows(i), :] = act.astype(bf16)
        put_shifted(shifted, i, act, 1)
        return carry

    over(start, 0)
    mover.send(first_ref)

    def conv1(i, s):
        value = conv_rows(shifted, weight, i, SIZE) + row(6)
        hidden_ref[rows(i, SIZE), :] = value
        return s + total(value)

    sums = lax.fori_loop(0, PIX // SIZE, conv1, jnp.zeros((1, C), f32))
    mover.send(hidden_ref)
    (mean1,) = group_means([sums], ones)
    (var1,) = group_means([square_sum(hidden_ref, mean1)], ones)
    inv1 = lax.rsqrt(var1 + norm_eps)
    zero = jnp.zeros((1, C), f32)
    stats_ref[...] = jnp.concatenate(
        [mean0, inv0, mean1, inv1, zero, zero, zero, zero] + [par[0:13, :], jnp.zeros((3, C), f32)],
        axis=0,
    )


def second_kernel(places, mover, *refs):
    pieces, refs = refs[: len(places)], refs[len(places) :]
    (
        order_ref, emb_ref, stats_ref, hidden_ref, x_ref,
        second_ref, residual_ref, attn_ref, projected_ref, w2_ref, wqkv_ref, wproj_ref, norm_ref,
        shifted, weight, raw, sems,
    ) = refs
    copies = fetch(pieces, places, raw, sems)
    ones = same_group()
    zero_edges(shifted)
    mover.ready(order_ref, emb_ref, stats_ref)
    order = order_ref[...]
    row = lambda k: stats_ref[8 + k : 9 + k, :]
    settle(copies)
    for tap in range(9):
        part = dot(order, raw[:, tap * C : (tap + 1) * C]).astype(bf16)
        weight[tap * C : (tap + 1) * C, :] = part
        w2_ref[:, tap * C : (tap + 1) * C] = part
    column = 9 * C
    wqkv_ref[...] = dot(order, raw[:, column : column + QKV]).astype(bf16)
    column += QKV
    wproj_ref[...] = dot(order, raw[:, column : column + ATT]).astype(bf16)
    column += ATT
    mover.send(w2_ref, wqkv_ref, wproj_ref)
    emb = dot(emb_ref[...], order).astype(bf16)
    wide = dot(emb, raw[:, column : column + 2 * C])
    column += 2 * C
    narrow = dot(emb, raw[:, column : column + 2 * PAD])
    film = total(wide[0:3]) + jnp.concatenate(
        [total(narrow[3 + 3 * k : 6 + 3 * k]) for k in range(3)], axis=1
    )
    scale = 1.0 + film[:, :C] + row(8)
    shift = film[:, C:] + row(9)
    mean1, inv1 = stats_ref[2:3, :], stats_ref[3:4, :]
    gain = inv1 * row(1) * scale
    bias = (row(4) - mean1 * inv1 * row(1)) * scale + shift
    mover.ready(hidden_ref, x_ref)

    def middle(i, carry):
        scaled = hidden_ref[rows(i), :] * gain + bias
        act = scaled * sigmoid(scaled)
        second_ref[rows(i), :] = act.astype(bf16)
        put_shifted(shifted, i, act, 1)
        return carry

    over(middle, 0)
    mover.send(second_ref)

    def conv2(i, s):
        value = (
            conv_rows(shifted, weight, i, SIZE) + row(7) + x_ref[rows(i, SIZE), :].astype(f32)
        )
        residual_ref[rows(i, SIZE), :] = value
        return s + total(value)

    sums = lax.fori_loop(0, PIX // SIZE, conv2, jnp.zeros((1, C), f32))
    mover.send(residual_ref)
    (mean2,) = group_means([sums], ones)
    (var2,) = group_means([square_sum(residual_ref, mean2)], ones)
    inv2 = lax.rsqrt(var2 + norm_eps)

    lane = lax.broadcasted_iota(jnp.int32, (8, PAD), 1)
    biases = []
    for g in range(HEADS):
        for which in (10, None, 11):
            if which is None:
                biases.append(jnp.zeros((1, PAD), f32))
            else:
                turned = jnp.broadcast_to(row(which), (8, C))
                if g:
                    turned = pltpu.roll(turned, C - g * HD, 1)
                biases.append(jnp.where(lane < HD, turned[:, :PAD], 0.0)[0:1])
    bias = jnp.concatenate(biases, axis=1)

    gain2, bias2 = inv2 * row(2), row(5) - mean2 * inv2 * row(2)

    def last(i, carry):
        attn = (residual_ref[rows(i, SIZE), :] * gain2 + bias2).astype(bf16)
        attn_ref[rows(i, SIZE), :] = attn
        projected_ref[rows(i, SIZE), :] = (dot(attn, wqkv_ref[...]) + bias).astype(bf16)
        return carry

    lax.fori_loop(0, PIX // SIZE, last, 0)
    norm_ref[...] = jnp.concatenate([mean2, inv2, scale, shift, jnp.zeros((4, C), f32)], axis=0)


def attention_kernel(
    loss_ref, order_any, residual_any, grad_ref, wproj_ref, stats_ref, qkv_ref,
    out_ref, gqkv_ref, wproj_grad_ref, sums_ref,
    branch, attended, keys_grad, values_grad, order_ref, residual_ref, sems,
):
    g = pl.program_id(0)
    factor = 1.0 / math.sqrt(HD)
    size = PIX
    loads = [
        pltpu.make_async_copy(residual_any, residual_ref, sems.at[0]),
        pltpu.make_async_copy(order_any, order_ref, sems.at[1]),
    ]

    @pl.when(g == 0)
    def _():
        for load in loads:
            load.start()

        def scaled(i, s):
            value = (grad_ref[rows(i), :].astype(f32) * loss_ref[0, 0]).astype(bf16)
            branch[rows(i), :] = value
            return s + total(value.astype(f32))

        sums_ref[...] = jnp.broadcast_to(over(scaled, jnp.zeros((1, C), f32)), (8, C))

    lanes = pl.ds(pl.multiple_of(g * PAD, PAD), PAD)
    keys_grad[...] = jnp.zeros_like(keys_grad)
    values_grad[...] = jnp.zeros_like(values_grad)

    def chunk(i, carry):
        queries = qkv_ref[rows(i, size), 0:PAD]
        keys = qkv_ref[:, PAD : 2 * PAD]
        values = qkv_ref[:, 2 * PAD : 3 * PAD]
        grad = dot(branch[rows(i, size), :], wproj_ref[:, lanes]).astype(bf16).astype(f32)
        scores = dot(queries, keys, 1, 1)
        top = jnp.max(scores, axis=1, keepdims=True)
        power = jnp.exp2((scores - top) * (factor * math.log2(math.e)))
        scale = 1.0 / jnp.sum(power, axis=1, keepdims=True)
        soft = power.astype(bf16)
        result = dot(soft, values) * scale
        attended[rows(i, size), lanes] = result.astype(bf16)
        inner = jnp.sum(grad * result, axis=1, keepdims=True) * scale
        grad = (grad * scale).astype(bf16)
        grad_scores = (power * (dot(grad, values, 1, 1) - inner)).astype(bf16)
        gqkv_ref[rows(i, size), 0:PAD] = (dot(grad_scores, keys) * factor).astype(bf16)
        keys_grad[...] += dot(queries, grad_scores, 0, 0)
        values_grad[...] += dot(grad, soft, 0, 0)
        return carry

    lax.fori_loop(0, PIX // size, chunk, 0)
    gqkv_ref[:, PAD : 2 * PAD] = (keys_grad[...].T * factor).astype(bf16)
    gqkv_ref[:, 2 * PAD : 3 * PAD] = values_grad[...].T.astype(bf16)

    @pl.when(g == HEADS - 1)
    def _():
        for load in loads:
            load.wait()

        def project(i, carry):
            value = residual_ref[rows(i, size), :] + dot(attended[rows(i, size), :], wproj_ref[...], 1, 1)
            out_ref[rows(i, size), :] = (value + stats_ref[20:21, :]).astype(bf16)
            return carry

        lax.fori_loop(0, PIX // size, project, 0)
        turned = dot(order_ref[...], branch[...], 0, 1).astype(bf16)
        wproj_grad_ref[...] = dot(turned, attended[...]).astype(bf16)


def put_halves(mover, own, others, column, value):
    at = slice(column, column + value.shape[1])
    block = C // 2 // len(others)
    for k, other in enumerate(others):
        other[:, at] = value[C // 2 + k * block : C // 2 + (k + 1) * block].astype(bf16)
        mover.send_columns(other, column, value.shape[1])
    own[:, at] = value[: C // 2].astype(bf16)
    mover.send_columns(own, column, value.shape[1])


def weight_grad(mover, own, others, order, act, shifted):
    turned = dot(order, act[...], 0, 1).astype(bf16)
    for kh in range(3):
        part = dot(turned, shifted[(2 - kh) * W : (2 - kh) * W + PIX, :])
        put_halves(mover, own, others, kh * TAPS, part)


def middle_kernel(
    mover, loss_ref, gqkv_ref, wqkv_ref, norm_ref, stats_ref, residual_ref, order_ref, attn_ref, grad_ref,
    second_ref, wproj_grad_ref, *refs,
):
    own_ref, *other_refs, grad_residual_ref, g2_ref, sums_ref, shifted, work = refs
    ones = same_group()
    zero_edges(shifted)
    size = SIZE
    mover.ready(gqkv_ref, wqkv_ref, norm_ref, stats_ref, residual_ref)
    mean, inv, gain = norm_ref[0:1, :], norm_ref[1:2, :], stats_ref[10:11, :]
    zero = jnp.zeros((1, C), f32)

    def step(i, carry):
        q_sum, u_sum, p_sum = carry
        packed = gqkv_ref[rows(i, size), :]
        q = dot(packed, wqkv_ref[...], 1, 1)
        work[rows(i, size), :] = q
        u = (residual_ref[rows(i, size), :] - mean) * inv
        return q_sum + total(q), u_sum + total(q * u), p_sum + total(packed.astype(f32))

    q_sum, u_sum, p_sum = lax.fori_loop(0, PIX // size, step, (zero, zero, jnp.zeros((1, QKV), f32)))
    first, second = group_means([q_sum * gain, u_sum * gain], ones)
    mover.ready(order_ref, attn_ref, grad_ref, second_ref, wproj_grad_ref)
    order = order_ref[...]
    turned = dot(order, attn_ref[...], 0, 1).astype(bf16)
    put_halves(mover, own_ref, other_refs, 9 * C, dot(turned, gqkv_ref[...]))
    put_halves(mover, own_ref, other_refs, 9 * C + QKV, wproj_grad_ref[...])

    def apply(i, s):
        u = (residual_ref[rows(i), :] - mean) * inv
        value = grad_ref[rows(i), :].astype(f32) * loss_ref[0, 0] + inv * (
            work[rows(i), :] * gain - first - u * second
        )
        grad_residual_ref[rows(i), :] = value
        rounded = value.astype(bf16)
        g2_ref[rows(i), :] = rounded
        rounded = rounded.astype(f32)
        put_shifted(shifted, i, rounded, -1)
        return s + total(rounded)

    conv_sum = over(apply, zero)
    mover.send(g2_ref, grad_residual_ref)
    weight_grad(mover, own_ref, other_refs, order, second_ref, shifted)

    def heads(k):
        value = jnp.zeros((8, C), f32)
        for g in range(HEADS):
            at = (3 * g + k) * PAD
            block = jnp.concatenate(
                [jnp.broadcast_to(p_sum[:, at : at + PAD], (8, PAD)), jnp.zeros((8, C - PAD), f32)], axis=1
            )
            value = value + (pltpu.roll(block, g * HD, 1) if g else block)
        return value[0:1]

    sums_ref[...] = jnp.concatenate(
        [u_sum, q_sum, conv_sum, heads(0), heads(2), jnp.zeros((3, C), f32)], axis=0
    )


def hidden_kernel(
    mover, g2_ref, w2_ref, hidden_ref, stats_ref, norm_ref, order_ref, emb_ref,
    g1_ref, sums_ref, own_ref, *refs,
):
    *other_refs, shifted, work = refs
    ones = same_group()
    size = SIZE
    lay_shifted(mover, shifted, g2_ref)
    mover.ready(w2_ref, hidden_ref, stats_ref, norm_ref)
    stat = lambda k: stats_ref[k : k + 1, :]
    mean, inv, gain, bias = stat(2), stat(3), stat(9), stat(12)
    scale, shift = norm_ref[2:3, :], norm_ref[3:4, :]
    zero = jnp.zeros((1, C), f32)

    def step(i, carry):
        u_sum, s_sum = carry
        u = (hidden_ref[rows(i, size), :] - mean) * inv
        scaled = (u * gain + bias) * scale + shift
        value = conv_back_rows(shifted, w2_ref, i, size) * silu_grad(scaled)
        work[rows(i, size), :] = value
        return u_sum + total(value * u), s_sum + total(value)

    u_sum, s_sum = lax.fori_loop(0, PIX // size, step, (zero, zero))
    film0 = u_sum * gain + s_sum * bias
    u_up, s_up = u_sum * scale, s_sum * scale
    first, second = group_means([s_up * gain, u_up * gain], ones)
    factor = scale * gain

    def apply(i, s):
        u = (hidden_ref[rows(i), :] - mean) * inv
        value = (inv * (work[rows(i), :] * factor - first - u * second)).astype(bf16)
        g1_ref[rows(i), :] = value
        return s + total(value.astype(f32))

    conv_sum = over(apply, zero)
    mover.send(g1_ref)
    sums_ref[...] = jnp.concatenate(
        [u_up, s_up, conv_sum, film0, s_sum, jnp.zeros((3, C), f32)], axis=0
    )
    mover.ready(order_ref, emb_ref)
    emb = sum(dot(order_ref[...], part, 0, 1) for part in split3(emb_ref[...]))
    film = jnp.concatenate([film0, s_sum], axis=1)
    put_halves(mover, own_ref, other_refs, 0, emb[:, 0:1] * film)
    narrow = sum(
        emb[:, k + 1 : k + 2] * film[:, k * 2 * PAD : (k + 1) * 2 * PAD] for k in range(3)
    )
    put_halves(mover, own_ref, other_refs, 2 * C, narrow)


def late_kernel(
    mover, g1_ref, first_ref, order_ref, proj_ref, sums2_ref, sums1_ref, sums0_ref, own_ref, *refs
):
    *other_refs, shifted = refs
    lay_shifted(mover, shifted, g1_ref)
    mover.ready(first_ref, order_ref, proj_ref, sums2_ref, sums1_ref, sums0_ref)
    order = order_ref[...]
    weight_grad(mover, own_ref, other_refs, order, first_ref, shifted)
    stacked = jnp.concatenate(
        [
            sums0_ref[0:1, :], sums1_ref[0:1, :], sums2_ref[0:1, :],
            sums0_ref[1:2, :], sums1_ref[1:2, :], sums2_ref[1:2, :],
            sums1_ref[2:3, :], sums2_ref[2:3, :], sums1_ref[3:5, :], sums2_ref[3:5, :], proj_ref[0:1, :],
            jnp.zeros((PAD - 13, C), f32),
        ],
        axis=0,
    )
    put_halves(mover, own_ref, other_refs, 9 * C, dot(order, stacked.astype(bf16), 0, 1))


def image_kernel(
    mover, g1_ref, w1_ref, stats_ref, x_ref, grad_residual_ref, out_ref, sums_ref, shifted, work
):
    ones = same_group()
    lay_shifted(mover, shifted, g1_ref)
    size = SIZE
    mover.ready(w1_ref, stats_ref, x_ref)
    stat = lambda k: stats_ref[k : k + 1, :]
    mean, inv, gain, bias = stat(0), stat(1), stat(8), stat(11)
    zero = jnp.zeros((1, C), f32)

    def step(i, carry):
        u_sum, s_sum = carry
        u = (x_ref[rows(i, size), :].astype(f32) - mean) * inv
        value = conv_back_rows(shifted, w1_ref, i, size) * silu_grad(u * gain + bias)
        work[rows(i, size), :] = value
        return u_sum + total(value * u), s_sum + total(value)

    u_sum, s_sum = lax.fori_loop(0, PIX // size, step, (zero, zero))
    first, second = group_means([s_sum * gain, u_sum * gain], ones)
    mover.ready(grad_residual_ref)

    def apply(i, carry):
        u = (x_ref[rows(i), :].astype(f32) - mean) * inv
        value = inv * (work[rows(i), :] * gain - first - u * second)
        out_ref[rows(i), :] = (grad_residual_ref[rows(i), :] + value).astype(bf16)
        return carry

    over(apply, 0)
    sums_ref[...] = jnp.concatenate([u_sum, s_sum, jnp.zeros((6, C), f32)], axis=0)


SMEM = pl.BlockSpec(memory_space=pltpu.SMEM)
ANY = pl.BlockSpec(memory_space=pl.ANY)
VMEM_LIMIT = 60 * 2**20
FIRST = 9 * C + PAD
SECOND = 9 * C + QKV + ATT + 2 * C + 2 * PAD
EARLY = 9 * C + QKV + ATT
FILM = 2 * C + 2 * PAD
LATE = 9 * C + PAD


def shape(*dims, dtype=bf16):
    return jax.ShapeDtypeStruct(dims, dtype)


def quarters(width):
    return [shape(C // 8, width)] * 4


def cost(us):
    return pl.CostEstimate(
        flops=int(us * 1_000_000_000), bytes_accessed=int(us * 3_600_000), transcendentals=0
    )


class Mover:
    def __init__(self, sources, inputs, outputs, targets, in_sems, out_sems):
        self.loads = {}
        for k, (source, buffer) in enumerate(zip(sources, inputs)):
            self.loads[id(buffer)] = pltpu.make_async_copy(source, buffer, in_sems.at[k])
            self.loads[id(buffer)].start()
        self.outputs = list(outputs)
        self.targets = {id(buffer): target for buffer, target in zip(outputs, targets)}
        self.sems = out_sems
        self.sent = []

    def ready(self, *buffers):
        for buffer in buffers:
            self.loads.pop(id(buffer)).wait()

    def store(self, source, target):
        copy = pltpu.make_async_copy(source, target, self.sems.at[len(self.sent)])
        copy.start()
        self.sent.append(copy)

    def send(self, *buffers):
        for buffer in buffers:
            self.outputs = [b for b in self.outputs if b is not buffer]
            self.store(buffer, self.targets[id(buffer)])

    def send_columns(self, buffer, start, width):
        self.outputs = [b for b in self.outputs if b is not buffer]
        at = (slice(None), pl.ds(start, width))
        self.store(buffer.at[at], self.targets[id(buffer)].at[at])

    def close(self):
        for load in self.loads.values():
            load.wait()
        self.send(*self.outputs)
        for copy in self.sent:
            copy.wait()


def call(kernel, operands, outs, scratch, us, name, scalars=0, pieces=0, room=60):
    count = len(operands) - scalars - pieces

    def body(*refs):
        fixed, refs = refs[: scalars + pieces], refs[scalars + pieces :]
        sources, refs = refs[:count], refs[count:]
        targets, refs = refs[: len(outs)], refs[len(outs) :]
        inputs, refs = refs[:count], refs[count:]
        outputs, refs = refs[: len(outs)], refs[len(outs) :]
        mover = Mover(sources, inputs, outputs, targets, refs[-2], refs[-1])
        kernel(mover, *fixed, *inputs, *outputs, *refs[:-2])
        mover.close()

    buffers = [pltpu.VMEM(v.shape, v.dtype) for v in [*operands[scalars + pieces :], *outs]]
    return pl.pallas_call(
        body,
        out_shape=outs,
        in_specs=[SMEM] * scalars + [ANY] * (pieces + count),
        out_specs=[ANY] * len(outs),
        scratch_shapes=buffers
        + scratch
        + [pltpu.SemaphoreType.DMA((max(count, 1),)), pltpu.SemaphoreType.DMA((len(outs) + 30,))],
        compiler_params=pltpu.CompilerParams(vmem_limit_bytes=room * 2**20),
        cost_estimate=cost(us),
        name=name,
    )(*operands)


class Still:
    def ready(self, *buffers):
        pass

    def send(self, *buffers):
        pass


def call_small(kernel, operands, outs, us, name):
    vmem = pl.BlockSpec(memory_space=pltpu.VMEM)
    return pl.pallas_call(
        lambda *refs: kernel(Still(), *refs),
        out_shape=outs,
        in_specs=[vmem] * len(operands),
        out_specs=[vmem] * len(outs),
        compiler_params=pltpu.CompilerParams(vmem_limit_bytes=16 * 2**20),
        cost_estimate=cost(us),
        name=name,
    )(*operands)


def prepare(conv, *small):
    share = conv.shape[2]
    return call(
        prepare_kernel, [conv.reshape(9, share, C), *small], [shape(share, FIRST)], [], 1, "prepare"
    )[0]


def weight_scratch(pieces, width):
    return [
        pltpu.VMEM((ROWS, TAPS), bf16), pltpu.VMEM((9 * C, C), bf16), pltpu.VMEM((C, width), bf16),
        pltpu.SemaphoreType.DMA((len(pieces),)),
    ]


def forward_first(places, pieces, order, x):
    return call(
        functools.partial(first_kernel, places),
        [*pieces, x, order],
        [shape(PIX, C), shape(PIX, C, dtype=f32), shape(C, 9 * C), shape(24, C, dtype=f32)],
        weight_scratch(pieces, FIRST), 13, "forward_first", 0, len(pieces),
    )


def forward_second(places, pieces, order, x, hidden, stats, emb):
    return call(
        functools.partial(second_kernel, places),
        [*pieces, order, emb, stats, hidden, x],
        [
            shape(PIX, C), shape(PIX, C, dtype=f32), shape(PIX, C), shape(PIX, QKV), shape(C, 9 * C),
            shape(C, QKV), shape(C, ATT), shape(8, C, dtype=f32),
        ],
        weight_scratch(pieces, SECOND), 10, "forward_second", 0, len(pieces),
    )


def attend(loss, order, grad, wproj, residual, stats, projected):
    whole = lambda *dims: pl.BlockSpec(dims, lambda g: (0, 0))
    head = pl.BlockSpec((PIX, 3 * PAD), lambda g: (0, g))
    return pl.pallas_call(
        attention_kernel,
        grid=(HEADS,),
        out_shape=[shape(PIX, C), shape(PIX, QKV), shape(C, ATT), shape(8, C, dtype=f32)],
        in_specs=[SMEM, ANY, ANY, whole(PIX, C), whole(C, ATT), whole(24, C), head],
        out_specs=[whole(PIX, C), head, whole(C, ATT), whole(8, C)],
        scratch_shapes=[
            pltpu.VMEM((PIX, C), bf16), pltpu.VMEM((PIX, ATT), bf16),
            pltpu.VMEM((PAD, PIX), f32), pltpu.VMEM((PAD, PIX), f32),
            pltpu.VMEM((C, C), bf16), pltpu.VMEM((PIX, C), f32), pltpu.SemaphoreType.DMA((2,)),
        ],
        compiler_params=pltpu.CompilerParams(vmem_limit_bytes=VMEM_LIMIT),
        cost_estimate=cost(31),
        name="attention",
    )(loss, order, residual, grad, wproj, stats, projected)


def backward_middle(loss, order, grad, attn, gqkv, wqkv, residual, stats, norm, second, wproj_grad):
    own, *others, grad_residual, g2, sums = call(
        middle_kernel,
        [loss, gqkv, wqkv, norm, stats, residual, order, attn, grad, second, wproj_grad],
        [
            shape(C // 2, EARLY), *quarters(EARLY), shape(PIX, C, dtype=f32), shape(PIX, C),
            shape(8, C, dtype=f32),
        ],
        [pltpu.VMEM((ROWS, TAPS), bf16), pltpu.VMEM((PIX, C), f32)], 16, "backward_middle", 1,
    )
    return own, others, grad_residual, g2, sums


def backward_hidden(order, emb, g2, w2, hidden, stats, norm):
    g1, sums, own, *others = call(
        hidden_kernel,
        [g2, w2, hidden, stats, norm, order, emb],
        [shape(PIX, C), shape(8, C, dtype=f32), shape(C // 2, FILM), shape(C // 2, FILM)],
        [pltpu.VMEM((ROWS, TAPS), bf16), pltpu.VMEM((PIX, C), f32)], 10, "backward_hidden",
    )
    return g1, sums, own, others


def backward_late(order, g1, first, proj_sums, sums2, sums1, sums0):
    own, *others = call(
        late_kernel,
        [g1, first, order, proj_sums, sums2, sums1, sums0],
        [shape(C // 2, LATE), *quarters(LATE)],
        [pltpu.VMEM((ROWS, TAPS), bf16)], 7, "backward_late", room=54,
    )
    return own, others


def backward_image(g1, w1, x, stats, grad_residual):
    return call(
        image_kernel,
        [g1, w1, stats, x, grad_residual],
        [shape(PIX, C), shape(8, C, dtype=f32)],
        [pltpu.VMEM((ROWS, TAPS), bf16), pltpu.VMEM((PIX, C), f32)], 10, "backward_image", room=54,
    )


def store_kernel(*refs):
    count = len(refs) // 2
    copies = [
        pltpu.make_async_copy(refs[k], refs[count + k], refs[-1].at[k]) for k in range(count)
    ]
    for copy in copies:
        copy.start()
    settle(copies)


def store(*arrays):
    return pl.pallas_call(
        store_kernel,
        out_shape=[shape(*a.shape, dtype=a.dtype) for a in arrays],
        in_specs=[pl.BlockSpec(memory_space=pltpu.VMEM)] * len(arrays),
        out_specs=[ANY] * len(arrays),
        scratch_shapes=[pltpu.SemaphoreType.DMA((len(arrays),))],
        compiler_params=pltpu.CompilerParams(vmem_limit_bytes=16 * 2**20),
        cost_estimate=cost(2),
        name="store",
    )(*arrays)


def finish_kernel(mover, *refs):
    parts, (conv_ref, *outs) = refs[:4], refs[4:]
    mover.ready(*parts)
    value = sum(part[...].astype(f32) for part in parts)
    for tap in range(9):
        conv_ref[tap] = value[:, tap * C : (tap + 1) * C]
    share = value.shape[0]
    small = jnp.concatenate([value[:, 9 * C :], jnp.zeros((PAD - share, PAD), f32)], axis=0).T
    row = 0
    for out in outs:
        out[...] = small[row : row + out.shape[0], :share]
        row += out.shape[0]


def finish(parts):
    share = parts[0].shape[0]
    return call_small(
        finish_kernel,
        parts,
        [shape(9, share, C, dtype=f32)] + [shape(n, share, dtype=f32) for n in (3, 3, 2, 2, 2, 1)],
        1,
        "finish",
    )


def halves(width):
    return width // 2 // PAD * PAD


def core_kernel(groups, mover, *refs):
    owns, gots = refs[:groups], refs[groups:-4]
    stays, goes = refs[-4:-2], refs[-2:]
    block, cut = stays[0].shape[0] // 2, stays[0].shape[1]
    mover.ready(*owns, *gots[4:])
    for k in range(4):
        mover.ready(gots[k])
        x, y = k // 2, k % 2
        column = 0
        for group, own in enumerate(owns):
            width = own.shape[1]
            split = min(max(cut - column, 0), width)
            got = gots[4][k * block : (k + 1) * block, :] if group else gots[k][...]
            value = own[k * block : (k + 1) * block, :].astype(f32) + got.astype(f32)
            value = value.astype(bf16)
            if split > 0:
                at = slice(y * block, (y + 1) * block)
                (goes if x else stays)[0][at, column : column + split] = value[:, :split]
            if split < width:
                at = slice(x * block, (x + 1) * block)
                start = column + split - cut
                (goes if y else stays)[1][at, start : start + width - split] = value[:, split:]
            column += width
        if k:
            mover.send((stays[0], stays[1], goes[0])[k - 1])


def reduce_core(owns, gots, large=False):
    block = owns[0].shape[0] // 4
    width = sum(own.shape[1] for own in owns)
    cut = halves(width)
    parts = [shape(2 * block, cut), shape(2 * block, width - cut)]
    kernel = functools.partial(core_kernel, len(owns))
    if large:
        outs = call(kernel, [*owns, *gots], parts * 2, [], 3, "reduce_core")
    else:
        outs = call_small(kernel, [*owns, *gots], parts * 2, 3, "reduce_core")
    return outs[:2], outs[2:]


def cross_kernel(mover, *refs):
    stays, gots, own_ref, goes = refs[:2], refs[2:4], refs[4], refs[5:]
    mover.ready(*stays, *gots)
    block, cut = goes[0].shape
    for k, columns in enumerate((slice(0, cut), slice(cut, own_ref.shape[1]))):
        value = (stays[k][...].astype(f32) + gots[k][...].astype(f32)).astype(bf16)
        own_ref[:, columns] = value[:block]
        goes[k][...] = value[block:]


def reduce_cross(stays, gots):
    block = stays[0].shape[0] // 2
    left, right = (stay.shape[1] for stay in stays)
    own, *goes = call_small(
        cross_kernel,
        [*stays, *gots],
        [shape(block, left + right), shape(block, left), shape(block, right)],
        2,
        "reduce_cross",
    )
    return own, goes


def column_kernel(mover, own_ref, left_ref, right_ref, *outs):
    mover.ready(own_ref, left_ref, right_ref)
    got = jnp.concatenate([left_ref[...].astype(f32), right_ref[...].astype(f32)], axis=1)
    value = own_ref[...].astype(f32) + got
    share = outs[0].shape[0]
    for k, out in enumerate(outs):
        out[...] = value[k * share : (k + 1) * share].astype(bf16)


def reduce_plane(own, gots):
    block, width = own.shape
    return call_small(
        column_kernel, [own, *gots], [shape(block // 4, width)] * 4, 1, "reduce_plane"
    )


both = ("dp", "sp")


def swap(value, axis, bit):
    count = lax.axis_size(axis)
    return lax.ppermute(value, axis, [(i, i ^ bit) for i in range(count)])


def after(value, *others):
    return lax.optimization_barrier((value, *others))[0]


def gather_pair(shard):
    return jnp.concatenate([shard, swap(shard, *Z_FAR)])


def gather_column(pair):
    return jnp.concatenate([pair, swap(pair, *Z_NEAR)])


def gather_plane(block):
    return swap(block, *X), swap(block, *Y)


def gather_corner(from_x, from_y):
    cut = halves(from_x.shape[1])
    return swap(from_y[:, :cut], *X), swap(from_x[:, cut:], *Y)


def gather_rest(block, from_x, from_y, left, right):
    mine = [block, from_y, from_x, left, right]
    return mine + [swap(piece, *CORE) for piece in mine]


def swap_plane(goes, first, second):
    return [swap(goes[0], *first), swap(goes[1], *second)]


def swap_column(shards):
    own, far, near, both_ways = shards
    return [own, swap(far, *Z_FAR), swap(near, *Z_NEAR), swap(both_ways, *Z_BOTH)]


def piece_places(width):
    cut = halves(width)
    places = [(0, 0), (48, 0), (96, 0), (144, 0), (144, cut)]
    return places + [(row + C // 2, column) for row, column in places]


def row_order(tree):
    row = jnp.arange(C)
    if tree:
        share = C // 32
        k = row // share
        dp = lax.axis_index("dp") ^ (k >> 4) ^ ((k >> 3 & 1) * 2)
        sp = lax.axis_index("sp") ^ (k >> 2 & 1) ^ ((k >> 1 & 1) * 2) ^ ((k & 1) * 4)
        row = (dp * 8 + sp) * share + row % share
    return (jnp.arange(C)[:, None] == row[None, :]).astype(bf16)


def time_embedding(steps):
    half_width = E // 2
    frequencies = jnp.exp(
        -math.log(10000.0) * jnp.arange(half_width, dtype=jnp.float32) / half_width
    )
    angles = steps.astype(jnp.float32)[:, None] * frequencies[None, :]
    return jnp.concatenate([jnp.cos(angles), jnp.sin(angles)], axis=1)


def padded_heads(value, axis):
    pads = [(0, 0)] * value.ndim
    pads[axis] = (0, PAD - HD)
    return jnp.pad(value, pads)


def embedding_rows(embedding, devices):
    share = C // devices
    by_device = embedding.reshape(devices, E // devices)
    wide = by_device[:, :share].reshape(C)
    narrow = jnp.repeat(by_device[:, share:], 3, axis=1).reshape(C)
    third = jnp.arange(C) % 3
    return jnp.stack([wide] + [jnp.where(third == k, narrow, 0.0) for k in range(3)])


def body(
    images,
    timesteps,
    loss_weight,
    out_grad,
    norm_gains,
    norm_biases,
    conv_biases,
    film_weight,
    film_bias,
    conv1_weight,
    conv2_weight,
    qkv_weight,
    qv_bias,
    proj_weight,
    proj_bias,
):
    row_parts = lax.axis_size("sp")
    devices = lax.axis_size("dp") * row_parts
    samples = images.shape[0] * images.shape[1]
    rows_here = images.shape[2]
    per = max(1, samples // row_parts)
    copies = max(1, row_parts // samples)
    share = C // devices
    embed_share = E // devices
    place = lax.axis_index("sp")
    tree = lax.axis_size("dp") == 4 and row_parts == 8

    def to_samples(value):
        value = value.reshape(samples // per, per * rows_here * W, C)
        if copies > 1:
            value = jnp.repeat(value, copies, axis=0)
        value = lax.all_to_all(value, "sp", split_axis=0, concat_axis=0, tiled=True)
        value = value.reshape(row_parts, per, rows_here * W, C).transpose(1, 0, 2, 3)
        return value.reshape(per, PIX, C)

    def to_rows(value):
        value = value.reshape(per, row_parts, rows_here * W, C).transpose(1, 0, 2, 3)
        value = value.reshape(row_parts, per * rows_here * W, C)
        value = lax.all_to_all(value, "sp", split_axis=0, concat_axis=0, tiled=True)
        return value[::copies].reshape(images.shape)

    first = (place // copies) * per
    steps = lax.dynamic_slice_in_dim(timesteps.reshape(samples), first, per)
    loss = lax.dynamic_slice_in_dim(loss_weight.reshape(samples), first, per)

    first_shard = prepare(
        conv1_weight, norm_gains, norm_biases, conv_biases, film_bias, qv_bias, proj_bias[None]
    )
    by_input = lambda w: w.transpose(2, 0, 1, 3).reshape(share, 9 * C)
    film = film_weight.reshape(embed_share, 2 * C)
    second_shard = jnp.concatenate(
        [
            by_input(conv2_weight),
            padded_heads(qkv_weight, 3).reshape(share, QKV),
            padded_heads(proj_weight.transpose(2, 0, 1), 2).reshape(share, ATT),
            film[:share],
            film[share:].reshape(share, 2 * PAD),
        ],
        axis=1,
    )
    order = row_order(tree)
    staged = tree and per == 1
    if tree:
        places = piece_places
        pair = gather_pair(first_shard)
        block = gather_column(pair)
        from_x, from_y = gather_plane(block)
        second_block = gather_column(gather_pair(after(second_shard, block)))
        images_in = to_samples(after(images, first_shard))
        left, right = gather_corner(from_x, from_y)
        first_pieces = gather_rest(block, from_x, from_y, left, right)
        from_x, from_y = gather_plane(after(second_block, left, right, images_in))
        if not staged:
            second_pieces = gather_rest(
                second_block, from_x, from_y, *gather_corner(from_x, from_y)
            )
    else:
        places = lambda width: [(0, 0)]
        gather = lambda shard: [lax.all_gather(shard, both, axis=0, tiled=True)]
        first_pieces, second_pieces = gather(first_shard), gather(second_shard)
        images_in = to_samples(images)
    if not staged:
        grads_in = to_samples(out_grad)

    outs, image_grads, totals = [], [], None
    for index in range(per):
        embedding = embedding_rows(
            jax.nn.silu(time_embedding(steps[index][None]))[0], devices
        )
        emb = jnp.pad(jnp.stack(split3(embedding), axis=1).reshape(12, C), ((0, 4), (0, 0)))
        embedding = jnp.pad(embedding, ((0, 4), (0, 0)))
        weight = loss[index].reshape(1, 1)
        x = images_in[index]
        if staged:
            x = after(x, second_block)
        first, hidden, w1, stats = forward_first(places(FIRST), first_pieces, order, x)
        if staged:
            from_x, from_y = after(from_x, hidden), after(from_y, hidden)
            left, right = gather_corner(from_x, from_y)
            grads_in = to_samples(after(out_grad, from_x, from_y))
            second_pieces = gather_rest(second_block, from_x, from_y, left, right)
        grad = grads_in[index]
        second, residual, attn, projected, w2, wqkv, wproj, norm = forward_second(
            places(SECOND), second_pieces, order, x, hidden, stats, emb
        )
        block_out, gqkv, wproj_grad, proj_sums = attend(
            weight, order, grad, wproj, residual, stats, projected
        )
        own, others, grad_residual, g2, sums2 = backward_middle(
            weight, order, grad, attn, gqkv, wqkv, residual, stats, norm, second, wproj_grad
        )
        if staged:
            out_rows = to_rows(block_out[None])
            gots = [swap(other, *CORE) for other in others]
        g1, sums1, film_own, film_others = backward_hidden(
            order, embedding, g2, w2, hidden, stats, norm
        )
        if staged:
            gots = [after(got, g1) for got in gots] + [swap(other, *CORE) for other in film_others]
            stays, goes = reduce_core([own, film_own], gots, large=True)
            g1 = after(g1, *goes, out_rows)
            gots = swap_plane(goes, X, Y)
        image_grad, sums0 = backward_image(g1, w1, x, stats, grad_residual)
        if staged:
            g1 = after(g1, image_grad)
        late_own, late_others = backward_late(order, g1, first, proj_sums, sums2, sums1, sums0)
        if staged:
            late_gots = [swap(other, *CORE) for other in late_others]
            image_rows = to_rows(image_grad[None])
        else:
            outs.append(block_out)
            image_grads.append(image_grad)
            grads = [
                jnp.concatenate(
                    [jnp.concatenate([own, *others]), jnp.concatenate([film_own, *film_others])], axis=1
                ),
                jnp.concatenate([late_own, *late_others]),
            ]
            grads = [g.astype(f32) for g in grads]
            totals = grads if totals is None else [a + b for a, b in zip(totals, grads)]
    if staged:
        own, goes = reduce_cross(stays, [after(got, late_own) for got in gots])
        gots = swap_plane(goes, Y, X)
        late_gots = [after(got, *goes) for got in late_gots]
        stays, goes = reduce_core([late_own], late_gots)
        late_gots = swap_plane(goes, X, Y)
        early = reduce_plane(own, [after(got, *goes) for got in gots])
        early = swap_column(early)
        late_gots[0], early[1] = lax.optimization_barrier((late_gots[0], early[1]))
        *late_gots, image_rows = lax.optimization_barrier((*late_gots, image_rows))
        late_own, goes = reduce_cross(stays, late_gots)
        late_gots = swap_plane(goes, Y, X)
        late = list(reduce_plane(late_own, late_gots))
        late = swap_column(late)
        early[1:] = [after(part, late[2]) for part in early[1:]]
        early = sum(part.astype(f32) for part in early)
        out_rows, image_rows = store(out_rows, image_rows)
        late[1], late[3] = (after(late[k], early, out_rows) for k in (1, 3))
    else:
        image_rows, out_rows = to_rows(jnp.stack(image_grads)), to_rows(jnp.stack(outs))
        if copies > 1:
            totals = [jnp.where(place % copies == 0, t, 0.0) for t in totals]
        if tree:
            totals = [jnp.dot(order, t.astype(bf16), preferred_element_type=f32) for t in totals]
        early, late = (
            lax.psum_scatter(
                t.astype(bf16).reshape(devices, share, -1), both, scatter_dimension=0
            ).astype(f32)
            for t in totals
        )
    if not staged:
        late = [late] + [jnp.zeros_like(late)] * 3
    conv1_grad, gains_grad, biases_grad, conv_b_grad, film_b_grad, qv_grad, proj_b_grad = finish(late)
    conv2_grad = early[:, : 9 * C].reshape(share, 3, 3, C).transpose(1, 2, 0, 3)
    wqkv_grad = early[:, 9 * C : 9 * C + QKV].reshape(share, HEADS, 3, PAD)[..., :HD]
    wproj_grad = early[:, 9 * C + QKV : EARLY].reshape(share, HEADS, PAD)[..., :HD]
    film_grad = jnp.concatenate(
        [early[:, EARLY : EARLY + 2 * C], early[:, EARLY + 2 * C :].reshape(-1, 2 * C)]
    )
    return (
        out_rows,
        image_rows,
        gains_grad,
        biases_grad,
        conv_b_grad,
        film_grad.reshape(embed_share, 2, C),
        film_b_grad,
        conv1_grad.reshape(3, 3, share, C),
        conv2_grad,
        wqkv_grad,
        qv_grad,
        wproj_grad.transpose(1, 2, 0),
        proj_b_grad[0],
    )


def solution(mesh):
    return jax.shard_map(
        body,
        mesh=mesh,
        in_specs=(
            P(None, "dp", "sp", None, None),
            P(None, "dp"),
            P(None, "dp"),
            P(None, "dp", "sp", None, None),
            P(None, both),
            P(None, both),
            P(None, both),
            P(both, None, None),
            P(None, both),
            P(None, None, both, None),
            P(None, None, both, None),
            P(both, None, None, None),
            P(None, both),
            P(None, None, both),
            P(both),
        ),
        out_specs=(
            P(None, "dp", "sp", None, None),
            P(None, "dp", "sp", None, None),
            P(None, both),
            P(None, both),
            P(None, both),
            P(both, None, None),
            P(None, both),
            P(None, None, both, None),
            P(None, None, both, None),
            P(both, None, None, None),
            P(None, both),
            P(None, None, both),
            P(both),
        ),
        check_vma=False,
    )
```
